32 devices in a mesh: dp: 8 (over y, x, core), ctx: 4 (over z).
Axes of the slice: x: 2, y: 2, z: 4, core: 2. Of those that a mesh axis runs over, the one named last changes fastest.
Arguments:
- tokens: bfloat16 [16, 1024, 768], P('dp', 'ctx'), may hold values from -6 to 6
- segment_ids: int32 [16, 1024], P('dp', 'ctx'), may hold values from 0 to 2, as said below
- prompt_slots: int32 [16, 1024], P('dp', 'ctx'), may hold values from -1 to 99, as said below
- cotangent: bfloat16 [16, 1024, 768], P('dp', 'ctx'), may hold values from -6 to 6
- w_query: bfloat16 [768, 768], replicated, may hold values from -0.0390625 to 0.0390625
- w_key: bfloat16 [768, 768], replicated, may hold values from -0.21875 to 0.21875
- w_value: bfloat16 [768, 768], replicated, may hold values from -0.21875 to 0.21875
- w_output: bfloat16 [768, 768], replicated, may hold values from -0.4375 to 0.4375
- w_inner: bfloat16 [768, 3072], replicated, may hold values from -0.21875 to 0.21875
- w_outer: bfloat16 [3072, 768], replicated, may hold values from -0.15625 to 0.15625
- gain_first: float32 [768], replicated, may hold values from 0.1 to 1.9
- gain_second: float32 [768], replicated, may hold values from 0.1 to 1.9
- bias_table: float32 [32, 12], replicated, may hold values from -4 to 4
- prompt: float32 [128, 768], P('dp', 'ctx'), may hold values from -6 to 6
- first_moment: float32 [128, 768], P('dp', 'ctx'), may hold values from -2 to 2
- second_moment: float32 [128, 768], P('dp', 'ctx'), may hold values from 0.0005 to 0.005
Outputs:
- output: bfloat16 [16, 1024, 768], P('dp', 'ctx')
- prompt_new: float32 [128, 768], P('dp', 'ctx')
- first_new: float32 [128, 768], P('dp', 'ctx')
- second_new: float32 [128, 768], P('dp', 'ctx')
The draws below stay inside these ranges and needn't reach their ends.
Inputs may be any that keep to these rules, and one draw needn't show every extreme that they name: `segment_ids`: within a row the numbers never fall; each row holds 3 segments of at least 101 positions each, filling the row. `prompt_slots`: the first 100 positions of each segment hold 0 to 99 in order; all other positions hold -1.
All inputs are finite; a program needn't handle non-finite values.
Results may differ from the reference program's by a relative error of at most 0.015.
The reference program's roundings to bfloat16 on the way count: a program that leaves them out, or rounds other values in their place, can miss the bound.
Values may be sent and summed in bfloat16 or wider, within the bound.
No kernel may reach another device: no remote copies, remote signals or barrier semaphores. Data moves between devices by JAX's collectives and lax.ppermute only.
A program may use at most 192 MiB of HBM per device.

```python
import math
import jax
import jax.numpy as jnp
from jax import lax

D = 768
HEADS = 12
FF = 3072
BUCKETS = 32
PROMPT = 100
PAD = 128
SEGS = 3
ROW_LEN = 1024
ROWS = 16


def segment_layout(key):
    base_key = jax.random.fold_in(key, 7)
    long_key = jax.random.fold_in(base_key, 1)
    small_key = jax.random.fold_in(base_key, 2)
    big_key = jax.random.fold_in(base_key, 3)
    long_pick = jax.random.randint(long_key, (ROWS, 1), 0, SEGS)
    small_weights = jax.random.randint(small_key, (ROWS, SEGS), 1, 5)
    big_weights = jax.random.randint(big_key, (ROWS, SEGS), 12, 17)
    is_long = jnp.arange(SEGS, dtype=jnp.int32)[None, :] == long_pick
    weights = jnp.where(is_long, big_weights, small_weights)
    spare_len = ROW_LEN - SEGS * (PROMPT + 1)
    extra_len = weights * spare_len // jnp.sum(weights, axis=1, keepdims=True)
    extra_len = extra_len.at[:, SEGS - 1].add(spare_len - jnp.sum(extra_len, axis=1))
    lengths = PROMPT + 1 + extra_len
    seg_ends = jnp.cumsum(lengths, axis=1)
    starts = seg_ends - lengths
    places = jnp.arange(ROW_LEN, dtype=jnp.int32)
    segment = jnp.sum((places[None, :, None] >= seg_ends[:, None, :]).astype(jnp.int32), axis=2)
    own_seg = segment[:, :, None] == jnp.arange(SEGS, dtype=jnp.int32)[None, None, :]
    start_here = jnp.sum(jnp.where(own_seg, starts[:, None, :], 0), axis=2)
    inside = places[None, :] - start_here
    slot_ids = jnp.where(inside < PROMPT, inside, -1)
    return (segment.astype(jnp.int32), slot_ids.astype(jnp.int32))


def draw_segment_ids(key, part):
    return segment_layout(key)[0]


def draw_prompt_slots(key, part):
    return segment_layout(key)[1]


def draw_cotangent(key, part):
    slot_ids = segment_layout(key)[1]
    cot_key = jax.random.fold_in(key, 11)
    values = jax.random.truncated_normal(cot_key, -6.0, 6.0, (ROWS, ROW_LEN, D), jnp.float32)
    rise = 6.0
    place = slot_ids.astype(jnp.float32) / (PROMPT - 1.0) - 1.0
    factor = jnp.where(slot_ids >= 0, jnp.exp(math.log(rise) * place), 1.0)
    return (values * factor[:, :, None]).astype(jnp.bfloat16)


def steps_of(rng, extent, split, least, largest):
    def one(axis_at, blocks):
        heights = jax.random.uniform(jax.random.fold_in(jax.random.fold_in(rng, 6), axis_at), (blocks,), jnp.float32, least / len(split), largest / len(split))
        return jnp.repeat(jnp.exp(heights), extent[axis_at] // blocks).reshape((-1,) + (1,) * (len(extent) - axis_at - 1))

    loudness = one(*split[0])
    for cut in split[1:]:
        loudness = loudness * one(*cut)
    return loudness


def normal_values(key, dims, spread, reach, cuts=(), kind=jnp.bfloat16):
    values = jax.random.normal(key, dims, jnp.float32) * spread
    if len(cuts) > 0:
        values = steps_of(key, dims, cuts, -0.22, 0.18) * values
    return jnp.clip(values, min=-reach, max=reach).astype(kind)


def setup_inputs(seed: int = 0) -> dict:
    key_of = jax.random.split(jax.random.key(seed), 17)
    tokens = normal_values(key_of[0], (ROWS, ROW_LEN, D), 1.0, 6.0, ((0, 8), (1, 4)))
    segment_ids = draw_segment_ids(jax.random.fold_in(key_of[16], 71), 0)
    prompt_slots = draw_prompt_slots(jax.random.fold_in(key_of[16], 71), 0)
    cotangent = draw_cotangent(jax.random.fold_in(key_of[16], 71), 0)
    w_query = normal_values(key_of[4], (D, D), (28 * D) ** -0.5, 0.0390625)
    w_key = normal_values(key_of[5], (D, D), D ** -0.5, 0.21875)
    w_value = normal_values(key_of[6], (D, D), D ** -0.5, 0.21875)
    w_output = normal_values(key_of[7], (D, D), (D // 4) ** -0.5, 0.4375)
    w_inner = normal_values(key_of[8], (D, FF), D ** -0.5, 0.21875)
    w_outer = normal_values(key_of[9], (FF, D), (FF // 2) ** -0.5, 0.15625)
    gain_first = jnp.clip(1.0 + 0.18 * jax.random.normal(key_of[10], (D,), jnp.float32), 0.1, 1.9)
    gain_second = jnp.clip(1.0 + 0.18 * jax.random.normal(key_of[11], (D,), jnp.float32), 0.1, 1.9)
    bias_table = normal_values(key_of[12], (BUCKETS, HEADS), 1.0, 4.0, (), jnp.float32)
    prompt = normal_values(key_of[13], (PAD, D), 1.0, 6.0, ((0, 8), (1, 4)), jnp.float32)
    first_moment = normal_values(key_of[14], (PAD, D), 0.3, 2.0, ((0, 8), (1, 4)), jnp.float32)
    second_moment = jnp.clip(jnp.exp(math.log(0.005) - 2.30258502 * jax.random.uniform(key_of[15], (PAD, D), jnp.float32) ** steps_of(key_of[15], (PAD, D), ((0, 8), (1, 4)), -0.2, 0.2)), 0.0005, 0.005)
    return {"tokens": tokens, "segment_ids": segment_ids, "prompt_slots": prompt_slots, "cotangent": cotangent, "w_query": w_query, "w_key": w_key, "w_value": w_value, "w_output": w_output, "w_inner": w_inner, "w_outer": w_outer, "gain_first": gain_first, "gain_second": gain_second, "bias_table": bias_table, "prompt": prompt, "first_moment": first_moment, "second_moment": second_moment}


@jax.custom_vjp
def low(v):
    return lax.optimization_barrier(v.astype(jnp.bfloat16)).astype(jnp.float32)

@jax.custom_vjp
def low_back(v):
    return v

def low_keep(v):
    return (low(v), None)

def low_pass(kept, grad):
    return (grad,)

def back_keep(v):
    return (v, None)

def back_low(kept, grad):
    return (low(grad),)
low.defvjp(low_keep, low_pass)
low_back.defvjp(back_keep, back_low)
highest = lax.Precision.HIGHEST
norm_eps = 1e-06
beta_first = 0.9
beta_second = 0.999
adam_eps = 1e-08
learn_rate = 0.1
first_fix = 1.0 - 0.9 ** 8
second_fix = 1.0 - 0.999 ** 8
far_marks = (12, 16, 23, 32, 46, 64, 91)

def round_both(values):
    return low(low_back(values))

def bucket_ids(offset):
    distance = jnp.abs(offset)
    passed = sum(((distance >= boundary).astype(jnp.int32) for boundary in far_marks))
    far_ids = jnp.minimum(8 + passed, 15)
    return jnp.where(distance < 8, distance, far_ids) + 16 * (offset > 0).astype(jnp.int32)

def rms_norm(values, gain_vector):
    return values * lax.rsqrt(lax.optimization_barrier(jnp.mean(values * values, axis=-1, keepdims=True)) + norm_eps) * gain_vector

def encoder_layer(prompt_now, tokens_row, segment_row, slot_row, weights):
    w_query, w_key, w_value, w_output, w_inner, w_outer, gain_first, gain_second, bias_table = weights
    seq_len = tokens_row.shape[0]
    head_count = bias_table.shape[1]
    sent_prompt = low(prompt_now)
    picked = jnp.take(sent_prompt, jnp.maximum(slot_row, 0), axis=0)
    hidden = jnp.where((slot_row >= 0)[:, None], picked, tokens_row)
    normed = low(rms_norm(hidden, gain_first))

    def project(weight):
        return round_both(jnp.dot(normed, weight, precision=highest)).reshape(seq_len, head_count, -1)
    query_heads = project(w_query)
    key_heads = project(w_key)
    value_heads = project(w_value)
    places = jnp.arange(seq_len, dtype=jnp.int32)
    offsets = places[None, :] - places[:, None]
    score_bias = jnp.transpose(bias_table[bucket_ids(offsets)], (2, 0, 1))
    scores = low_back(jnp.einsum('qhd,khd->hqk', query_heads, key_heads, precision=highest) + score_bias)
    same_seg = segment_row[:, None] == segment_row[None, :]
    scores = jnp.where(same_seg[None], scores, -1000000000.0)
    soft_weights = low(jax.nn.softmax(scores, axis=-1))
    mixed_rows = jnp.einsum('hqk,khd->qhd', soft_weights, value_heads, precision=highest).reshape(seq_len, -1)
    attended = low_back(jnp.dot(round_both(mixed_rows), w_output, precision=highest))
    after_attn = hidden + attended
    inner_pre = low_back(jnp.dot(low(rms_norm(after_attn, gain_second)), w_inner, precision=highest))
    outer_out = low_back(jnp.dot(low(jax.nn.relu(inner_pre)), w_outer, precision=highest))
    return after_attn + outer_out

def reference(tokens, segment_ids, prompt_slots, cotangent, w_query, w_key, w_value, w_output, w_inner, w_outer, gain_first, gain_second, bias_table, prompt, first_moment, second_moment):
    weights = tuple((weight.astype(jnp.float32) for weight in (w_query, w_key, w_value, w_output, w_inner, w_outer, gain_first, gain_second, bias_table)))

    def one_row(grad_total, row_items):
        tokens_row, segment_row, slot_row, cot_row = row_items
        tokens_wide = tokens_row.astype(jnp.float32)

        def layer_of(prompt_now):
            return encoder_layer(prompt_now, tokens_wide, segment_row, slot_row, weights)
        output_row, pull_back = jax.vjp(layer_of, prompt)
        grad_rows = pull_back(cot_row.astype(jnp.float32))[0]
        return (grad_total + grad_rows, output_row.astype(jnp.bfloat16))
    grad_total, output = lax.scan(one_row, jnp.zeros_like(prompt), (tokens, segment_ids, prompt_slots, cotangent))
    max_norm = 0.5 * jnp.sqrt(jnp.float32(PROMPT * D))
    norm_total = jnp.sqrt(jnp.sum(grad_total * grad_total))
    clipped = grad_total * (max_norm / jnp.maximum(norm_total, max_norm))
    first_new = beta_first * first_moment + (1.0 - beta_first) * clipped
    second_new = beta_second * second_moment + (1.0 - beta_second) * clipped * clipped
    prompt_new = prompt - learn_rate * (first_new / first_fix) / (jnp.sqrt(second_new / second_fix) + adam_eps)
    return (output, prompt_new, first_new, second_new)
```

```python
import functools

import jax
import jax.numpy as jnp
import numpy as np
from jax import lax
from jax.experimental import pallas as pl
from jax.experimental.pallas import tpu as pltpu
from jax.sharding import PartitionSpec as P

PROMPT = 100
HEAD = 64
PAIR = 2 * HEAD
BLK = 128
QROWS = 256
norm_eps = 1e-06
beta_first = 0.9
beta_second = 0.999
adam_eps = 1e-08
learn_rate = 0.1
first_fix = 1.0 - 0.9**8
second_fix = 1.0 - 0.999**8
far_marks = (12, 16, 23, 32, 46, 64, 91)
f32 = jnp.float32
bf16 = jnp.bfloat16
i32 = jnp.int32
MASKED = -float(2**30)
AXES = ("dp", "ctx")
MIB = 1 << 20


def bucket_table(offset):
    distance = np.abs(offset)
    passed = sum((distance >= mark).astype(np.int32) for mark in far_marks)
    far_ids = np.minimum(8 + passed, 15)
    return np.where(distance < 8, distance, far_ids) + 16 * (offset > 0).astype(np.int32)


def dot_nn(a, b):
    return lax.dot_general(a, b, (((1,), (0,)), ((), ())), preferred_element_type=f32)


def dot_nt(a, b):
    return lax.dot_general(a, b, (((1,), (1,)), ((), ())), preferred_element_type=f32)


def dot_tn(a, b):
    return lax.dot_general(a, b, (((0,), (0,)), ((), ())), preferred_element_type=f32)


def split_two(values):
    high = values.astype(bf16)
    return high, (values - high.astype(f32)).astype(bf16)


def inv_rms(values):
    return lax.rsqrt(jnp.mean(values * values, axis=-1, keepdims=True) + norm_eps)


def segment_of(place, first, second):
    seg = (place >= first).astype(i32) + (place >= second).astype(i32)
    start = jnp.where(seg == 0, 0, jnp.where(seg == 1, first, second))
    return seg, place - start


def vmem_spec():
    return pl.BlockSpec(memory_space=pltpu.VMEM)


def smem_spec():
    return pl.BlockSpec(memory_space=pltpu.SMEM)


def any_spec():
    return pl.BlockSpec(memory_space=pl.ANY)


def out(shape, dtype):
    return jax.ShapeDtypeStruct(shape, dtype)


def params(mib):
    return pltpu.CompilerParams(vmem_limit_bytes=mib * MIB)


def cost(flops, nbytes, trans=0):
    return pl.CostEstimate(flops=int(flops), bytes_accessed=int(nbytes), transcendentals=int(trans))


def pick_piece(pieces, turn, j):
    count = len(pieces)
    place = lax.rem(turn - j + count, count)
    picked = pieces[0][...]
    for k in range(1, count):
        picked = jnp.where(place == k, pieces[k][...], picked)
    return picked


def bias_kernel(base_ref, tile_ref, table_ref):
    heads = tile_ref.shape[0]
    for h in range(heads):
        row = jnp.broadcast_to(base_ref[h : h + 1, :], (BLK, 4 * BLK))
        spread = pltpu.roll(row, 0, 1, stride=1, stride_axis=0)
        low, mid, top = (spread[:, k * BLK : (k + 1) * BLK] for k in (1, 2, 3))
        tile_ref[h, 0] = low
        tile_ref[h, 1] = mid
        tile_ref[h, 2] = top
        mid_high, mid_low = split_two(mid)
        low_high, low_low = split_two(low)
        table_ref[h, 0:BLK, :] = mid_high
        table_ref[h, BLK : 2 * BLK, :] = low_high
        table_ref[h, 2 * BLK : 3 * BLK, :] = mid_low
        table_ref[h, 3 * BLK : 4 * BLK, :] = low_low


def first_kernel(count, piece, sc_ref, *refs):
    pieces = refs[:count]
    (prompt_ref, gain_ref, wq_ref, wk_ref, wv_ref, hid_ref, q_ref, k_ref, v_ref, kp_ref, vp_ref, norm_ref) = refs[count:]
    half, turn, first, second = (sc_ref[n] for n in range(4))
    half_len = count * piece
    gain = gain_ref[...]
    slots = lax.broadcasted_iota(i32, (1, BLK), 1)
    for j in range(count):
        rows = slice(j * piece, (j + 1) * piece)
        place = half * half_len + j * piece + lax.broadcasted_iota(i32, (piece, 1), 0)
        inside = segment_of(place, first, second)[1]
        shown = inside < PROMPT
        choose = jnp.where((inside == slots) & shown, 1.0, 0.0).astype(bf16)
        picked = dot_nn(choose, prompt_ref[...])
        hidden = jnp.where(shown, picked, pick_piece(pieces, turn, j).astype(f32))
        hid_ref[rows, :] = hidden.astype(bf16)
        norm_ref[rows, :] = (hidden * inv_rms(hidden) * gain).astype(bf16)
    hidden = prompt_ref[...].astype(f32)
    norm_ref[half_len : half_len + BLK, :] = (hidden * inv_rms(hidden) * gain).astype(bf16)
    wide = 2 * BLK

    @pl.loop(0, wq_ref.shape[1] // wide)
    def _(t):
        cols = pl.ds(pl.multiple_of(t * wide, wide), wide)
        q_ref[:, cols] = dot_nn(norm_ref[0:half_len, :], wq_ref[:, cols]).astype(bf16)
        keys = dot_nn(norm_ref[...], wk_ref[:, cols]).astype(bf16)
        k_ref[:, cols] = keys[:half_len]
        kp_ref[:, cols] = keys[half_len:]
        vals = dot_nn(norm_ref[...], wv_ref[:, cols]).astype(bf16)
        v_ref[:, cols] = vals[:half_len]
        vp_ref[:, cols] = vals[half_len:]


def forward_kernel(count, piece, sc_ref, tab_ref, *refs):
    pieces = refs[:count]
    (
        q_ref, k_ref, v_ref, kp_ref, vp_ref, hid_ref, gain_first_ref, gain_second_ref, wk_ref, wv_ref, wo_ref, wi_ref,
        tile_ref, table_ref,
        e_ref, kall_ref, vall_ref, mixed_ref, inv_ref, after_ref, act_ref,
        norm_ref, e_buf, sems,
    ) = refs[count:]
    half, turn, first, second = (sc_ref[n] for n in range(4))
    half_len = count * piece
    width = q_ref.shape[1]
    keys_all = 2 * half_len + BLK
    gain = gain_first_ref[...]
    for j in range(count):
        tok = pick_piece(pieces, turn, j).astype(f32)
        norm_ref[j * piece : (j + 1) * piece, :] = (tok * inv_rms(tok) * gain).astype(bf16)
    wide = 2 * BLK

    @pl.loop(0, width // wide)
    def _(t):
        cols = pl.ds(pl.multiple_of(t * wide, wide), wide)
        kall_ref[half_len : 2 * half_len, cols] = dot_nn(norm_ref[...], wk_ref[:, cols]).astype(bf16)
        vall_ref[half_len : 2 * half_len, cols] = dot_nn(norm_ref[...], wv_ref[:, cols]).astype(bf16)
        kall_ref[0:half_len, cols] = k_ref[:, cols]
        vall_ref[0:half_len, cols] = v_ref[:, cols]
        kall_ref[2 * half_len :, cols] = kp_ref[:, cols]
        vall_ref[2 * half_len :, cols] = vp_ref[:, cols]

    lane = lax.broadcasted_iota(i32, (1, PAIR), 1)
    low_lane = lane < HEAD
    lane_seg = lax.rem(lane, HEAD)
    spot = lax.broadcasted_iota(i32, (half_len, 1), 0)
    own_seg, own_inside = segment_of(half * half_len + spot, first, second)
    par_seg, par_inside = segment_of((1 - half) * half_len + spot, first, second)
    q_aug = jnp.where(own_seg == lane_seg, 1.0, 0.0).astype(bf16)

    def key_aug(seg, inside):
        closed = ((seg != lane_seg) | (inside < PROMPT)) & (lane_seg < 3)
        return jnp.where(closed, MASKED, 0.0).astype(bf16)

    slot = lax.broadcasted_iota(i32, (BLK, 1), 0)
    k_aug = jnp.concatenate(
        [
            key_aug(own_seg, own_inside),
            key_aug(par_seg, par_inside),
            jnp.where((slot >= PROMPT) & (lane_seg < 3), MASKED, 0.0).astype(bf16),
        ],
        axis=0,
    )
    far = lax.rem(lax.broadcasted_iota(i32, (1, 4 * BLK), 1), 2 * BLK)
    spread = jnp.where(jnp.minimum(own_inside, 2 * BLK - 1) == far, 1.0, 0.0).astype(bf16)
    blocks = half_len // BLK
    per = QROWS // BLK

    def e_copy(hp, at):
        return pltpu.make_async_copy(e_buf.at[at], e_ref.at[pl.ds(2 * hp, 2)], sems.at[at])

    @pl.loop(0, width // PAIR)
    def _(hp):
        at = lax.rem(hp, 2)

        @pl.when(hp >= 2)
        def _():
            e_copy(hp - 2, at).wait()

        cols = pl.ds(pl.multiple_of(hp * PAIR, PAIR), PAIR)
        q_pair, k_pair, v_pair = q_ref[:, cols], kall_ref[:, cols], vall_ref[:, cols]
        results = []
        for s in range(2):
            h = 2 * hp + s
            keep = low_lane if s == 0 else jnp.logical_not(low_lane)
            q_e = jnp.where(keep, q_pair, q_aug)
            k_e = jnp.where(keep, k_pair, k_aug)
            v_e = jnp.where(keep, v_pair, jnp.ones((), bf16))
            back_far, ahead_far = tab_ref[15, h], tab_ref[31, h]
            other_far = jnp.where(half == 0, ahead_far, back_far)
            table = table_ref[h]
            head_rows = []
            for qt in range(half_len // QROWS):
                qrows = slice(qt * QROWS, (qt + 1) * QROWS)
                raw = dot_nt(q_e[qrows], k_e)
                prompt_bias = dot_nn(spread[qrows], table)
                e_rows = []
                for sub in range(per):
                    qb = qt * per + sub
                    rr = slice(sub * BLK, (sub + 1) * BLK)
                    parts, consts = [], []
                    for kb in range(2 * blocks):
                        part = raw[rr, kb * BLK : (kb + 1) * BLK]
                        const = None
                        if kb < blocks:
                            gap = kb - qb
                            if abs(gap) <= 1:
                                part = part + tile_ref[h, gap + 1]
                            else:
                                const = 0 if gap < 0 else 1
                        elif qb == blocks - 1 and kb == blocks:
                            part = part + jnp.where(half == 0, tile_ref[h, 2], back_far)
                        elif qb == 0 and kb == 2 * blocks - 1:
                            part = part + jnp.where(half == 0, ahead_far, tile_ref[h, 0])
                        else:
                            const = 2
                        parts.append(part)
                        consts.append(const)
                    parts.append(raw[rr, 2 * blocks * BLK :] + prompt_bias[rr])
                    consts.append(None)
                    values = (back_far, ahead_far, other_far)
                    best = None
                    for group in (None, 0, 1, 2):
                        members = [p for p, c in zip(parts, consts) if c == group]
                        if not members:
                            continue
                        top = functools.reduce(jnp.maximum, members)
                        if group is not None:
                            top = top + values[group]
                        best = top if best is None else jnp.maximum(best, top)
                    peak = jnp.max(best, axis=1, keepdims=True)
                    shifts = [peak - value for value in values]
                    e_rows.append(
                        jnp.concatenate(
                            [
                                jnp.exp(p - (peak if c is None else shifts[c])).astype(bf16)
                                for p, c in zip(parts, consts)
                            ],
                            axis=1,
                        )
                    )
                raised = jnp.concatenate(e_rows, axis=0)
                e_buf[at, s, qrows, :] = raised
                head_rows.append(dot_nn(raised, v_e))
            results.append(jnp.concatenate(head_rows, axis=0))
        sums = pltpu.roll(jnp.where(low_lane, results[1], results[0]), HEAD, 1)
        inv = 1.0 / sums
        inv_ref[:, cols] = inv
        mixed_ref[:, cols] = (jnp.where(low_lane, results[0], results[1]) * inv).astype(bf16)
        e_copy(hp, at).start()

    for rest in range(2):
        e_copy(width // PAIR - 2 + rest, rest).wait()

    @pl.loop(0, half_len // BLK)
    def _(t):
        rows = pl.ds(pl.multiple_of(t * BLK, BLK), BLK)
        after = hid_ref[rows, :].astype(f32) + dot_nn(mixed_ref[rows, :], wo_ref[...])
        after_ref[rows, :] = after
        norm_ref[rows, :] = (after * inv_rms(after) * gain_second_ref[...]).astype(bf16)

    @pl.loop(0, wi_ref.shape[1] // wide)
    def _(t):
        cols = pl.ds(pl.multiple_of(t * wide, wide), wide)
        act_ref[:, cols] = jnp.maximum(dot_nn(norm_ref[...], wi_ref[:, cols]), 0.0).astype(bf16)


def backward_kernel(count, piece, sc_ref, *refs):
    cots = refs[:count]
    (
        act_ref, after_ref, mixed_ref, inv_ref, q_ref, kall_ref, vall_ref, prompt_ref, gain_first_ref, gain_second_ref,
        wout_ref, wi_ref, wo_ref, wq_ref, wk_ref, wv_ref, e_hbm,
        grad_ref,
        e_ref, cot_ref, acc_ref, do_ref, delta_ref, dq_ref, gk_ref, gv_ref, sem,
    ) = refs[count:]
    fetch = pltpu.make_async_copy(e_hbm, e_ref, sem)
    fetch.start()
    half, turn, first, second = (sc_ref[n] for n in range(4))
    half_len = count * piece
    width = q_ref.shape[1]
    for j in range(count):
        cot_ref[j * piece : (j + 1) * piece, :] = pick_piece(cots, turn, j)
    wide = 4 * BLK
    acc_ref[...] = jnp.zeros_like(acc_ref)

    @pl.loop(0, wi_ref.shape[1] // wide)
    def _(t):
        cols = pl.ds(pl.multiple_of(t * wide, wide), wide)
        grad_act = dot_nt(cot_ref[...], wout_ref[cols, :])
        grad_inner = jnp.where(act_ref[:, cols] > 0, grad_act, 0.0).astype(bf16)
        acc_ref[...] += dot_nt(grad_inner, wi_ref[:, cols])

    gain = gain_second_ref[...]

    @pl.loop(0, half_len // BLK)
    def _(t):
        rows = pl.ds(pl.multiple_of(t * BLK, BLK), BLK)
        after = after_ref[rows, :]
        scale = inv_rms(after)
        pulled = gain * acc_ref[rows, :]
        along = jnp.mean(after * pulled, axis=-1, keepdims=True)
        grad_after = cot_ref[rows, :].astype(f32) + scale * pulled - after * (scale * scale * scale * along)
        acc_ref[rows, :] = grad_after
        grad_mixed = dot_nt(grad_after.astype(bf16), wo_ref[...])
        do_ref[rows, :] = (grad_mixed * inv_ref[rows, :]).astype(bf16)

    fetch.wait()
    lane = lax.broadcasted_iota(i32, (1, PAIR), 1)
    low_lane = lane < HEAD
    lane_at = lax.rem(lane, HEAD)

    @pl.loop(0, width // PAIR)
    def _(hp):
        cols = pl.ds(pl.multiple_of(hp * PAIR, PAIR), PAIR)
        q_pair, k_pair, v_pair, do_pair = q_ref[:, cols], kall_ref[:, cols], vall_ref[:, cols], do_ref[:, cols]
        inner = do_pair.astype(f32) * mixed_ref[:, cols].astype(f32)
        dqs, dks, dvs = [], [], []
        for s in range(2):
            keep = low_lane if s == 0 else jnp.logical_not(low_lane)
            delta = jnp.sum(jnp.where(keep, inner, 0.0), axis=1, keepdims=True)
            high, low = split_two(-delta)
            aug = jnp.where(lane_at == 0, high, jnp.where(lane_at == 1, low, jnp.zeros((), bf16)))
            do_e = jnp.where(keep, do_pair, aug)
            v_e = jnp.where(keep, v_pair, jnp.ones((), bf16))
            dq, dk, dv = [], None, None
            for qt in range(half_len // QROWS):
                qrows = slice(qt * QROWS, (qt + 1) * QROWS)
                raised = e_ref[2 * hp + s, qrows, :]
                grad_probs = dot_nt(do_e[qrows], v_e)
                grad_scores = (raised.astype(f32) * grad_probs).astype(bf16)
                dq.append(dot_nn(grad_scores, k_pair))
                dk_now = dot_tn(grad_scores[:, 2 * half_len :], q_pair[qrows])
                dv_now = dot_tn(raised[:, 2 * half_len :], do_pair[qrows])
                dk = dk_now if dk is None else dk + dk_now
                dv = dv_now if dv is None else dv + dv_now
            dqs.append(jnp.concatenate(dq, axis=0))
            dks.append(dk)
            dvs.append(dv)
        dq_ref[:, cols] = jnp.where(low_lane, dqs[0], dqs[1]).astype(bf16)
        gk_ref[:, cols] = jnp.where(low_lane, dks[0], dks[1]).astype(bf16)
        gv_ref[:, cols] = jnp.where(low_lane, dvs[0], dvs[1]).astype(bf16)

    spot = lax.broadcasted_iota(i32, (1, half_len), 1)
    inside = segment_of(half * half_len + spot, first, second)[1]
    slots = lax.broadcasted_iota(i32, (BLK, 1), 0)
    choose = jnp.where((inside == slots) & (inside < PROMPT), 1.0, 0.0).astype(bf16)
    gq = dot_nn(choose, dq_ref[...]).astype(bf16)
    pulled = dot_nt(gq, wq_ref[...]) + dot_nt(gk_ref[...], wk_ref[...]) + dot_nt(gv_ref[...], wv_ref[...])
    high, low = split_two(acc_ref[...])
    direct = dot_nn(choose, high) + dot_nn(choose, low)
    hidden = prompt_ref[...].astype(f32)
    scale = inv_rms(hidden)
    pulled = gain_first_ref[...] * pulled
    along = jnp.mean(hidden * pulled, axis=-1, keepdims=True)
    grad_ref[...] = direct + scale * pulled - hidden * (scale * scale * scale * along)


def output_kernel(act_ref, after_ref, wout_ref, out_ref):
    wide = 2 * BLK

    @pl.loop(0, out_ref.shape[1] // wide)
    def _(t):
        cols = pl.ds(pl.multiple_of(t * wide, wide), wide)
        out_ref[:, cols] = (after_ref[:, cols] + dot_nn(act_ref[...], wout_ref[:, cols])).astype(bf16)


def on_device(
    sizes, tokens, segment_ids, prompt_slots, cotangent, w_query, w_key, w_value, w_output, w_inner, w_outer,
    gain_first, gain_second, bias_table, prompt, first_moment, second_moment,
):
    n_dp, n_ctx = sizes
    count, piece, width = tokens.shape
    half_len = count * piece
    heads = bias_table.shape[1]
    dp, ctx = lax.axis_index("dp"), lax.axis_index("ctx")
    core, turn = lax.rem(dp, 2), lax.rem(ctx, count)

    def permute(value, target):
        pairs = []
        for d in range(n_dp):
            for z in range(n_ctx):
                d2, z2 = target(d, z)
                pairs.append((d * n_ctx + z, d2 * n_ctx + z2))
        return lax.ppermute(value, AXES, pairs)

    def swap_dp(value, bit):
        return permute(value, lambda d, z: (d ^ bit, z))

    def swap_ctx(value, bit):
        return permute(value, lambda d, z: (d, z ^ bit))

    def there(k):
        return lambda d, z: (2 * (d // 2) + z // count, (d % 2) * count + (z + k) % count)

    def send_pieces(rows):
        return [
            permute(lax.dynamic_index_in_dim(rows, lax.rem(ctx + k, count), keepdims=False), there(k))
            for k in range(count)
        ]

    own = send_pieces(tokens)
    partner = [swap_dp(piece_rows, 1) for piece_rows in own]
    cot_rows, partner = lax.optimization_barrier((cotangent, partner))
    cots = send_pieces(cot_rows)

    rows_own, cols_own = prompt.shape
    tallies = jnp.concatenate(
        [jnp.sum((segment_ids <= n).astype(f32), axis=1) for n in range(2)]
    )
    tally_row = jnp.zeros((8, cols_own), f32).at[0, : 2 * count].set(tallies)
    block = jnp.concatenate([prompt, tally_row], axis=0).astype(bf16)
    block = jnp.concatenate([jnp.where(ctx == n, block, 0) for n in range(n_ctx)], axis=1)
    bit = 1
    while bit < n_ctx:
        block = block + swap_ctx(block, bit)
        bit *= 2
    other = swap_dp(block, 1)

    def joined(mine, theirs, up):
        return jnp.where(up, jnp.concatenate([theirs, mine], 0), jnp.concatenate([mine, theirs], 0))

    tally_mine, tally_theirs = (
        jnp.sum(b[rows_own].astype(f32).reshape(n_ctx, cols_own)[:, : 2 * count], axis=0).reshape(2, count)
        for b in (block, other)
    )
    tally = jnp.where(ctx // count == core, tally_mine, tally_theirs)
    marks = lax.dynamic_index_in_dim(tally, turn, axis=1, keepdims=False).astype(i32)
    scalars = jnp.concatenate([jnp.stack([core, turn]).astype(i32), marks])
    sent = joined(block[:rows_own], other[:rows_own], core == 1)
    bit = 2
    while bit < n_dp:
        sent = joined(sent, swap_dp(sent, bit), (dp & bit) != 0)
        bit *= 2

    choose = (np.arange(bias_table.shape[0])[:, None] == bucket_table(np.arange(4 * BLK) - 2 * BLK)[None]).astype(np.float32)
    base = lax.dot_general(
        bias_table, jnp.asarray(choose), (((0,), (0,)), ((), ())), precision=lax.Precision.HIGHEST
    )
    tiles, table = pl.pallas_call(
        bias_kernel,
        out_shape=(out((heads, 3, BLK, BLK), f32), out((heads, 4 * BLK, BLK), bf16)),
        compiler_params=params(24),
        cost_estimate=cost(1e6, 4e6),
    )(base)

    gain_1, gain_2 = gain_first[None], gain_second[None]
    act_like = out((half_len, width), bf16)
    pair_like = out((BLK, width), bf16)
    hid, q, k, v, kp, vp = pl.pallas_call(
        functools.partial(first_kernel, count, piece),
        out_shape=(act_like, act_like, act_like, act_like, pair_like, pair_like),
        in_specs=[smem_spec()] + [vmem_spec()] * (count + 5),
        out_specs=[vmem_spec()] * 6,
        scratch_shapes=[pltpu.VMEM((half_len + BLK, width), bf16)],
        compiler_params=params(32),
        cost_estimate=cost(6 * half_len * width * width, 8e6),
    )(scalars, *own, sent, gain_1, w_query, w_key, w_value)

    keys_all = 2 * half_len + BLK
    hidden_ff = w_inner.shape[1]
    e, kall, vall, mixed, inv, after, act = pl.pallas_call(
        functools.partial(forward_kernel, count, piece),
        out_shape=(
            out((heads, half_len, keys_all), bf16),
            out((keys_all, width), bf16),
            out((keys_all, width), bf16),
            act_like,
            out((half_len, width), f32),
            out((half_len, width), f32),
            out((half_len, hidden_ff), bf16),
        ),
        in_specs=[smem_spec(), smem_spec()] + [vmem_spec()] * (count + 14),
        out_specs=[any_spec()] + [vmem_spec()] * 6,
        scratch_shapes=[
            pltpu.VMEM((half_len, width), bf16),
            pltpu.VMEM((2, 2, half_len, keys_all), bf16),
            pltpu.SemaphoreType.DMA((2,)),
        ],
        compiler_params=params(56),
        cost_estimate=cost(3e10, 4e7, heads * half_len * keys_all),
    )(
        scalars, bias_table, *partner, q, k, v, kp, vp, hid, gain_1, gain_2, w_key, w_value, w_output, w_inner, tiles,
        table,
    )

    grad = pl.pallas_call(
        functools.partial(backward_kernel, count, piece),
        out_shape=out((BLK, width), f32),
        in_specs=[smem_spec()] + [vmem_spec()] * (count + 16) + [any_spec()],
        out_specs=vmem_spec(),
        scratch_shapes=[
            pltpu.VMEM((heads, half_len, keys_all), bf16),
            pltpu.VMEM((half_len, width), bf16),
            pltpu.VMEM((half_len, width), f32),
            pltpu.VMEM((half_len, width), bf16),
            pltpu.VMEM((8, BLK), f32),
            pltpu.VMEM((half_len, width), bf16),
            pltpu.VMEM((BLK, width), bf16),
            pltpu.VMEM((BLK, width), bf16),
            pltpu.SemaphoreType.DMA,
        ],
        compiler_params=params(60),
        cost_estimate=cost(3e10, 4e7),
    )(
        scalars, *cots, act, after, mixed, inv, q, kall, vall, sent, gain_1, gain_2, w_outer, w_inner, w_output, w_query,
        w_key, w_value, e,
    )

    rows_out = pl.pallas_call(
        output_kernel,
        out_shape=act_like,
        compiler_params=params(32),
        cost_estimate=cost(2 * half_len * width * hidden_ff, 1e7),
    )(act, after, w_outer)

    halves = rows_out.reshape(count, piece, width)
    got = [
        permute(lax.dynamic_index_in_dim(halves, lax.rem(turn - k + count, count), keepdims=False), back_of(count, k))
        for k in range(count)
    ]
    order = [lax.rem(ctx + j, count) for j in range(count)]
    output = jnp.stack(
        [functools.reduce(lambda a, k: jnp.where(order[k] == r, got[k], a), range(1, count), got[0]) for r in range(count)]
    )

    per = rows_own
    grad = grad[: per * n_dp]
    bit = 1
    keep = grad.reshape(1, n_dp, per, width)
    while bit < n_dp:
        left = keep.shape[1]
        view = keep.reshape(left // 2, 2, per, width)
        up = (dp & bit) != 0
        mine = jnp.where(up, view[:, 1], view[:, 0])
        theirs = jnp.where(up, view[:, 0], view[:, 1])
        keep = (mine + swap_dp(theirs.astype(bf16), bit).astype(f32))[None]
        bit *= 2
    total = keep.reshape(per, width)
    bit = 1
    while bit < n_ctx:
        total = total + swap_ctx(total.astype(bf16), bit).astype(f32)
        bit *= 2
    square = jnp.full((8, BLK), jnp.sum(total * total), f32)
    bit = 1
    while bit < n_dp:
        square = square + swap_dp(square, bit)
        bit *= 2
    max_norm = 0.5 * jnp.sqrt(f32(PROMPT * width))
    norm_total = jnp.sqrt(square[0, 0])
    grad_own = lax.dynamic_slice_in_dim(total, ctx * cols_own, cols_own, axis=1)
    clipped = grad_own * (max_norm / jnp.maximum(norm_total, max_norm))
    first_new = beta_first * first_moment + (1.0 - beta_first) * clipped
    second_new = beta_second * second_moment + (1.0 - beta_second) * clipped * clipped
    prompt_new = prompt - learn_rate * (first_new / first_fix) / (jnp.sqrt(second_new / second_fix) + adam_eps)
    return (output, prompt_new, first_new, second_new)


def back_of(count, k):
    def target(d, z):
        half, c, r = d % 2, z // count, z % count
        return (2 * (d // 2) + c, half * count + (r - k) % count)

    return target


def solution(mesh):
    rows, cols = P("dp", "ctx", None), P("dp", "ctx")
    placed = (rows, cols, cols, rows) + (P(),) * 9 + (cols,) * 3
    return jax.shard_map(
        functools.partial(on_device, (mesh.shape["dp"], mesh.shape["ctx"])),
        mesh=mesh,
        in_specs=placed,
        out_specs=(rows, cols, cols, cols),
        check_vma=False,
    )
```

```python
import functools

import jax
import jax.numpy as jnp
import numpy as np
from jax import lax
from jax.experimental import pallas as pl
from jax.experimental.pallas import tpu as pltpu
from jax.sharding import PartitionSpec as P

PROMPT = 100
HEAD = 64
PAIR = 2 * HEAD
BLK = 128
QROWS = 256
norm_eps = 1e-06
beta_first = 0.9
beta_second = 0.999
adam_eps = 1e-08
learn_rate = 0.1
first_fix = 1.0 - 0.9**8
second_fix = 1.0 - 0.999**8
far_marks = (12, 16, 23, 32, 46, 64, 91)
f32 = jnp.float32
bf16 = jnp.bfloat16
i32 = jnp.int32
MASKED = -float(2**30)
AXES = ("dp", "ctx")
MIB = 1 << 20
A_MIB, F_MIB, B_MIB = 6, 12, 13


def bucket_table(offset):
    distance = np.abs(offset)
    passed = sum((distance >= mark).astype(np.int32) for mark in far_marks)
    far_ids = np.minimum(8 + passed, 15)
    return np.where(distance < 8, distance, far_ids) + 16 * (offset > 0).astype(np.int32)


def dot_nn(a, b):
    return lax.dot_general(a, b, (((1,), (0,)), ((), ())), preferred_element_type=f32)


def dot_nt(a, b):
    return lax.dot_general(a, b, (((1,), (1,)), ((), ())), preferred_element_type=f32)


def dot_tn(a, b):
    return lax.dot_general(a, b, (((0,), (0,)), ((), ())), preferred_element_type=f32)


def split_two(values):
    high = values.astype(bf16)
    return high, (values - high.astype(f32)).astype(bf16)


def inv_rms(values):
    return lax.rsqrt(jnp.mean(values * values, axis=-1, keepdims=True) + norm_eps)


def segment_of(place, first, second):
    seg = (place >= first).astype(i32) + (place >= second).astype(i32)
    start = jnp.where(seg == 0, 0, jnp.where(seg == 1, first, second))
    return seg, place - start


def vmem_spec():
    return pl.BlockSpec(memory_space=pltpu.VMEM)


def smem_spec():
    return pl.BlockSpec(memory_space=pltpu.SMEM)


def any_spec():
    return pl.BlockSpec(memory_space=pl.ANY)


def out(shape, dtype):
    return jax.ShapeDtypeStruct(shape, dtype)


def held(shape, dtype):
    return pltpu.VMEM(shape, dtype)


def in_vmem(value):
    return pltpu.with_memory_space_constraint(value, pltpu.VMEM)


def in_hbm(value):
    return pltpu.with_memory_space_constraint(value, pltpu.HBM)


def params(mib):
    return pltpu.CompilerParams(vmem_limit_bytes=mib * MIB)


def cost(flops, nbytes, trans=0):
    return pl.CostEstimate(flops=int(flops), bytes_accessed=int(nbytes), transcendentals=int(trans))


def pick_piece(pieces, turn, j):
    count = len(pieces)
    place = lax.rem(turn - j + count, count)
    picked = pieces[0][...]
    for k in range(1, count):
        picked = jnp.where(place == k, pieces[k][...], picked)
    return picked


def slot_of(index, count):
    return lax.rem(index + 2 * count, count)


def pack_kernel(count, tokens_ref, seg_ref, prompt_ref, *refs):
    pieces, (block_ref, wide_ref, sems) = refs[:count], refs[count:]
    ctx = lax.axis_index("ctx")
    copies = [
        pltpu.make_async_copy(tokens_ref.at[slot_of(ctx + k, count)], pieces[k], sems.at[k]) for k in range(count)
    ]
    for copy in copies:
        copy.start()
    rows = prompt_ref.shape[0]
    wide_ref[...] = jnp.zeros_like(wide_ref)
    wide_ref[0:rows, :] = prompt_ref[...]
    for n in range(2):
        tally = jnp.sum((seg_ref[...] <= n).astype(f32), axis=1, keepdims=True)
        wide_ref[rows + n * count : rows + (n + 1) * count, :] = jnp.broadcast_to(tally, (count, prompt_ref.shape[1]))
    block_ref[...] = wide_ref[...].astype(bf16)
    for copy in copies:
        copy.wait()


def prepare_kernel(count, base_ref, cot_ref, *refs):
    weights, (tile_ref, table_ref) = refs[:6], refs[6:8]
    pieces, kept, sems = refs[8 : 8 + count], refs[8 + count : 14 + count], refs[14 + count]
    ctx = lax.axis_index("ctx")
    copies = [pltpu.make_async_copy(weights[n], kept[n], sems.at[n]) for n in range(6)] + [
        pltpu.make_async_copy(cot_ref.at[slot_of(ctx + k, count)], pieces[k], sems.at[6 + k]) for k in range(count)
    ]
    for copy in copies:
        copy.start()
    heads = tile_ref.shape[0]
    for h in range(heads):
        row = jnp.broadcast_to(base_ref[h : h + 1, :], (BLK, 4 * BLK))
        spread = pltpu.roll(row, 0, 1, stride=1, stride_axis=0)
        low, mid, top = (spread[:, k * BLK : (k + 1) * BLK] for k in (1, 2, 3))
        tile_ref[h, 0] = low
        tile_ref[h, 1] = mid
        tile_ref[h, 2] = top
        mid_high, mid_low = split_two(mid)
        low_high, low_low = split_two(low)
        table_ref[h, 0:BLK, :] = mid_high
        table_ref[h, BLK : 2 * BLK, :] = low_high
        table_ref[h, 2 * BLK : 3 * BLK, :] = mid_low
        table_ref[h, 3 * BLK : 4 * BLK, :] = low_low
    for copy in copies:
        copy.wait()


def places(count):
    return lax.rem(lax.axis_index("dp"), 2), lax.rem(lax.axis_index("ctx"), count)


def first_kernel(count, piece, rows_own, *refs):
    own = refs[:count]
    (
        block_ref, other_ref, prompt_ref, gain_ref, wq_ref, wk_ref, wv_ref,
        marks_ref, hid_ref, q_ref, kall_ref, vall_ref, norm_ref,
    ) = refs[count:]
    half, turn = places(count)
    half_len = count * piece
    width = q_ref.shape[1]
    mine = lax.div(lax.axis_index("ctx"), count) == half
    line = jnp.where(mine, block_ref[...], other_ref[...]).astype(f32)
    line_row = lax.broadcasted_iota(i32, (line.shape[0], 1), 0)
    marks = []
    for n in range(2):
        tally = jnp.where(line_row == rows_own + n * count + turn, line, 0.0)
        tally = jnp.sum(jnp.sum(tally, axis=1, keepdims=True), axis=0, keepdims=True)
        marks.append((tally * (1.0 / (width // lax.axis_size("ctx"))) + 0.5).astype(i32))
        marks_ref[n : n + 1, :] = jnp.broadcast_to(marks[n], (1, BLK))
    first, second = marks
    gain = gain_ref[...]
    slots = lax.broadcasted_iota(i32, (1, BLK), 1)
    for j in range(count):
        rows = slice(j * piece, (j + 1) * piece)
        place = half * half_len + j * piece + lax.broadcasted_iota(i32, (piece, 1), 0)
        inside = segment_of(place, first, second)[1]
        shown = inside < PROMPT
        choose = jnp.where((inside == slots) & shown, 1.0, 0.0).astype(bf16)
        picked = dot_nn(choose, prompt_ref[...])
        hidden = jnp.where(shown, picked, pick_piece(own, turn, j).astype(f32))
        hid_ref[rows, :] = hidden.astype(bf16)
        norm_ref[rows, :] = (hidden * inv_rms(hidden) * gain).astype(bf16)
    hidden = prompt_ref[...].astype(f32)
    norm_ref[half_len:, :] = (hidden * inv_rms(hidden) * gain).astype(bf16)
    wide = 2 * BLK

    @pl.loop(0, width // wide)
    def _(t):
        cols = pl.ds(pl.multiple_of(t * wide, wide), wide)
        q_ref[:, cols] = dot_nn(norm_ref[0:half_len, :], wq_ref[:, cols]).astype(bf16)
        for all_ref, weight_ref in ((kall_ref, wk_ref), (vall_ref, wv_ref)):
            made = dot_nn(norm_ref[...], weight_ref[:, cols]).astype(bf16)
            all_ref[0:half_len, cols] = made[:half_len]
            all_ref[2 * half_len :, cols] = made[half_len:]


def forward_kernel(count, piece, tab_ref, *refs):
    partner = refs[:count]
    (
        marks_ref, q_ref, hid_ref, kown_ref, vown_ref, gain_first_ref, gain_second_ref, wk_ref, wv_ref, wo_ref, wi_ref,
        wout_ref, tile_ref, table_ref,
    ) = refs[count : count + 14]
    e_ref, kall_ref, vall_ref, mixed_ref, inv_ref, after_ref, act_ref = refs[count + 14 : count + 21]
    going, (norm_ref, e_buf, sems) = refs[count + 21 : 2 * count + 21], refs[2 * count + 21 :]
    half, turn = places(count)
    first, second = marks_ref[0:1, 0:1], marks_ref[1:2, 0:1]
    half_len = count * piece
    width = q_ref.shape[1]
    gain = gain_first_ref[...]
    for j in range(count):
        tok = pick_piece(partner, turn, j).astype(f32)
        norm_ref[j * piece : (j + 1) * piece, :] = (tok * inv_rms(tok) * gain).astype(bf16)
    wide = 2 * BLK

    @pl.loop(0, width // wide)
    def _(t):
        cols = pl.ds(pl.multiple_of(t * wide, wide), wide)
        kall_ref[half_len : 2 * half_len, cols] = dot_nn(norm_ref[...], wk_ref[:, cols]).astype(bf16)
        vall_ref[half_len : 2 * half_len, cols] = dot_nn(norm_ref[...], wv_ref[:, cols]).astype(bf16)

    lane = lax.broadcasted_iota(i32, (1, PAIR), 1)
    low_lane = lane < HEAD
    lane_seg = lax.rem(lane, HEAD)
    spot = lax.broadcasted_iota(i32, (half_len, 1), 0)
    own_seg, own_inside = segment_of(half * half_len + spot, first, second)
    par_seg, par_inside = segment_of((1 - half) * half_len + spot, first, second)
    q_aug = jnp.where(own_seg == lane_seg, 1.0, 0.0).astype(bf16)

    def key_aug(seg, inside):
        closed = ((seg != lane_seg) | (inside < PROMPT)) & (lane_seg < 3)
        return jnp.where(closed, MASKED, 0.0).astype(bf16)

    slot = lax.broadcasted_iota(i32, (BLK, 1), 0)
    k_aug = jnp.concatenate(
        [
            key_aug(own_seg, own_inside),
            key_aug(par_seg, par_inside),
            jnp.where((slot >= PROMPT) & (lane_seg < 3), MASKED, 0.0).astype(bf16),
        ],
        axis=0,
    )
    far = lax.rem(lax.broadcasted_iota(i32, (1, 4 * BLK), 1), 2 * BLK)
    spread = jnp.where(jnp.minimum(own_inside, 2 * BLK - 1) == far, 1.0, 0.0).astype(bf16)
    blocks = half_len // BLK
    per = QROWS // BLK

    def e_copy(hp):
        at = lax.rem(hp, 2)
        return pltpu.make_async_copy(e_buf.at[at], e_ref.at[hp], sems.at[at])

    @pl.loop(0, width // PAIR)
    def _(hp):
        @pl.when(hp >= 2)
        def _():
            e_copy(hp - 2).wait()

        cols = pl.ds(pl.multiple_of(hp * PAIR, PAIR), PAIR)
        q_pair, k_pair, v_pair = q_ref[:, cols], kall_ref[:, cols], vall_ref[:, cols]
        results = []
        for s in range(2):
            h = 2 * hp + s
            keep = low_lane if s == 0 else jnp.logical_not(low_lane)
            q_e = jnp.where(keep, q_pair, q_aug)
            k_e = jnp.where(keep, k_pair, k_aug)
            v_e = jnp.where(keep, v_pair, jnp.ones((), bf16))
            back_far, ahead_far = tab_ref[15, h], tab_ref[31, h]
            other_far = jnp.where(half == 0, ahead_far, back_far)
            table = table_ref[h]
            head_rows = []
            for qt in range(half_len // QROWS):
                qrows = slice(qt * QROWS, (qt + 1) * QROWS)
                raw = dot_nt(q_e[qrows], k_e)
                prompt_bias = dot_nn(spread[qrows], table)
                e_rows = []
                for sub in range(per):
                    qb = qt * per + sub
                    rr = slice(sub * BLK, (sub + 1) * BLK)
                    parts, consts = [], []
                    for kb in range(2 * blocks):
                        part = raw[rr, kb * BLK : (kb + 1) * BLK]
                        const = None
                        if kb < blocks:
                            gap = kb - qb
                            if abs(gap) <= 1:
                                part = part + tile_ref[h, gap + 1]
                            else:
                                const = 0 if gap < 0 else 1
                        elif qb == blocks - 1 and kb == blocks:
                            part = part + jnp.where(half == 0, tile_ref[h, 2], back_far)
                        elif qb == 0 and kb == 2 * blocks - 1:
                            part = part + jnp.where(half == 0, ahead_far, tile_ref[h, 0])
                        else:
                            const = 2
                        parts.append(part)
                        consts.append(const)
                    parts.append(raw[rr, 2 * blocks * BLK :] + prompt_bias[rr])
                    consts.append(None)
                    values = (back_far, ahead_far, other_far)
                    best = None
                    for group in (None, 0, 1, 2):
                        members = [p for p, c in zip(parts, consts) if c == group]
                        if not members:
                            continue
                        top = functools.reduce(jnp.maximum, members)
                        if group is not None:
                            top = top + values[group]
                        best = top if best is None else jnp.maximum(best, top)
                    peak = jnp.max(best, axis=1, keepdims=True)
                    shifts = [peak - value for value in values]
                    e_rows.append(
                        jnp.concatenate(
                            [
                                jnp.exp(p - (peak if c is None else shifts[c])).astype(bf16)
                                for p, c in zip(parts, consts)
                            ],
                            axis=1,
                        )
                    )
                raised = jnp.concatenate(e_rows, axis=0)
                e_buf[lax.rem(hp, 2), s, qrows, :] = raised
                head_rows.append(dot_nn(raised, v_e))
            results.append(jnp.concatenate(head_rows, axis=0))
        sums = pltpu.roll(jnp.where(low_lane, results[1], results[0]), HEAD, 1)
        inv = 1.0 / sums
        inv_ref[:, cols] = inv
        mixed_ref[:, cols] = (jnp.where(low_lane, results[0], results[1]) * inv).astype(bf16)
        e_copy(hp).start()

    @pl.loop(0, half_len // BLK)
    def _(t):
        rows = pl.ds(pl.multiple_of(t * BLK, BLK), BLK)
        after = hid_ref[rows, :].astype(f32) + dot_nn(mixed_ref[rows, :], wo_ref[...])
        after_ref[rows, :] = after
        norm_ref[rows, :] = (after * inv_rms(after) * gain_second_ref[...]).astype(bf16)

    @pl.loop(0, wi_ref.shape[1] // wide)
    def _(t):
        cols = pl.ds(pl.multiple_of(t * wide, wide), wide)
        act_ref[:, cols] = jnp.maximum(dot_nn(norm_ref[...], wi_ref[:, cols]), 0.0).astype(bf16)

    @pl.loop(0, width // wide)
    def _(t):
        cols = pl.ds(pl.multiple_of(t * wide, wide), wide)
        made = (after_ref[:, cols] + dot_nn(act_ref[...], wout_ref[:, cols])).astype(bf16)
        made = [made[j * piece : (j + 1) * piece] for j in range(count)]
        for k in range(count):
            place = slot_of(turn - k, count)
            sent = made[0]
            for j in range(1, count):
                sent = jnp.where(place == j, made[j], sent)
            going[k][:, cols] = sent

    for hp in range(width // PAIR - 2, width // PAIR):
        e_copy(hp).wait()


def backward_kernel(count, piece, *refs):
    cots = refs[:count]
    (
        marks_ref, act_ref, after_ref, mixed_ref, inv_ref, q_ref, kall_ref, vall_ref, prompt_ref, gain_first_ref, gain_second_ref,
        wout_ref, wi_ref, wo_ref, wq_ref, wk_ref, wv_ref, e_ref,
        grad_ref,
        cot_ref, acc_ref, do_ref, dq_ref, gk_ref, gv_ref, e_buf, sems,
    ) = refs[count:]
    half, turn = places(count)
    first, second = marks_ref[0:1, 0:1], marks_ref[1:2, 0:1]
    half_len = count * piece
    width = q_ref.shape[1]
    pairs = width // PAIR

    def e_copy(hp):
        at = lax.rem(hp, 2)
        return pltpu.make_async_copy(e_ref.at[hp], e_buf.at[at], sems.at[at])

    for hp in range(2):
        e_copy(hp).start()
    for j in range(count):
        cot_ref[j * piece : (j + 1) * piece, :] = pick_piece(cots, turn, j)
    wide = 4 * BLK
    acc_ref[...] = jnp.zeros_like(acc_ref)

    @pl.loop(0, wi_ref.shape[1] // wide)
    def _(t):
        cols = pl.ds(pl.multiple_of(t * wide, wide), wide)
        grad_act = dot_nt(cot_ref[...], wout_ref[cols, :])
        grad_inner = jnp.where(act_ref[:, cols] > 0, grad_act, 0.0).astype(bf16)
        acc_ref[...] += dot_nt(grad_inner, wi_ref[:, cols])

    gain = gain_second_ref[...]

    @pl.loop(0, half_len // BLK)
    def _(t):
        rows = pl.ds(pl.multiple_of(t * BLK, BLK), BLK)
        after = after_ref[rows, :]
        scale = inv_rms(after)
        pulled = gain * acc_ref[rows, :]
        along = jnp.mean(after * pulled, axis=-1, keepdims=True)
        grad_after = cot_ref[rows, :].astype(f32) + scale * pulled - after * (scale * scale * scale * along)
        acc_ref[rows, :] = grad_after
        grad_mixed = dot_nt(grad_after.astype(bf16), wo_ref[...])
        do_ref[rows, :] = (grad_mixed * inv_ref[rows, :]).astype(bf16)

    lane = lax.broadcasted_iota(i32, (1, PAIR), 1)
    low_lane = lane < HEAD
    lane_at = lax.rem(lane, HEAD)

    @pl.loop(0, width // PAIR)
    def _(hp):
        e_copy(hp).wait()
        cols = pl.ds(pl.multiple_of(hp * PAIR, PAIR), PAIR)
        q_pair, k_pair, v_pair, do_pair = q_ref[:, cols], kall_ref[:, cols], vall_ref[:, cols], do_ref[:, cols]
        inner = do_pair.astype(f32) * mixed_ref[:, cols].astype(f32)
        dqs, dks, dvs = [], [], []
        for s in range(2):
            keep = low_lane if s == 0 else jnp.logical_not(low_lane)
            delta = jnp.sum(jnp.where(keep, inner, 0.0), axis=1, keepdims=True)
            high, low = split_two(-delta)
            aug = jnp.where(lane_at == 0, high, jnp.where(lane_at == 1, low, jnp.zeros((), bf16)))
            do_e = jnp.where(keep, do_pair, aug)
            v_e = jnp.where(keep, v_pair, jnp.ones((), bf16))
            dq, dk, dv = [], None, None
            for qt in range(half_len // QROWS):
                qrows = slice(qt * QROWS, (qt + 1) * QROWS)
                raised = e_buf[lax.rem(hp, 2), s, qrows, :]
                grad_probs = dot_nt(do_e[qrows], v_e)
                grad_scores = (raised.astype(f32) * grad_probs).astype(bf16)
                dq.append(dot_nn(grad_scores, k_pair))
                dk_now = dot_tn(grad_scores[:, 2 * half_len :], q_pair[qrows])
                dv_now = dot_tn(raised[:, 2 * half_len :], do_pair[qrows])
                dk = dk_now if dk is None else dk + dk_now
                dv = dv_now if dv is None else dv + dv_now
            dqs.append(jnp.concatenate(dq, axis=0))
            dks.append(dk)
            dvs.append(dv)
        dq_ref[:, cols] = jnp.where(low_lane, dqs[0], dqs[1]).astype(bf16)
        gk_ref[:, cols] = jnp.where(low_lane, dks[0], dks[1]).astype(bf16)
        gv_ref[:, cols] = jnp.where(low_lane, dvs[0], dvs[1]).astype(bf16)

        @pl.when(hp + 2 < pairs)
        def _():
            e_copy(hp + 2).start()

    spot = lax.broadcasted_iota(i32, (1, half_len), 1)
    inside = segment_of(half * half_len + spot, first, second)[1]
    slots = lax.broadcasted_iota(i32, (BLK, 1), 0)
    choose = jnp.where((inside == slots) & (inside < PROMPT), 1.0, 0.0).astype(bf16)
    gq = dot_nn(choose, dq_ref[...]).astype(bf16)
    pulled = dot_nt(gq, wq_ref[...]) + dot_nt(gk_ref[...], wk_ref[...]) + dot_nt(gv_ref[...], wv_ref[...])
    high, low = split_two(acc_ref[...])
    direct = dot_nn(choose, high) + dot_nn(choose, low)
    hidden = prompt_ref[...].astype(f32)
    scale = inv_rms(hidden)
    pulled = gain_first_ref[...] * pulled
    along = jnp.mean(hidden * pulled, axis=-1, keepdims=True)
    grad_ref[...] = direct + scale * pulled - hidden * (scale * scale * scale * along)


def on_device(
    sizes, tokens, segment_ids, prompt_slots, cotangent, w_query, w_key, w_value, w_output, w_inner, w_outer,
    gain_first, gain_second, bias_table, prompt, first_moment, second_moment,
):
    n_dp, n_ctx = sizes
    count, piece, width = tokens.shape
    half_len = count * piece
    heads = bias_table.shape[1]
    dp, ctx = lax.axis_index("dp"), lax.axis_index("ctx")
    core = lax.rem(dp, 2)

    def permute(value, target):
        pairs = []
        for d in range(n_dp):
            for z in range(n_ctx):
                d2, z2 = target(d, z)
                pairs.append((d * n_ctx + z, d2 * n_ctx + z2))
        return lax.ppermute(value, AXES, pairs)

    def swap_dp(value, bit):
        return permute(value, lambda d, z: (d ^ bit, z))

    def swap_ctx(value, bit):
        return permute(value, lambda d, z: (d, z ^ bit))

    def there(k):
        return lambda d, z: (2 * (d // 2) + z // count, (d % 2) * count + (z + k) % count)

    def in_order(parts, me, axis):
        ordered = []
        for place in range(len(parts)):
            picked = parts[0]
            for n in range(1, len(parts)):
                picked = jnp.where((me ^ n) == place, parts[n], picked)
            ordered.append(picked)
        return jnp.concatenate(ordered, axis=axis)

    rows_own, cols_own = prompt.shape
    piece_like = held((piece, width), bf16)
    packed = pl.pallas_call(
        functools.partial(pack_kernel, count),
        out_shape=[piece_like] * count + [held((rows_own + 8, cols_own), bf16)],
        in_specs=[any_spec(), vmem_spec(), vmem_spec()],
        out_specs=[vmem_spec()] * (count + 1),
        scratch_shapes=[pltpu.VMEM((rows_own + 8, cols_own), f32), pltpu.SemaphoreType.DMA((count,))],
        compiler_params=params(4),
        cost_estimate=cost(1e5, 2e6),
    )(in_hbm(tokens), segment_ids, prompt)

    block = packed[count]
    blocks = [block] + [swap_ctx(block, n) for n in range(1, n_ctx)]
    own = [permute(packed[k], there(k)) for k in range(count)]
    block = in_order(blocks, ctx, 1)
    other = swap_dp(block, 1)
    chip_rows = in_order([block[:rows_own], other[:rows_own]], core, 0)
    sent = in_order([chip_rows] + [swap_dp(chip_rows, 2 * n) for n in range(1, n_dp // 2)], dp // 2, 0)

    choose = (np.arange(bias_table.shape[0])[:, None] == bucket_table(np.arange(4 * BLK) - 2 * BLK)[None]).astype(np.float32)
    base = lax.dot_general(
        bias_table, jnp.asarray(choose), (((0,), (0,)), ((), ())), precision=lax.Precision.HIGHEST
    )
    weights = (w_query, w_key, w_value, w_output, w_inner, w_outer)
    prepared = pl.pallas_call(
        functools.partial(prepare_kernel, count),
        out_shape=[held((heads, 3, BLK, BLK), f32), held((heads, 4 * BLK, BLK), bf16)]
        + [piece_like] * count
        + [held(w.shape, bf16) for w in weights],
        in_specs=[vmem_spec()] + [any_spec()] * 7,
        out_specs=[vmem_spec()] * (8 + count),
        scratch_shapes=[pltpu.SemaphoreType.DMA((6 + count,))],
        compiler_params=params(4),
        cost_estimate=cost(1e6, 1.5e7),
    )(base, in_hbm(cotangent), *[in_hbm(w) for w in weights])
    tiles, table = prepared[:2]
    cot_pieces = prepared[2 : 2 + count]
    w_q, w_k, w_v, w_o, w_i, w_out = prepared[2 + count :]

    gain_1, gain_2 = gain_first[None], gain_second[None]
    keys_all = 2 * half_len + BLK
    hidden_ff = w_inner.shape[1]
    partner = [swap_dp(piece_rows, 1) for piece_rows in own]
    marks, hid, q, kall, vall = pl.pallas_call(
        functools.partial(first_kernel, count, piece, rows_own),
        out_shape=[
            held((8, BLK), i32),
            held((half_len, width), bf16),
            held((half_len, width), bf16),
            held((keys_all, width), bf16),
            held((keys_all, width), bf16),
        ],
        in_specs=[vmem_spec()] * (count + 7),
        out_specs=[vmem_spec()] * 5,
        scratch_shapes=[pltpu.VMEM((half_len + BLK, width), bf16)],
        compiler_params=params(A_MIB),
        cost_estimate=cost(6 * half_len * width * width, 8e6),
    )(*own, block, other, sent, gain_1, w_q, w_k, w_v)

    cot_pieces, q = lax.optimization_barrier((cot_pieces, q))
    cots = [permute(cot_pieces[k], there(k)) for k in range(count)]

    made = pl.pallas_call(
        functools.partial(forward_kernel, count, piece),
        out_shape=[
            pltpu.HBM((heads // 2, 2, half_len, keys_all), bf16),
            held((keys_all, width), bf16),
            held((keys_all, width), bf16),
            held((half_len, width), bf16),
            held((half_len, width), f32),
            held((half_len, width), f32),
            held((half_len, hidden_ff), bf16),
        ]
        + [piece_like] * count,
        in_specs=[smem_spec()] + [vmem_spec()] * (count + 14),
        out_specs=[any_spec()] + [vmem_spec()] * (6 + count),
        scratch_shapes=[
            pltpu.VMEM((half_len, width), bf16),
            pltpu.VMEM((2, 2, half_len, keys_all), bf16),
            pltpu.SemaphoreType.DMA((2,)),
        ],
        input_output_aliases={count + 4: 1, count + 5: 2},
        compiler_params=params(F_MIB),
        cost_estimate=cost(3e10, 4e7, heads * half_len * keys_all),
    )(
        bias_table, *partner, marks, q, hid, kall, vall, gain_1, gain_2, w_k, w_v, w_o, w_i, w_out, tiles, table,
    )
    e, kall, vall, mixed, inv, after, act = made[:7]
    got = [permute(made[7 + k], back_of(count, k)) for k in range(count)]

    grad = pl.pallas_call(
        functools.partial(backward_kernel, count, piece),
        out_shape=held((BLK, width), f32),
        in_specs=[vmem_spec()] * (count + 17) + [any_spec()],
        out_specs=vmem_spec(),
        scratch_shapes=[
            pltpu.VMEM((half_len, width), bf16),
            pltpu.VMEM((half_len, width), f32),
            pltpu.VMEM((half_len, width), bf16),
            pltpu.VMEM((half_len, width), bf16),
            pltpu.VMEM((BLK, width), bf16),
            pltpu.VMEM((BLK, width), bf16),
            pltpu.VMEM((2, 2, half_len, keys_all), bf16),
            pltpu.SemaphoreType.DMA((2,)),
        ],
        compiler_params=params(B_MIB),
        cost_estimate=cost(3e10, 4e7),
    )(
        *cots, marks, act, after, mixed, inv, q, kall, vall, sent, gain_1, gain_2, w_out, w_i, w_o, w_q, w_k, w_v, in_hbm(e),
    )

    got, grad = lax.optimization_barrier((got, grad))
    order = [lax.rem(ctx + j, count) for j in range(count)]
    output = jnp.stack(
        [functools.reduce(lambda a, k: jnp.where(order[k] == r, got[k], a), range(1, count), got[0]) for r in range(count)]
    )

    per = rows_own
    view = grad.reshape(n_dp // 2, 2, per, width)
    mine = jnp.where(core == 1, view[:, 1], view[:, 0])
    theirs = jnp.where(core == 1, view[:, 0], view[:, 1]).astype(bf16)
    total = (mine + swap_dp(theirs, 1).astype(f32)).reshape(n_dp // 2 * per, width)
    plane = total.astype(bf16)
    for n in range(1, n_dp // 2):
        total = total + swap_dp(plane, 2 * n).astype(f32)
    line = total.astype(bf16)
    for n in range(1, n_ctx):
        total = total + swap_ctx(line, n).astype(f32)
    square = jnp.full((8, BLK), jnp.sum(total * total), f32)
    square = square + swap_dp(square, 1)
    max_norm = 0.5 * jnp.sqrt(f32(PROMPT * width))
    norm_total = jnp.sqrt(square[0, 0])
    grad_own = lax.dynamic_slice(total, (dp // 2 * per, ctx * cols_own), (per, cols_own))
    clipped = grad_own * (max_norm / jnp.maximum(norm_total, max_norm))
    first_new = beta_first * first_moment + (1.0 - beta_first) * clipped
    second_new = beta_second * second_moment + (1.0 - beta_second) * clipped * clipped
    prompt_new = prompt - learn_rate * (first_new / first_fix) / (jnp.sqrt(second_new / second_fix) + adam_eps)
    return (output, prompt_new, first_new, second_new)


def back_of(count, k):
    def target(d, z):
        half, c, r = d % 2, z // count, z % count
        return (2 * (d // 2) + c, half * count + (r - k) % count)

    return target


def solution(mesh):
    rows, cols = P("dp", "ctx", None), P("dp", "ctx")
    placed = (rows, cols, cols, rows) + (P(),) * 9 + (cols,) * 3
    return jax.shard_map(
        functools.partial(on_device, (mesh.shape["dp"], mesh.shape["ctx"])),
        mesh=mesh,
        in_specs=placed,
        out_specs=(rows, cols, cols, cols),
        check_vma=False,
    )
```

```python
import functools

import jax
import jax.numpy as jnp
import numpy as np
from jax import lax
from jax.experimental import pallas as pl
from jax.experimental.pallas import tpu as pltpu
from jax.sharding import PartitionSpec as P

PROMPT = 100
HEAD = 64
PAIR = 2 * HEAD
BLK = 128
norm_eps = 1e-06
beta_first = 0.9
beta_second = 0.999
adam_eps = 1e-08
learn_rate = 0.1
first_fix = 1.0 - 0.9**8
second_fix = 1.0 - 0.999**8
far_marks = (12, 16, 23, 32, 46, 64, 91)
f32 = jnp.float32
bf16 = jnp.bfloat16
i32 = jnp.int32
MASKED = -float(2**30)
AXES = ("dp", "ctx")
MIB = 1 << 20
A_MIB, F_MIB, B_MIB = 6, 20, 18


def bucket_table(offset):
    distance = np.abs(offset)
    passed = sum((distance >= mark).astype(np.int32) for mark in far_marks)
    far_ids = np.minimum(8 + passed, 15)
    return np.where(distance < 8, distance, far_ids) + 16 * (offset > 0).astype(np.int32)


def dot_nn(a, b):
    return lax.dot_general(a, b, (((1,), (0,)), ((), ())), preferred_element_type=f32)


def dot_nt(a, b):
    return lax.dot_general(a, b, (((1,), (1,)), ((), ())), preferred_element_type=f32)


def dot_tn(a, b):
    return lax.dot_general(a, b, (((0,), (0,)), ((), ())), preferred_element_type=f32)


def split_two(values):
    high = values.astype(bf16)
    return high, (values - high.astype(f32)).astype(bf16)


def inv_rms(values):
    return lax.rsqrt(jnp.mean(values * values, axis=-1, keepdims=True) + norm_eps)


def segment_of(place, first, second):
    seg = (place >= first).astype(i32) + (place >= second).astype(i32)
    start = jnp.where(seg == 0, 0, jnp.where(seg == 1, first, second))
    return seg, place - start


def vmem_spec():
    return pl.BlockSpec(memory_space=pltpu.VMEM)


def smem_spec():
    return pl.BlockSpec(memory_space=pltpu.SMEM)


def any_spec():
    return pl.BlockSpec(memory_space=pl.ANY)


def out(shape, dtype):
    return jax.ShapeDtypeStruct(shape, dtype)


def held(shape, dtype):
    return pltpu.VMEM(shape, dtype)


def in_vmem(value):
    return pltpu.with_memory_space_constraint(value, pltpu.VMEM)


def in_hbm(value):
    return pltpu.with_memory_space_constraint(value, pltpu.HBM)


def params(mib):
    return pltpu.CompilerParams(vmem_limit_bytes=mib * MIB)


def cost(flops, nbytes, trans=0):
    return pl.CostEstimate(flops=int(flops), bytes_accessed=int(nbytes), transcendentals=int(trans))


def pick_piece(pieces, turn, j):
    count = len(pieces)
    place = lax.rem(turn - j + count, count)
    picked = pieces[0][...]
    for k in range(1, count):
        picked = jnp.where(place == k, pieces[k][...], picked)
    return picked


def slot_of(index, count):
    return lax.rem(index + 2 * count, count)


def pack_kernel(count, tokens_ref, seg_hbm, prompt_hbm, *refs):
    pieces, (block_ref, seg_ref, prompt_ref, wide_ref, sems) = refs[:count], refs[count:]
    ctx = lax.axis_index("ctx")
    copies = [
        pltpu.make_async_copy(tokens_ref.at[slot_of(ctx + k, count)], pieces[k], sems.at[k]) for k in range(count)
    ]
    small = [
        pltpu.make_async_copy(seg_hbm, seg_ref, sems.at[count]),
        pltpu.make_async_copy(prompt_hbm, prompt_ref, sems.at[count + 1]),
    ]
    for copy in small + copies:
        copy.start()
    for copy in small:
        copy.wait()
    rows = prompt_ref.shape[0]
    wide_ref[...] = jnp.zeros_like(wide_ref)
    wide_ref[0:rows, :] = prompt_ref[...]
    for n in range(2):
        tally = jnp.sum((seg_ref[...] <= n).astype(f32), axis=1, keepdims=True)
        wide_ref[rows + n * count : rows + (n + 1) * count, :] = jnp.broadcast_to(tally, (count, prompt_ref.shape[1]))
    block_ref[...] = wide_ref[...].astype(bf16)
    for copy in copies:
        copy.wait()


def prepare_kernel(count, base_ref, gain_first_ref, gain_second_ref, cot_ref, *refs):
    weights, (tile_ref, table_ref, first_ref, second_ref) = refs[:6], refs[6:10]
    pieces, kept, sems = refs[10 : 10 + count], refs[10 + count : 16 + count], refs[16 + count]
    first_ref[...] = gain_first_ref[...]
    second_ref[...] = gain_second_ref[...]
    ctx = lax.axis_index("ctx")
    copies = [pltpu.make_async_copy(weights[n], kept[n], sems.at[n]) for n in range(6)] + [
        pltpu.make_async_copy(cot_ref.at[slot_of(ctx + k, count)], pieces[k], sems.at[6 + k]) for k in range(count)
    ]
    for copy in copies:
        copy.start()
    heads = tile_ref.shape[0]
    for h in range(heads):
        row = jnp.broadcast_to(base_ref[h : h + 1, :], (BLK, 4 * BLK))
        spread = pltpu.roll(row, 0, 1, stride=1, stride_axis=0)
        low, mid, top = (spread[:, k * BLK : (k + 1) * BLK] for k in (3, 2, 1))
        tile_ref[h, 0] = low
        tile_ref[h, 1] = mid
        tile_ref[h, 2] = top
        rows = slice(h * BLK, (h + 1) * BLK)
        parts = [part for pair in zip(split_two(mid), split_two(low)) for part in pair]
        for k in range(4):
            table_ref[rows, k * BLK : (k + 1) * BLK] = parts[k]
    for copy in copies:
        copy.wait()


def places(count):
    return lax.rem(lax.axis_index("dp"), 2), lax.rem(lax.axis_index("ctx"), count)


def first_kernel(count, piece, *refs):
    own = refs[:count]
    gain_ref, wk_ref, wv_ref, kall_ref, vall_ref, norm_ref = refs[count:]
    turn = places(count)[1]
    half_len = count * piece
    gain = gain_ref[...]
    for j in range(count):
        tok = pick_piece(own, turn, j).astype(f32)
        norm_ref[j * piece : (j + 1) * piece, :] = (tok * inv_rms(tok) * gain).astype(bf16)
    wide = 2 * BLK

    @pl.loop(0, gain.shape[1] // wide)
    def _(t):
        cols = pl.ds(pl.multiple_of(t * wide, wide), wide)
        kall_ref[0:half_len, cols] = dot_nn(norm_ref[...], wk_ref[:, cols]).astype(bf16)
        vall_ref[0:half_len, cols] = dot_nn(norm_ref[...], wv_ref[:, cols]).astype(bf16)


def forward_kernel(count, piece, rows_own, *refs):
    own, partner = refs[:count], refs[count : 2 * count]
    (
        block_ref, other_ref, prompt_ref, kown_ref, vown_ref, gain_first_ref, gain_second_ref, wq_ref, wk_ref, wv_ref,
        wo_ref, wi_ref, wout_ref, tile_ref, table_ref,
    ) = refs[2 * count : 2 * count + 15]
    refs = refs[2 * count + 15 :]
    e_ref, marks_ref, q_ref, kall_ref, vall_ref, mixed_ref, inv_ref, after_ref, act_ref = refs[:9]
    going, (norm_ref, hid_ref, slot_bias_ref, e_buf, sems) = refs[9 : 9 + count], refs[9 + count :]
    half, turn = places(count)
    half_len = count * piece
    width = q_ref.shape[1]
    mine = lax.div(lax.axis_index("ctx"), count) == half
    line = jnp.where(mine, block_ref[...], other_ref[...]).astype(f32)
    line_row = lax.broadcasted_iota(i32, (line.shape[0], 1), 0)
    marks = []
    for n in range(2):
        tally = jnp.where(line_row == rows_own + n * count + turn, line, 0.0)
        tally = jnp.sum(jnp.sum(tally, axis=1, keepdims=True), axis=0, keepdims=True)
        marks.append((tally * (1.0 / (width // lax.axis_size("ctx"))) + 0.5).astype(i32))
        marks_ref[n : n + 1, :] = jnp.broadcast_to(marks[n], (1, BLK))
    first, second = marks
    gain = gain_first_ref[...]
    slots = lax.broadcasted_iota(i32, (1, BLK), 1)
    for j in range(count):
        rows = slice(j * piece, (j + 1) * piece)
        place = half * half_len + j * piece + lax.broadcasted_iota(i32, (piece, 1), 0)
        inside = segment_of(place, first, second)[1]
        shown = inside < PROMPT
        choose = jnp.where((inside == slots) & shown, 1.0, 0.0).astype(bf16)
        picked = dot_nn(choose, prompt_ref[...])
        hidden = jnp.where(shown, picked, pick_piece(own, turn, j).astype(f32))
        hid_ref[rows, :] = hidden.astype(bf16)
        norm_ref[half_len + BLK + j * piece : half_len + BLK + (j + 1) * piece, :] = (
            hidden * inv_rms(hidden) * gain
        ).astype(bf16)
        tok = pick_piece(partner, turn, j).astype(f32)
        norm_ref[rows, :] = (tok * inv_rms(tok) * gain).astype(bf16)
    hidden = prompt_ref[...].astype(f32)
    norm_ref[half_len : half_len + BLK, :] = (hidden * inv_rms(hidden) * gain).astype(bf16)
    wide = 2 * BLK

    @pl.loop(0, width // wide)
    def _(t):
        cols = pl.ds(pl.multiple_of(t * wide, wide), wide)
        kall_ref[half_len:, cols] = dot_nn(norm_ref[0 : half_len + BLK, :], wk_ref[:, cols]).astype(bf16)
        vall_ref[half_len:, cols] = dot_nn(norm_ref[0 : half_len + BLK, :], wv_ref[:, cols]).astype(bf16)
        q_ref[:, cols] = dot_nn(norm_ref[half_len + BLK :, :], wq_ref[:, cols]).astype(bf16)

    lane = lax.broadcasted_iota(i32, (1, PAIR), 1)
    low_lane = lane < HEAD
    lane_seg = lax.rem(lane, HEAD)
    spot = lax.broadcasted_iota(i32, (half_len, 1), 0)
    own_seg, own_inside = segment_of(half * half_len + spot, first, second)
    par_seg, par_inside = segment_of((1 - half) * half_len + spot, first, second)
    q_aug = jnp.where(own_seg == lane_seg, 1.0, 0.0).astype(bf16)

    def key_aug(seg, inside):
        closed = ((seg != lane_seg) | (inside < PROMPT)) & (lane_seg < 3)
        return jnp.where(closed, MASKED, 0.0).astype(bf16)

    slot = lax.broadcasted_iota(i32, (BLK, 1), 0)
    k_aug = jnp.concatenate(
        [
            key_aug(own_seg, own_inside),
            key_aug(par_seg, par_inside),
            jnp.where((slot >= PROMPT) & (lane_seg < 3), MASKED, 0.0).astype(bf16),
        ],
        axis=0,
    )
    across = segment_of(half * half_len + lax.broadcasted_iota(i32, (1, half_len), 1), first, second)[1]
    far = lax.rem(lax.broadcasted_iota(i32, (4 * BLK, 1), 0), 2 * BLK)
    spread = jnp.where(jnp.minimum(across, 2 * BLK - 1) == far, 1.0, 0.0).astype(bf16)
    slot_bias_ref[...] = dot_nn(table_ref[...], spread)
    blocks = half_len // BLK
    ones = jnp.ones((16, 2 * half_len + BLK), bf16)

    def e_copy(hp):
        at = lax.rem(hp, 2)
        return pltpu.make_async_copy(e_buf.at[at], e_ref.at[hp], sems.at[at])

    @pl.loop(0, width // PAIR)
    def _(hp):
        @pl.when(hp >= 2)
        def _():
            e_copy(hp - 2).wait()

        cols = pl.ds(pl.multiple_of(hp * PAIR, PAIR), PAIR)
        q_pair, k_pair = q_ref[:, cols], kall_ref[:, cols]
        v_turned = vall_ref[:, cols].T
        for s in range(2):
            h = 2 * hp + s
            keep = low_lane if s == 0 else jnp.logical_not(low_lane)
            raw = dot_nt(jnp.where(keep, k_pair, k_aug), jnp.where(keep, q_pair, q_aug))
            back_far, ahead_far = tile_ref[h, 0, 0:1, BLK - 1 :], tile_ref[h, 2, BLK - 1 :, 0:1]
            other_far = jnp.where(half == 0, ahead_far, back_far)
            values = (back_far, ahead_far, other_far)
            slot_bias = slot_bias_ref[pl.ds(pl.multiple_of(h * BLK, BLK), BLK), :]
            columns = []
            for qb in range(blocks):
                here = slice(qb * BLK, (qb + 1) * BLK)
                parts, consts = [], []
                for kb in range(2 * blocks):
                    part = raw[kb * BLK : (kb + 1) * BLK, here]
                    const = None
                    if kb < blocks:
                        gap = kb - qb
                        if abs(gap) <= 1:
                            part = part + tile_ref[h, gap + 1]
                        else:
                            const = 0 if gap < 0 else 1
                    elif qb == blocks - 1 and kb == blocks:
                        part = part + jnp.where(half == 0, tile_ref[h, 2], back_far)
                    elif qb == 0 and kb == 2 * blocks - 1:
                        part = part + jnp.where(half == 0, ahead_far, tile_ref[h, 0])
                    else:
                        const = 2
                    parts.append(part)
                    consts.append(const)
                parts.append(raw[2 * blocks * BLK :, here] + slot_bias[:, here])
                consts.append(None)
                peak = None
                for group in (None, 0, 1, 2):
                    members = [p for p, c in zip(parts, consts) if c == group]
                    if not members:
                        continue
                    top = jnp.max(functools.reduce(jnp.maximum, members), axis=0, keepdims=True)
                    if group is not None:
                        top = top + values[group]
                    peak = top if peak is None else jnp.maximum(peak, top)
                shifts = [peak - value for value in values]
                columns.append(
                    [jnp.exp(p - (peak if c is None else shifts[c])).astype(bf16) for p, c in zip(parts, consts)]
                )
            raised = jnp.concatenate(
                [jnp.concatenate([column[kb] for column in columns], axis=1) for kb in range(2 * blocks + 1)], axis=0
            )
            e_buf[lax.rem(hp, 2), s] = raised
            turned = jnp.concatenate([v_turned[s * HEAD : (s + 1) * HEAD], ones], axis=0)
            total = dot_nn(turned, raised)
            inv = 1.0 / total[HEAD : HEAD + 1]
            inv_ref[pl.ds(h, 1), :] = inv
            mixed_ref[pl.ds(pl.multiple_of(h * HEAD, HEAD), HEAD), :] = (total[:HEAD] * inv).astype(bf16)
        e_copy(hp).start()

    @pl.loop(0, half_len // BLK)
    def _(t):
        rows = pl.ds(pl.multiple_of(t * BLK, BLK), BLK)
        after = hid_ref[rows, :].astype(f32) + dot_tn(mixed_ref[:, rows], wo_ref[...])
        after_ref[rows, :] = after
        norm_ref[rows, :] = (after * inv_rms(after) * gain_second_ref[...]).astype(bf16)

    @pl.loop(0, wi_ref.shape[1] // wide)
    def _(t):
        cols = pl.ds(pl.multiple_of(t * wide, wide), wide)
        act_ref[:, cols] = jnp.maximum(dot_nn(norm_ref[0:half_len, :], wi_ref[:, cols]), 0.0).astype(bf16)

    @pl.loop(0, width // wide)
    def _(t):
        cols = pl.ds(pl.multiple_of(t * wide, wide), wide)
        made = (after_ref[:, cols] + dot_nn(act_ref[...], wout_ref[:, cols])).astype(bf16)
        made = [made[j * piece : (j + 1) * piece] for j in range(count)]
        for k in range(count):
            place = slot_of(turn - k, count)
            sent = made[0]
            for j in range(1, count):
                sent = jnp.where(place == j, made[j], sent)
            going[k][:, cols] = sent

    for hp in range(width // PAIR - 2, width // PAIR):
        e_copy(hp).wait()


def backward_kernel(count, piece, *refs):
    cots = refs[:count]
    (
        marks_ref, act_ref, after_ref, mixed_ref, inv_ref, q_ref, kall_ref, vall_ref, prompt_ref, gain_first_ref, gain_second_ref,
        wout_ref, wi_ref, wo_ref, wq_ref, wk_ref, wv_ref, e_ref,
        grad_ref,
        cot_ref, acc_ref, low_ref, do_ref, dq_ref, gk_ref, gv_ref, e_buf, sems,
    ) = refs[count:]
    half, turn = places(count)
    first, second = marks_ref[0:1, 0:1], marks_ref[1:2, 0:1]
    half_len = count * piece
    width = q_ref.shape[1]
    pairs = width // PAIR

    def e_copy(hp):
        at = lax.rem(hp, 2)
        return pltpu.make_async_copy(e_ref.at[hp], e_buf.at[at], sems.at[at])

    for hp in range(2):
        e_copy(hp).start()
    for j in range(count):
        cot_ref[j * piece : (j + 1) * piece, :] = pick_piece(cots, turn, j)
    wide = 4 * BLK
    acc_ref[...] = jnp.zeros_like(acc_ref)

    @pl.loop(0, wi_ref.shape[1] // wide)
    def _(t):
        cols = pl.ds(pl.multiple_of(t * wide, wide), wide)
        grad_act = dot_nt(cot_ref[...], wout_ref[cols, :])
        grad_inner = jnp.where(act_ref[:, cols] > 0, grad_act, 0.0).astype(bf16)
        acc_ref[...] += dot_nt(grad_inner, wi_ref[:, cols])

    gain = gain_second_ref[...]

    @pl.loop(0, half_len // BLK)
    def _(t):
        rows = pl.ds(pl.multiple_of(t * BLK, BLK), BLK)
        after = after_ref[rows, :]
        scale = inv_rms(after)
        pulled = gain * acc_ref[rows, :]
        along = jnp.mean(after * pulled, axis=-1, keepdims=True)
        grad_after = cot_ref[rows, :].astype(f32) + scale * pulled - after * (scale * scale * scale * along)
        acc_ref[rows, :] = grad_after
        low_ref[rows, :] = grad_after.astype(bf16)

    do_ref[...] = dot_nt(wo_ref[...], low_ref[...])

    low_lane = lax.broadcasted_iota(i32, (1, PAIR), 1) < HEAD
    row = lax.broadcasted_iota(i32, (PAIR, 1), 0)
    row_at = lax.rem(row, HEAD)

    @pl.loop(0, pairs)
    def _(hp):
        e_copy(hp).wait()
        cols = pl.ds(pl.multiple_of(hp * PAIR, PAIR), PAIR)
        q_pair, k_turned, v_pair = q_ref[:, cols], kall_ref[:, cols].T, vall_ref[:, cols]
        inv_both = jnp.where(row < HEAD, inv_ref[pl.ds(2 * hp, 1), :], inv_ref[pl.ds(2 * hp + 1, 1), :])
        do_pair = (do_ref[cols, :] * inv_both).astype(bf16)
        inner = do_pair.astype(f32) * mixed_ref[cols, :].astype(f32)
        slot_scores, slot_raised = [], []
        for s in range(2):
            mine = (row < HEAD) == (s == 0)
            keep = low_lane if s == 0 else jnp.logical_not(low_lane)
            high, low = split_two(-jnp.sum(inner[s * HEAD : (s + 1) * HEAD], axis=0, keepdims=True))
            zero = jnp.zeros((), bf16)
            do_e = jnp.where(mine, do_pair, jnp.where(row_at == 0, high, jnp.where(row_at == 1, low, zero)))
            raised = e_buf[lax.rem(hp, 2), s]
            grad_probs = dot_nn(jnp.where(keep, v_pair, jnp.ones((), bf16)), do_e)
            grad_scores = (raised.astype(f32) * grad_probs).astype(bf16)
            made = dot_nn(k_turned[s * HEAD : (s + 1) * HEAD], grad_scores)
            dq_ref[pl.ds(pl.multiple_of(hp * PAIR + s * HEAD, HEAD), HEAD), :] = made.astype(bf16)
            slot_scores.append(grad_scores[2 * half_len :])
            slot_raised.append(raised[2 * half_len :])
        dk = dot_nn(jnp.concatenate(slot_scores, axis=0), q_pair)
        dv = dot_nt(jnp.concatenate(slot_raised, axis=0), do_pair)
        gk_ref[:, cols] = jnp.where(low_lane, dk[:BLK], dk[BLK:]).astype(bf16)
        gv_ref[:, cols] = jnp.where(low_lane, dv[:BLK], dv[BLK:]).astype(bf16)

        @pl.when(hp + 2 < pairs)
        def _():
            e_copy(hp + 2).start()

    spot = lax.broadcasted_iota(i32, (1, half_len), 1)
    inside = segment_of(half * half_len + spot, first, second)[1]
    slots = lax.broadcasted_iota(i32, (BLK, 1), 0)
    choose = jnp.where((inside == slots) & (inside < PROMPT), 1.0, 0.0).astype(bf16)
    gq = dot_nt(choose, dq_ref[...]).astype(bf16)
    pulled = dot_nt(gq, wq_ref[...]) + dot_nt(gk_ref[...], wk_ref[...]) + dot_nt(gv_ref[...], wv_ref[...])
    high, low = split_two(acc_ref[...])
    direct = dot_nn(choose, high) + dot_nn(choose, low)
    hidden = prompt_ref[...].astype(f32)
    scale = inv_rms(hidden)
    pulled = gain_first_ref[...] * pulled
    along = jnp.mean(hidden * pulled, axis=-1, keepdims=True)
    grad_ref[...] = direct + scale * pulled - hidden * (scale * scale * scale * along)


def on_device(
    sizes, tokens, segment_ids, prompt_slots, cotangent, w_query, w_key, w_value, w_output, w_inner, w_outer,
    gain_first, gain_second, bias_table, prompt, first_moment, second_moment,
):
    n_dp, n_ctx = sizes
    count, piece, width = tokens.shape
    half_len = count * piece
    heads = bias_table.shape[1]
    dp, ctx = lax.axis_index("dp"), lax.axis_index("ctx")
    core = lax.rem(dp, 2)

    def permute(value, target):
        pairs = []
        for d in range(n_dp):
            for z in range(n_ctx):
                d2, z2 = target(d, z)
                pairs.append((d * n_ctx + z, d2 * n_ctx + z2))
        return lax.ppermute(value, AXES, pairs)

    def swap_dp(value, bit):
        return permute(value, lambda d, z: (d ^ bit, z))

    def swap_ctx(value, bit):
        return permute(value, lambda d, z: (d, z ^ bit))

    def there(k):
        return lambda d, z: (2 * (d // 2) + z // count, (d % 2) * count + (z + k) % count)

    def in_order(parts, me, axis):
        ordered = []
        for place in range(len(parts)):
            picked = parts[0]
            for n in range(1, len(parts)):
                picked = jnp.where((me ^ n) == place, parts[n], picked)
            ordered.append(picked)
        return jnp.concatenate(ordered, axis=axis)

    rows_own, cols_own = prompt.shape
    piece_like = held((piece, width), bf16)
    packed = pl.pallas_call(
        functools.partial(pack_kernel, count),
        out_shape=[piece_like] * count + [held((rows_own + 8, cols_own), bf16)],
        in_specs=[any_spec()] * 3,
        out_specs=[vmem_spec()] * (count + 1),
        scratch_shapes=[
            pltpu.VMEM(segment_ids.shape, i32),
            pltpu.VMEM(prompt.shape, f32),
            pltpu.VMEM((rows_own + 8, cols_own), f32),
            pltpu.SemaphoreType.DMA((count + 2,)),
        ],
        compiler_params=params(4),
        cost_estimate=cost(1e5, 2e6),
    )(in_hbm(tokens), in_hbm(segment_ids), in_hbm(prompt))

    block = packed[count]
    blocks = [block] + [swap_ctx(block, n) for n in range(1, n_ctx)]
    own = [permute(packed[k], there(k)) for k in range(count)]
    choose = (np.arange(bias_table.shape[0])[:, None] == bucket_table(2 * BLK - np.arange(4 * BLK))[None]).astype(np.float32)
    base = lax.dot_general(
        bias_table, jnp.asarray(choose), (((0,), (0,)), ((), ())), precision=lax.Precision.HIGHEST
    )
    weights = (w_query, w_key, w_value, w_output, w_inner, w_outer)
    prepared = pl.pallas_call(
        functools.partial(prepare_kernel, count),
        out_shape=[held((heads, 3, BLK, BLK), f32), held((heads * BLK, 4 * BLK), bf16)]
        + [held((1, width), f32)] * 2
        + [piece_like] * count
        + [held(w.shape, bf16) for w in weights],
        in_specs=[vmem_spec()] * 3 + [any_spec()] * 7,
        out_specs=[vmem_spec()] * (10 + count),
        scratch_shapes=[pltpu.SemaphoreType.DMA((6 + count,))],
        compiler_params=params(4),
        cost_estimate=cost(1e6, 1.5e7),
    )(base, gain_first[None], gain_second[None], in_hbm(cotangent), *[in_hbm(w) for w in weights])
    tiles, table, gain_1, gain_2 = prepared[:4]
    cot_pieces = prepared[4 : 4 + count]
    w_q, w_k, w_v, w_o, w_i, w_out = prepared[4 + count :]

    block = in_order(blocks, ctx, 1)
    other = swap_dp(block, 1)
    chip_rows = in_order([block[:rows_own], other[:rows_own]], core, 0)
    sent = in_order([chip_rows] + [swap_dp(chip_rows, 2 * n) for n in range(1, n_dp // 2)], dp // 2, 0)

    keys_all = 2 * half_len + BLK
    hidden_ff = w_inner.shape[1]
    partner = [swap_dp(piece_rows, 1) for piece_rows in own]
    kall, vall = pl.pallas_call(
        functools.partial(first_kernel, count, piece),
        out_shape=[held((keys_all, width), bf16), held((keys_all, width), bf16)],
        in_specs=[vmem_spec()] * (count + 3),
        out_specs=[vmem_spec()] * 2,
        scratch_shapes=[pltpu.VMEM((half_len, width), bf16)],
        compiler_params=params(A_MIB),
        cost_estimate=cost(1e10, 8e6),
    )(*own, gain_1, w_k, w_v)
    cots = [permute(cot_pieces[k], there(k)) for k in range(count)]

    made = pl.pallas_call(
        functools.partial(forward_kernel, count, piece, rows_own),
        out_shape=[
            pltpu.HBM((heads // 2, 2, keys_all, half_len), bf16),
            held((8, BLK), i32),
            held((half_len, width), bf16),
            held((keys_all, width), bf16),
            held((keys_all, width), bf16),
            held((width, half_len), bf16),
            held((heads, half_len), f32),
            held((half_len, width), f32),
            held((half_len, hidden_ff), bf16),
        ]
        + [piece_like] * count,
        in_specs=[vmem_spec()] * (2 * count + 15),
        out_specs=[any_spec()] + [vmem_spec()] * (8 + count),
        scratch_shapes=[
            pltpu.VMEM((2 * half_len + BLK, width), bf16),
            pltpu.VMEM((half_len, width), bf16),
            pltpu.VMEM((heads * BLK, half_len), f32),
            pltpu.VMEM((2, 2, keys_all, half_len), bf16),
            pltpu.SemaphoreType.DMA((2,)),
        ],
        input_output_aliases={2 * count + 3: 3, 2 * count + 4: 4},
        compiler_params=params(F_MIB),
        cost_estimate=cost(3e10, 4e7, heads * half_len * keys_all),
    )(
        *own, *partner, block, other, sent, kall, vall, gain_1, gain_2, w_q, w_k, w_v, w_o, w_i, w_out, tiles,
        table,
    )
    got = [permute(made[9 + k], back_of(count, k)) for k in range(count)]
    e, marks, q, kall, vall, mixed, inv, after, act = made[:9]

    grad = pl.pallas_call(
        functools.partial(backward_kernel, count, piece),
        out_shape=held((BLK, width), f32),
        in_specs=[vmem_spec()] * (count + 17) + [any_spec()],
        out_specs=vmem_spec(),
        scratch_shapes=[
            pltpu.VMEM((half_len, width), bf16),
            pltpu.VMEM((half_len, width), f32),
            pltpu.VMEM((half_len, width), bf16),
            pltpu.VMEM((width, half_len), f32),
            pltpu.VMEM((width, half_len), bf16),
            pltpu.VMEM((BLK, width), bf16),
            pltpu.VMEM((BLK, width), bf16),
            pltpu.VMEM((2, 2, keys_all, half_len), bf16),
            pltpu.SemaphoreType.DMA((2,)),
        ],
        compiler_params=params(B_MIB),
        cost_estimate=cost(3e10, 4e7),
    )(
        *cots, marks, act, after, mixed, inv, q, kall, vall, sent, gain_1, gain_2, w_out, w_i, w_o, w_q, w_k, w_v, in_hbm(e),
    )

    got, grad = lax.optimization_barrier((got, grad))
    order = [lax.rem(ctx + j, count) for j in range(count)]
    output = jnp.stack(
        [functools.reduce(lambda a, k: jnp.where(order[k] == r, got[k], a), range(1, count), got[0]) for r in range(count)]
    )

    per = rows_own
    view = grad.reshape(n_dp // 2, 2, per, width)
    mine = jnp.where(core == 1, view[:, 1], view[:, 0])
    theirs = jnp.where(core == 1, view[:, 0], view[:, 1]).astype(bf16)
    total = (mine + swap_dp(theirs, 1).astype(f32)).reshape(n_dp // 2 * per, width)
    plane = total.astype(bf16)
    for n in range(1, n_dp // 2):
        total = total + swap_dp(plane, 2 * n).astype(f32)
    line = total.astype(bf16)
    for n in range(1, n_ctx):
        total = total + swap_ctx(line, n).astype(f32)
    square = jnp.full((8, BLK), jnp.sum(total * total), f32)
    square = square + swap_dp(square, 1)
    max_norm = 0.5 * jnp.sqrt(f32(PROMPT * width))
    norm_total = jnp.sqrt(square[0, 0])
    grad_own = lax.dynamic_slice(total, (dp // 2 * per, ctx * cols_own), (per, cols_own))
    clipped = grad_own * (max_norm / jnp.maximum(norm_total, max_norm))
    first_new = beta_first * first_moment + (1.0 - beta_first) * clipped
    second_new = beta_second * second_moment + (1.0 - beta_second) * clipped * clipped
    prompt_new = prompt - learn_rate * (first_new / first_fix) / (jnp.sqrt(second_new / second_fix) + adam_eps)
    return (output, prompt_new, first_new, second_new)


def back_of(count, k):
    def target(d, z):
        half, c, r = d % 2, z // count, z % count
        return (2 * (d // 2) + c, half * count + (r - k) % count)

    return target


def solution(mesh):
    rows, cols = P("dp", "ctx", None), P("dp", "ctx")
    placed = (rows, cols, cols, rows) + (P(),) * 9 + (cols,) * 3
    return jax.shard_map(
        functools.partial(on_device, (mesh.shape["dp"], mesh.shape["ctx"])),
        mesh=mesh,
        in_specs=placed,
        out_specs=(rows, cols, cols, cols),
        check_vma=False,
    )
```

```python
import functools

import jax
import jax.numpy as jnp
import numpy as np
from jax import lax
from jax.experimental import pallas as pl
from jax.experimental.pallas import tpu as pltpu
from jax.sharding import PartitionSpec as P

PROMPT = 100
HEAD = 64
PAIR = 2 * HEAD
BLK = 128
QCOLS = 256
norm_eps = 1e-06
beta_first = 0.9
beta_second = 0.999
adam_eps = 1e-08
learn_rate = 0.1
first_fix = 1.0 - 0.9**8
second_fix = 1.0 - 0.999**8
far_marks = (12, 16, 23, 32, 46, 64, 91)
f32 = jnp.float32
bf16 = jnp.bfloat16
i32 = jnp.int32
MASKED = -float(2**30)
AXES = ("dp", "ctx")
MIB = 1 << 20
A_MIB, F_MIB, B_MIB = 6, 20, 18


def bucket_table(offset):
    distance = np.abs(offset)
    passed = sum((distance >= mark).astype(np.int32) for mark in far_marks)
    far_ids = np.minimum(8 + passed, 15)
    return np.where(distance < 8, distance, far_ids) + 16 * (offset > 0).astype(np.int32)


def dot_nn(a, b):
    return lax.dot_general(a, b, (((1,), (0,)), ((), ())), preferred_element_type=f32)


def dot_nt(a, b):
    return lax.dot_general(a, b, (((1,), (1,)), ((), ())), preferred_element_type=f32)


def dot_tn(a, b):
    return lax.dot_general(a, b, (((0,), (0,)), ((), ())), preferred_element_type=f32)


def split_two(values):
    high = values.astype(bf16)
    return high, (values - high.astype(f32)).astype(bf16)


def inv_rms(values):
    return lax.rsqrt(jnp.mean(values * values, axis=-1, keepdims=True) + norm_eps)


def segment_of(place, first, second):
    seg = (place >= first).astype(i32) + (place >= second).astype(i32)
    start = jnp.where(seg == 0, 0, jnp.where(seg == 1, first, second))
    return seg, place - start


def vmem_spec():
    return pl.BlockSpec(memory_space=pltpu.VMEM)


def smem_spec():
    return pl.BlockSpec(memory_space=pltpu.SMEM)


def any_spec():
    return pl.BlockSpec(memory_space=pl.ANY)


def out(shape, dtype):
    return jax.ShapeDtypeStruct(shape, dtype)


def held(shape, dtype):
    return pltpu.VMEM(shape, dtype)


def in_vmem(value):
    return pltpu.with_memory_space_constraint(value, pltpu.VMEM)


def in_hbm(value):
    return pltpu.with_memory_space_constraint(value, pltpu.HBM)


def params(mib):
    return pltpu.CompilerParams(vmem_limit_bytes=mib * MIB)


def cost(flops, nbytes, trans=0):
    return pl.CostEstimate(flops=int(flops), bytes_accessed=int(nbytes), transcendentals=int(trans))


def pick_piece(pieces, turn, j):
    count = len(pieces)
    place = lax.rem(turn - j + count, count)
    picked = pieces[0][...]
    for k in range(1, count):
        picked = jnp.where(place == k, pieces[k][...], picked)
    return picked


def slot_of(index, count):
    return lax.rem(index + 2 * count, count)


def pack_kernel(count, tokens_ref, seg_hbm, prompt_hbm, *refs):
    pieces, (block_ref, seg_ref, prompt_ref, wide_ref, sems) = refs[:count], refs[count:]
    ctx = lax.axis_index("ctx")
    copies = [
        pltpu.make_async_copy(tokens_ref.at[slot_of(ctx + k, count)], pieces[k], sems.at[k]) for k in range(count)
    ]
    small = [
        pltpu.make_async_copy(seg_hbm, seg_ref, sems.at[count]),
        pltpu.make_async_copy(prompt_hbm, prompt_ref, sems.at[count + 1]),
    ]
    for copy in small + copies:
        copy.start()
    for copy in small:
        copy.wait()
    rows = prompt_ref.shape[0]
    wide_ref[...] = jnp.zeros_like(wide_ref)
    wide_ref[0:rows, :] = prompt_ref[...]
    for n in range(2):
        tally = jnp.sum((seg_ref[...] <= n).astype(f32), axis=1, keepdims=True)
        wide_ref[rows + n * count : rows + (n + 1) * count, :] = jnp.broadcast_to(tally, (count, prompt_ref.shape[1]))
    block_ref[...] = wide_ref[...].astype(bf16)
    for copy in copies:
        copy.wait()


def prepare_kernel(count, base_ref, gain_first_ref, gain_second_ref, cot_ref, *refs):
    weights, (tile_ref, table_ref, first_ref, second_ref) = refs[:6], refs[6:10]
    pieces, kept, sems = refs[10 : 10 + count], refs[10 + count : 16 + count], refs[16 + count]
    first_ref[...] = gain_first_ref[...]
    second_ref[...] = gain_second_ref[...]
    ctx = lax.axis_index("ctx")
    copies = [pltpu.make_async_copy(weights[n], kept[n], sems.at[n]) for n in range(6)] + [
        pltpu.make_async_copy(cot_ref.at[slot_of(ctx + k, count)], pieces[k], sems.at[6 + k]) for k in range(count)
    ]
    for copy in copies:
        copy.start()
    heads = tile_ref.shape[0]
    for h in range(heads):
        row = jnp.broadcast_to(base_ref[h : h + 1, :], (BLK, 4 * BLK))
        spread = pltpu.roll(row, 0, 1, stride=1, stride_axis=0)
        low, mid, top = (spread[:, k * BLK : (k + 1) * BLK] for k in (3, 2, 1))
        tile_ref[h, 0] = low
        tile_ref[h, 1] = mid
        tile_ref[h, 2] = top
        rows = slice(h * BLK, (h + 1) * BLK)
        parts = [part for pair in zip(split_two(mid), split_two(low)) for part in pair]
        for k in range(4):
            table_ref[rows, k * BLK : (k + 1) * BLK] = parts[k]
    for copy in copies:
        copy.wait()


def plane_kernel(rows_own, *refs):
    parts, (out_ref, wide_ref) = refs[:-2], refs[-2:]
    core, chip = lax.rem(lax.axis_index("dp"), 2), lax.div(lax.axis_index("dp"), 2)
    high = rows_own + 8
    parts = [part[...].astype(f32) for part in parts]
    parts = [[jnp.where(core == c, part[:high], part[high:]) for c in range(2)] for part in parts]
    for place in range(len(parts)):
        for c in range(2):
            picked = parts[0][c]
            for n in range(1, len(parts)):
                picked = jnp.where((chip ^ n) == place, parts[n][c], picked)
            start = (2 * place + c) * rows_own
            wide_ref[start : start + rows_own, :] = picked[:rows_own]
    for c in range(2):
        wide_ref[BLK + 8 * c : BLK + 8 * (c + 1), :] = parts[0][c][rows_own:]
    out_ref[...] = wide_ref[...].astype(bf16)


def places(count):
    return lax.rem(lax.axis_index("dp"), 2), lax.rem(lax.axis_index("ctx"), count)


def first_kernel(count, piece, *refs):
    own, (gain_ref, norm_ref) = refs[:count], refs[count:]
    turn = places(count)[1]
    for j in range(count):
        tok = pick_piece(own, turn, j).astype(f32)
        norm_ref[j * piece : (j + 1) * piece, :] = (tok * inv_rms(tok) * gain_ref[...]).astype(bf16)


def forward_kernel(count, piece, rows_own, *refs):
    own, partner = refs[:count], refs[count : 2 * count]
    (
        normed_ref, gain_first_ref, gain_second_ref, wq_ref, wk_ref, wv_ref, wo_ref, wi_ref, wout_ref,
        tile_ref, table_ref,
    ) = refs[2 * count : 2 * count + 11]
    refs = refs[2 * count + 11 :]
    cols_of, refs = refs[: 2 * count], refs[2 * count :]
    e_ref, marks_ref, prompt_ref, q_ref, kall_ref, vall_ref, mixed_ref, inv_ref, after_ref, act_ref = refs[:10]
    going, refs = refs[10 : 10 + count], refs[10 + count :]
    norm_ref, hid_ref, slot_bias_ref, score_ref, aug_ref, shown_ref, e_buf, sems = refs
    ctx = lax.axis_index("ctx")
    few = cols_of[0].shape[1]
    for place in range(2 * count):
        picked = cols_of[0][0:BLK]
        for n in range(1, 2 * count):
            picked = jnp.where((ctx ^ n) == place, cols_of[n][0:BLK], picked)
        shown_ref[:, place * few : (place + 1) * few] = picked.astype(f32)
    prompt_ref[...] = shown_ref[...].astype(bf16)
    half, turn = places(count)
    half_len = count * piece
    width = q_ref.shape[1]
    tally = functools.reduce(jnp.add, [cols[BLK:].astype(f32) for cols in cols_of])
    tally_row = lax.broadcasted_iota(i32, (tally.shape[0], 1), 0)
    marks = []
    for n in range(2):
        here = tally_row == 8 * lax.div(ctx, count) + n * count + turn
        total = jnp.sum(jnp.where(here, tally, 0.0), axis=0, keepdims=True)[:, 0:1]
        marks.append((total + 0.5).astype(i32))
        marks_ref[n : n + 1, :] = jnp.broadcast_to(marks[n], (1, BLK))
    first, second = marks
    gain = gain_first_ref[...]
    slots = lax.broadcasted_iota(i32, (1, BLK), 1)
    for j in range(count):
        rows = slice(j * piece, (j + 1) * piece)
        place = half * half_len + j * piece + lax.broadcasted_iota(i32, (piece, 1), 0)
        inside = segment_of(place, first, second)[1]
        shown = inside < PROMPT
        choose = jnp.where((inside == slots) & shown, 1.0, 0.0).astype(bf16)
        picked = dot_nn(choose, prompt_ref[...])
        hidden = jnp.where(shown, picked, pick_piece(own, turn, j).astype(f32))
        hid_ref[rows, :] = hidden.astype(bf16)
        norm_ref[half_len + BLK + j * piece : half_len + BLK + (j + 1) * piece, :] = (
            hidden * inv_rms(hidden) * gain
        ).astype(bf16)
        tok = pick_piece(partner, turn, j).astype(f32)
        norm_ref[rows, :] = (tok * inv_rms(tok) * gain).astype(bf16)
    hidden = prompt_ref[...].astype(f32)
    norm_ref[half_len : half_len + BLK, :] = (hidden * inv_rms(hidden) * gain).astype(bf16)
    wide = 2 * BLK

    @pl.loop(0, width // wide)
    def _(t):
        cols = pl.ds(pl.multiple_of(t * wide, wide), wide)
        normed = jnp.concatenate([normed_ref[...], norm_ref[0 : half_len + BLK, :]], axis=0)
        kall_ref[:, cols] = dot_nn(normed, wk_ref[:, cols]).astype(bf16)
        vall_ref[:, cols] = dot_nn(normed, wv_ref[:, cols]).astype(bf16)
        q_ref[:, cols] = dot_nn(norm_ref[half_len + BLK :, :], wq_ref[:, cols]).astype(bf16)

    lane = lax.broadcasted_iota(i32, (1, PAIR), 1)
    low_lane = lane < HEAD
    lane_seg = lane
    spot = lax.broadcasted_iota(i32, (half_len, 1), 0)
    own_seg, own_inside = segment_of(half * half_len + spot, first, second)
    par_seg, par_inside = segment_of((1 - half) * half_len + spot, first, second)
    q_aug = jnp.where(own_seg == lane_seg, 1.0, 0.0).astype(bf16)

    def key_aug(seg, inside):
        closed = ((seg != lane_seg) | (inside < PROMPT)) & (lane_seg < 3)
        return jnp.where(closed, MASKED, 0.0).astype(bf16)

    slot = lax.broadcasted_iota(i32, (BLK, 1), 0)
    aug_ref[0:half_len] = key_aug(own_seg, own_inside)
    aug_ref[half_len : 2 * half_len] = key_aug(par_seg, par_inside)
    aug_ref[2 * half_len :] = jnp.where((slot >= PROMPT) & (lane_seg < 3), MASKED, 0.0).astype(bf16)
    across = segment_of(half * half_len + lax.broadcasted_iota(i32, (1, half_len), 1), first, second)[1]
    far = lax.rem(lax.broadcasted_iota(i32, (4 * BLK, 1), 0), 2 * BLK)
    spread = jnp.where(jnp.minimum(across, 2 * BLK - 1) == far, 1.0, 0.0).astype(bf16)
    slot_bias_ref[...] = dot_nn(table_ref[...], spread)
    blocks = half_len // BLK
    ones = jnp.ones((16, 2 * half_len + BLK), bf16)

    def e_copy(hp):
        at = lax.rem(hp, 2)
        return pltpu.make_async_copy(e_buf.at[at], e_ref.at[hp], sems.at[at])

    keys_all = 2 * half_len + BLK
    tiles_q = half_len // QCOLS
    chunk = keys_all // 3
    units = [(s, qt) for s in range(2) for qt in range(tiles_q)]

    def kept(s):
        return low_lane if s == 0 else jnp.logical_not(low_lane)

    def score_steps(hp, s, qt, slot):
        cols = pl.ds(pl.multiple_of(hp * PAIR, PAIR), PAIR)
        here = slice(qt * QCOLS, (qt + 1) * QCOLS)
        q_e = jnp.concatenate([jnp.where(kept(s), q_ref[here, cols], jnp.zeros((), bf16)), q_aug[here]], axis=1)

        def step(n):
            rows = slice(n * chunk, (n + 1) * chunk)
            score_ref[slot, rows, :] = dot_nt(jnp.concatenate([kall_ref[rows, cols], aug_ref[rows]], axis=1), q_e)

        return [functools.partial(step, n) for n in range(3)]

    for step in score_steps(0, 0, 0, 0):
        step()

    @pl.loop(0, width // PAIR)
    def _(hp):
        @pl.when(hp >= 2)
        def _():
            e_copy(hp - 2).wait()

        cols = pl.ds(pl.multiple_of(hp * PAIR, PAIR), PAIR)
        v_turned = vall_ref[:, cols].T
        for u, (s, qt) in enumerate(units):
            h = 2 * hp + s
            coming = units[(u + 1) % len(units)]
            at = hp if u + 1 < len(units) else jnp.minimum(hp + 1, width // PAIR - 1)
            steps = score_steps(at, *coming, (u + 1) % 2)
            back_far, ahead_far = tile_ref[h, 0, 0:1, BLK - 1 :], tile_ref[h, 2, BLK - 1 :, 0:1]
            other_far = jnp.where(half == 0, ahead_far, back_far)
            values = (back_far, ahead_far, other_far)
            columns = []
            for sub in range(QCOLS // BLK):
                qb = qt * (QCOLS // BLK) + sub
                here = slice(sub * BLK, (sub + 1) * BLK)

                def part_of(kb):
                    part = score_ref[u % 2, kb * BLK : (kb + 1) * BLK, here]
                    if kb == 2 * blocks:
                        slot_rows = pl.ds(pl.multiple_of(h * BLK, BLK), BLK)
                        return part + slot_bias_ref[slot_rows, qb * BLK : (qb + 1) * BLK], None
                    gap = kb - qb
                    if kb < blocks and abs(gap) <= 1:
                        return part + tile_ref[h, gap + 1], None
                    if kb < blocks:
                        return part, 0 if gap < 0 else 1
                    if qb == blocks - 1 and kb == blocks:
                        return part + jnp.where(half == 0, tile_ref[h, 2], back_far), None
                    if qb == 0 and kb == 2 * blocks - 1:
                        return part + jnp.where(half == 0, ahead_far, tile_ref[h, 0]), None
                    return part, 2

                tops, group = {}, {}
                for kb in range(2 * blocks + 1):
                    part, const = part_of(kb)
                    if const is None:
                        score_ref[u % 2, kb * BLK : (kb + 1) * BLK, here] = part
                    group[kb] = const
                    top = jnp.max(part.reshape(BLK // 8, 8, BLK), axis=0)
                    tops[const] = top if const not in tops else jnp.maximum(tops[const], top)
                    if steps and kb == 4:
                        steps.pop(0)()
                peak = functools.reduce(
                    jnp.maximum, [top if const is None else top + values[const] for const, top in tops.items()]
                )
                peak = jnp.max(peak, axis=0, keepdims=True)
                shifts = [peak - value for value in values]
                column = []
                for kb in range(2 * blocks + 1):
                    part = score_ref[u % 2, kb * BLK : (kb + 1) * BLK, here]
                    shift = peak if group[kb] is None else shifts[group[kb]]
                    column.append(jnp.exp(part - shift).astype(bf16))
                    if steps and kb == 4:
                        steps.pop(0)()
                columns.append(jnp.concatenate(column, axis=0))
            for step in steps:
                step()
            raised = jnp.concatenate(columns, axis=1)
            qcols = slice(qt * QCOLS, (qt + 1) * QCOLS)
            e_buf[lax.rem(hp, 2), s, :, qcols] = raised
            total = dot_nn(jnp.concatenate([v_turned[s * HEAD : (s + 1) * HEAD], ones], axis=0), raised)
            inv = 1.0 / total[HEAD : HEAD + 1]
            inv_ref[pl.ds(h, 1), qcols] = inv
            mixed_ref[pl.ds(pl.multiple_of(h * HEAD, HEAD), HEAD), qcols] = (total[:HEAD] * inv).astype(bf16)
        e_copy(hp).start()

    @pl.loop(0, half_len // BLK)
    def _(t):
        rows = pl.ds(pl.multiple_of(t * BLK, BLK), BLK)
        after = hid_ref[rows, :].astype(f32) + dot_tn(mixed_ref[:, rows], wo_ref[...])
        after_ref[rows, :] = after
        norm_ref[rows, :] = (after * inv_rms(after) * gain_second_ref[...]).astype(bf16)

    @pl.loop(0, wi_ref.shape[1] // wide)
    def _(t):
        cols = pl.ds(pl.multiple_of(t * wide, wide), wide)
        act_ref[:, cols] = jnp.maximum(dot_nn(norm_ref[0:half_len, :], wi_ref[:, cols]), 0.0).astype(bf16)

    @pl.loop(0, width // wide)
    def _(t):
        cols = pl.ds(pl.multiple_of(t * wide, wide), wide)
        made = (after_ref[:, cols] + dot_nn(act_ref[...], wout_ref[:, cols])).astype(bf16)
        made = [made[j * piece : (j + 1) * piece] for j in range(count)]
        for k in range(count):
            place = slot_of(turn - k, count)
            sent = made[0]
            for j in range(1, count):
                sent = jnp.where(place == j, made[j], sent)
            going[k][:, cols] = sent

    for hp in range(width // PAIR - 2, width // PAIR):
        e_copy(hp).wait()


def backward_kernel(count, piece, rows_own, *refs):
    cots = refs[:count]
    (
        marks_ref, act_ref, after_ref, mixed_ref, inv_ref, q_ref, kall_ref, vall_ref, prompt_ref, gain_first_ref, gain_second_ref,
        wout_ref, wi_ref, wo_ref, wq_ref, wk_ref, wv_ref, e_ref,
        kept_ref, sent_ref,
        cot_ref, acc_ref, low_ref, do_ref, dq_ref, gk_ref, gv_ref, cast_ref, e_buf, sems,
    ) = refs[count:]
    half, turn = places(count)
    first, second = marks_ref[0:1, 0:1], marks_ref[1:2, 0:1]
    half_len = count * piece
    width = q_ref.shape[1]
    pairs = width // PAIR

    def e_copy(hp):
        at = lax.rem(hp, 2)
        return pltpu.make_async_copy(e_ref.at[hp], e_buf.at[at], sems.at[at])

    for hp in range(2):
        e_copy(hp).start()
    for j in range(count):
        cot_ref[j * piece : (j + 1) * piece, :] = pick_piece(cots, turn, j)
    wide = 4 * BLK
    acc_ref[...] = jnp.zeros_like(acc_ref)

    @pl.loop(0, wi_ref.shape[1] // wide)
    def _(t):
        cols = pl.ds(pl.multiple_of(t * wide, wide), wide)
        grad_act = dot_nt(cot_ref[...], wout_ref[cols, :])
        grad_inner = jnp.where(act_ref[:, cols] > 0, grad_act, 0.0).astype(bf16)
        acc_ref[...] += dot_nt(grad_inner, wi_ref[:, cols])

    gain = gain_second_ref[...]

    @pl.loop(0, half_len // BLK)
    def _(t):
        rows = pl.ds(pl.multiple_of(t * BLK, BLK), BLK)
        after = after_ref[rows, :]
        scale = inv_rms(after)
        pulled = gain * acc_ref[rows, :]
        along = jnp.mean(after * pulled, axis=-1, keepdims=True)
        grad_after = cot_ref[rows, :].astype(f32) + scale * pulled - after * (scale * scale * scale * along)
        acc_ref[rows, :] = grad_after
        low_ref[rows, :] = grad_after.astype(bf16)

    do_ref[...] = dot_nt(wo_ref[...], low_ref[...])

    low_lane = lax.broadcasted_iota(i32, (1, PAIR), 1) < HEAD
    row = lax.broadcasted_iota(i32, (PAIR, 1), 0)
    ones = jnp.ones((2 * half_len + BLK, PAIR), bf16)

    @pl.loop(0, pairs)
    def _(hp):
        e_copy(hp).wait()
        cols = pl.ds(pl.multiple_of(hp * PAIR, PAIR), PAIR)
        q_pair, k_turned, v_pair = q_ref[:, cols], kall_ref[:, cols].T, vall_ref[:, cols]
        inv_both = jnp.where(row < HEAD, inv_ref[pl.ds(2 * hp, 1), :], inv_ref[pl.ds(2 * hp + 1, 1), :])
        do_pair = (do_ref[cols, :] * inv_both).astype(bf16)
        inner = do_pair.astype(f32) * mixed_ref[cols, :].astype(f32)
        slot_scores, slot_raised = [], []
        for s in range(2):
            mine = (row < HEAD) == (s == 0)
            high, low = split_two(-jnp.sum(inner[s * HEAD : (s + 1) * HEAD], axis=0, keepdims=True))
            zero = jnp.zeros((), bf16)
            shift = jnp.where(row == 0, high, jnp.where(row == 1, low, zero))
            do_e = jnp.concatenate([jnp.where(mine, do_pair, zero), shift], axis=0)
            raised = e_buf[lax.rem(hp, 2), s]
            grad_probs = dot_nn(jnp.concatenate([v_pair, ones], axis=1), do_e)
            grad_scores = (raised.astype(f32) * grad_probs).astype(bf16)
            made = dot_nn(k_turned[s * HEAD : (s + 1) * HEAD], grad_scores)
            dq_ref[pl.ds(pl.multiple_of(hp * PAIR + s * HEAD, HEAD), HEAD), :] = made.astype(bf16)
            slot_scores.append(grad_scores[2 * half_len :])
            slot_raised.append(raised[2 * half_len :])
        dk = dot_nn(jnp.concatenate(slot_scores, axis=0), q_pair)
        dv = dot_nt(jnp.concatenate(slot_raised, axis=0), do_pair)
        gk_ref[:, cols] = jnp.where(low_lane, dk[:BLK], dk[BLK:]).astype(bf16)
        gv_ref[:, cols] = jnp.where(low_lane, dv[:BLK], dv[BLK:]).astype(bf16)

        @pl.when(hp + 2 < pairs)
        def _():
            e_copy(hp + 2).start()

    spot = lax.broadcasted_iota(i32, (1, half_len), 1)
    inside = segment_of(half * half_len + spot, first, second)[1]
    slots = lax.broadcasted_iota(i32, (BLK, 1), 0)
    choose = jnp.where((inside == slots) & (inside < PROMPT), 1.0, 0.0).astype(bf16)
    gq = dot_nt(choose, dq_ref[...]).astype(bf16)
    pulled = dot_nt(gq, wq_ref[...]) + dot_nt(gk_ref[...], wk_ref[...]) + dot_nt(gv_ref[...], wv_ref[...])
    high, low = split_two(acc_ref[...])
    direct = dot_nn(choose, high) + dot_nn(choose, low)
    hidden = prompt_ref[...].astype(f32)
    scale = inv_rms(hidden)
    pulled = gain_first_ref[...] * pulled
    along = jnp.mean(hidden * pulled, axis=-1, keepdims=True)
    grad = direct + scale * pulled - hidden * (scale * scale * scale * along)
    for place in range(BLK // (2 * rows_own)):
        rows = slice(place * rows_own, (place + 1) * rows_own)
        low, high = (grad[(2 * place + c) * rows_own : (2 * place + c + 1) * rows_own] for c in range(2))
        kept_ref[rows, :] = jnp.where(half == 0, low, high)
        cast_ref[rows, :] = jnp.where(half == 0, high, low)
    sent_ref[...] = cast_ref[...].astype(bf16)


def share_kernel(rows_own, kept_ref, came_ref, mine_ref, *refs):
    parts, (total_ref,) = refs[:-1], refs[-1:]
    chip = lax.div(lax.axis_index("dp"), 2)
    total = kept_ref[...] + came_ref[...].astype(f32)
    for place in range(len(parts) + 1):
        total_ref[place] = total[place * rows_own : (place + 1) * rows_own]
    mine_ref[...] = total_ref[chip]
    for n in range(1, len(parts) + 1):
        parts[n - 1][...] = total_ref[chip ^ n].astype(bf16)


def square_kernel(total_ref, *refs):
    parts, (own_ref, square_ref) = refs[:-2], refs[-2:]
    total = total_ref[...]
    for part in parts:
        total = total + part[...].astype(f32)
    few = own_ref.shape[1]
    own = total[:, 0:few]
    for place in range(1, len(parts) + 1):
        own = jnp.where(lax.axis_index("ctx") == place, total[:, place * few : (place + 1) * few], own)
    own_ref[...] = own
    square = jnp.sum(jnp.sum(total * total, axis=1, keepdims=True), axis=0, keepdims=True)
    square_ref[...] = jnp.broadcast_to(square, square_ref.shape)


def update_kernel(max_norm, grad_ref, prompt_ref, first_ref, second_ref, *refs):
    squares, (prompt_out, first_out, second_out) = refs[:-3], refs[-3:]
    square = functools.reduce(jnp.add, [square[0:1, 0:1] for square in squares])
    clipped = grad_ref[...] * (max_norm / jnp.maximum(jnp.sqrt(square), max_norm))
    first_new = beta_first * first_ref[...] + (1.0 - beta_first) * clipped
    second_new = beta_second * second_ref[...] + (1.0 - beta_second) * clipped * clipped
    step = learn_rate * (first_new / first_fix) / (jnp.sqrt(second_new / second_fix) + adam_eps)
    prompt_out[...] = prompt_ref[...] - step
    first_out[...] = first_new
    second_out[...] = second_new


def on_device(
    sizes, tokens, segment_ids, prompt_slots, cotangent, w_query, w_key, w_value, w_output, w_inner, w_outer,
    gain_first, gain_second, bias_table, prompt, first_moment, second_moment,
):
    n_dp, n_ctx = sizes
    count, piece, width = tokens.shape
    half_len = count * piece
    heads = bias_table.shape[1]
    dp, ctx = lax.axis_index("dp"), lax.axis_index("ctx")
    core = lax.rem(dp, 2)

    def permute(value, target):
        pairs = []
        for d in range(n_dp):
            for z in range(n_ctx):
                d2, z2 = target(d, z)
                pairs.append((d * n_ctx + z, d2 * n_ctx + z2))
        return lax.ppermute(value, AXES, pairs)

    def swap_dp(value, bit):
        return permute(value, lambda d, z: (d ^ bit, z))

    def swap_ctx(value, bit):
        return permute(value, lambda d, z: (d, z ^ bit))

    def there(k):
        return lambda d, z: (2 * (d // 2) + z // count, (d % 2) * count + (z + k) % count)

    rows_own, cols_own = prompt.shape
    piece_like = held((piece, width), bf16)
    packed = pl.pallas_call(
        functools.partial(pack_kernel, count),
        out_shape=[piece_like] * count + [held((rows_own + 8, cols_own), bf16)],
        in_specs=[any_spec()] * 3,
        out_specs=[vmem_spec()] * (count + 1),
        scratch_shapes=[
            pltpu.VMEM(segment_ids.shape, i32),
            pltpu.VMEM(prompt.shape, f32),
            pltpu.VMEM((rows_own + 8, cols_own), f32),
            pltpu.SemaphoreType.DMA((count + 2,)),
        ],
        compiler_params=params(4),
        cost_estimate=cost(1e5, 2e6),
    )(in_hbm(tokens), in_hbm(segment_ids), in_hbm(prompt))

    own = [permute(packed[k], there(k)) for k in range(count)]
    chip_rows = jnp.concatenate([packed[count], swap_dp(packed[count], 1)], axis=0)
    chip_parts = [chip_rows] + [swap_dp(chip_rows, 2 * n) for n in range(1, n_dp // 2)]
    plane = pl.pallas_call(
        functools.partial(plane_kernel, rows_own),
        out_shape=held((BLK + 16, cols_own), bf16),
        in_specs=[vmem_spec()] * len(chip_parts),
        out_specs=vmem_spec(),
        scratch_shapes=[pltpu.VMEM((BLK + 16, cols_own), f32)],
        compiler_params=params(4),
        cost_estimate=cost(1e5, 1e5),
    )(*chip_parts)
    cols_of = [plane] + [swap_ctx(plane, n) for n in range(1, n_ctx)]

    choose = (np.arange(bias_table.shape[0])[:, None] == bucket_table(2 * BLK - np.arange(4 * BLK))[None]).astype(np.float32)
    base = lax.dot_general(
        bias_table, jnp.asarray(choose), (((0,), (0,)), ((), ())), precision=lax.Precision.HIGHEST
    )
    weights = (w_query, w_key, w_value, w_output, w_inner, w_outer)
    prepared = pl.pallas_call(
        functools.partial(prepare_kernel, count),
        out_shape=[held((heads, 3, BLK, BLK), f32), held((heads * BLK, 4 * BLK), bf16)]
        + [held((1, width), f32)] * 2
        + [piece_like] * count
        + [held(w.shape, bf16) for w in weights],
        in_specs=[vmem_spec()] * 3 + [any_spec()] * 7,
        out_specs=[vmem_spec()] * (10 + count),
        scratch_shapes=[pltpu.SemaphoreType.DMA((6 + count,))],
        compiler_params=params(4),
        cost_estimate=cost(1e6, 1.5e7),
    )(base, gain_first[None], gain_second[None], in_hbm(cotangent), *[in_hbm(w) for w in weights])
    tiles, table, gain_1, gain_2 = prepared[:4]
    cot_pieces = prepared[4 : 4 + count]
    w_q, w_k, w_v, w_o, w_i, w_out = prepared[4 + count :]

    keys_all = 2 * half_len + BLK
    hidden_ff = w_inner.shape[1]
    partner = [swap_dp(piece_rows, 1) for piece_rows in own]
    normed = pl.pallas_call(
        functools.partial(first_kernel, count, piece),
        out_shape=held((half_len, width), bf16),
        in_specs=[vmem_spec()] * (count + 1),
        out_specs=vmem_spec(),
        compiler_params=params(A_MIB),
        cost_estimate=cost(1e10, 8e6),
    )(*own, gain_1)
    cots = [permute(cot_pieces[k], there(k)) for k in range(count)]

    made = pl.pallas_call(
        functools.partial(forward_kernel, count, piece, rows_own),
        out_shape=[
            pltpu.HBM((heads // 2, 2, keys_all, half_len), bf16),
            held((8, BLK), i32),
            held((BLK, width), bf16),
            held((half_len, width), bf16),
            held((keys_all, width), bf16),
            held((keys_all, width), bf16),
            held((width, half_len), bf16),
            held((heads, half_len), f32),
            held((half_len, width), f32),
            held((half_len, hidden_ff), bf16),
        ]
        + [piece_like] * count,
        in_specs=[vmem_spec()] * (4 * count + 11),
        out_specs=[any_spec()] + [vmem_spec()] * (9 + count),
        scratch_shapes=[
            pltpu.VMEM((2 * half_len + BLK, width), bf16),
            pltpu.VMEM((half_len, width), bf16),
            pltpu.VMEM((heads * BLK, half_len), f32),
            pltpu.VMEM((2, keys_all, QCOLS), f32),
            pltpu.VMEM((keys_all, PAIR), bf16),
            pltpu.VMEM((BLK, width), f32),
            pltpu.VMEM((2, 2, keys_all, half_len), bf16),
            pltpu.SemaphoreType.DMA((2,)),
        ],
        compiler_params=params(F_MIB),
        cost_estimate=cost(3e10, 4e7, heads * half_len * keys_all),
    )(
        *own, *partner, normed, gain_1, gain_2, w_q, w_k, w_v, w_o, w_i, w_out, tiles, table, *cols_of,
    )
    got = [permute(made[10 + k], back_of(count, k)) for k in range(count)]
    e, marks, sent, q, kall, vall, mixed, inv, after, act = made[:10]

    half_rows = n_dp // 2 * rows_own
    kept, leaving = pl.pallas_call(
        functools.partial(backward_kernel, count, piece, rows_own),
        out_shape=[held((half_rows, width), f32), held((half_rows, width), bf16)],
        in_specs=[vmem_spec()] * (count + 17) + [any_spec()],
        out_specs=[vmem_spec()] * 2,
        scratch_shapes=[
            pltpu.VMEM((half_len, width), bf16),
            pltpu.VMEM((half_len, width), f32),
            pltpu.VMEM((half_len, width), bf16),
            pltpu.VMEM((width, half_len), f32),
            pltpu.VMEM((width, half_len), bf16),
            pltpu.VMEM((BLK, width), bf16),
            pltpu.VMEM((BLK, width), bf16),
            pltpu.VMEM((half_rows, width), f32),
            pltpu.VMEM((2, 2, keys_all, half_len), bf16),
            pltpu.SemaphoreType.DMA((2,)),
        ],
        compiler_params=params(B_MIB),
        cost_estimate=cost(3e10, 4e7),
    )(
        *cots, marks, act, after, mixed, inv, q, kall, vall, sent, gain_1, gain_2, w_out, w_i, w_o, w_q, w_k, w_v, in_hbm(e),
    )

    got, leaving = lax.optimization_barrier((got, leaving))
    order = [lax.rem(ctx + j, count) for j in range(count)]
    output = jnp.stack(
        [functools.reduce(lambda a, k: jnp.where(order[k] == r, got[k], a), range(1, count), got[0]) for r in range(count)]
    )

    chips = n_dp // 2
    own_like = held((rows_own, width), f32)
    mine, *parts = pl.pallas_call(
        functools.partial(share_kernel, rows_own),
        out_shape=[own_like] + [held((rows_own, width), bf16)] * (chips - 1),
        in_specs=[vmem_spec()] * 2,
        out_specs=[vmem_spec()] * chips,
        scratch_shapes=[pltpu.VMEM((chips, rows_own, width), f32)],
        compiler_params=params(4),
        cost_estimate=cost(1e5, 1e5),
    )(kept, swap_dp(leaving, 1))
    for n in range(1, chips):
        mine = mine + swap_dp(parts[n - 1], 2 * n).astype(f32)
    line = mine.astype(bf16)
    line_parts = [swap_ctx(line, n) for n in range(1, n_ctx)]
    line_parts, output = lax.optimization_barrier((line_parts, output))
    grad_own, square = pl.pallas_call(
        square_kernel,
        out_shape=[held((rows_own, cols_own), f32), held((8, BLK), f32)],
        in_specs=[vmem_spec()] * n_ctx,
        out_specs=[vmem_spec()] * 2,
        compiler_params=params(4),
        cost_estimate=cost(1e5, 1e5),
    )(mine, *line_parts)
    square = square + swap_dp(square, 1)
    squares = [square] + [swap_dp(square, 2 * n) for n in range(1, chips)]
    own_out = out((rows_own, cols_own), f32)
    prompt_new, first_new, second_new = pl.pallas_call(
        functools.partial(update_kernel, float(0.5 * np.sqrt(np.float32(PROMPT * width)))),
        out_shape=[own_out] * 3,
        in_specs=[vmem_spec()] * (4 + chips),
        out_specs=[vmem_spec()] * 3,
        compiler_params=params(4),
        cost_estimate=cost(1e5, 1e5),
    )(grad_own, prompt, first_moment, second_moment, *squares)
    return (output, prompt_new, first_new, second_new)


def back_of(count, k):
    def target(d, z):
        half, c, r = d % 2, z // count, z % count
        return (2 * (d // 2) + c, half * count + (r - k) % count)

    return target


def solution(mesh):
    rows, cols = P("dp", "ctx", None), P("dp", "ctx")
    placed = (rows, cols, cols, rows) + (P(),) * 9 + (cols,) * 3
    return jax.shard_map(
        functools.partial(on_device, (mesh.shape["dp"], mesh.shape["ctx"])),
        mesh=mesh,
        in_specs=placed,
        out_specs=(rows, cols, cols, cols),
        check_vma=False,
    )
```

```python
import functools

import jax
import jax.numpy as jnp
import numpy as np
from jax import lax
from jax.experimental import pallas as pl
from jax.experimental.pallas import tpu as pltpu
from jax.sharding import PartitionSpec as P

PROMPT = 100
HEAD = 64
PAIR = 2 * HEAD
BLK = 128
SHOWN = 112
QCOLS = 256
norm_eps = 1e-06
beta_first = 0.9
beta_second = 0.999
adam_eps = 1e-08
learn_rate = 0.1
first_fix = 1.0 - 0.9**8
second_fix = 1.0 - 0.999**8
far_marks = (12, 16, 23, 32, 46, 64, 91)
f32 = jnp.float32
bf16 = jnp.bfloat16
i32 = jnp.int32
MASKED = -float(2**30)
AXES = ("dp", "ctx")
MIB = 1 << 20
A_MIB, F_MIB, B_MIB = 6, 20, 18


def bucket_table(offset):
    distance = np.abs(offset)
    passed = sum((distance >= mark).astype(np.int32) for mark in far_marks)
    far_ids = np.minimum(8 + passed, 15)
    return np.where(distance < 8, distance, far_ids) + 16 * (offset > 0).astype(np.int32)


def dot_nn(a, b):
    return lax.dot_general(a, b, (((1,), (0,)), ((), ())), preferred_element_type=f32)


def dot_nt(a, b):
    return lax.dot_general(a, b, (((1,), (1,)), ((), ())), preferred_element_type=f32)


def dot_tn(a, b):
    return lax.dot_general(a, b, (((0,), (0,)), ((), ())), preferred_element_type=f32)


def split_two(values):
    high = values.astype(bf16)
    return high, (values - high.astype(f32)).astype(bf16)


def inv_rms(values):
    return lax.rsqrt(jnp.mean(values * values, axis=-1, keepdims=True) + norm_eps)


def segment_of(place, first, second):
    seg = (place >= first).astype(i32) + (place >= second).astype(i32)
    start = jnp.where(seg == 0, 0, jnp.where(seg == 1, first, second))
    return seg, place - start


def vmem_spec():
    return pl.BlockSpec(memory_space=pltpu.VMEM)


def smem_spec():
    return pl.BlockSpec(memory_space=pltpu.SMEM)


def any_spec():
    return pl.BlockSpec(memory_space=pl.ANY)


def out(shape, dtype):
    return jax.ShapeDtypeStruct(shape, dtype)


def held(shape, dtype):
    return pltpu.VMEM(shape, dtype)


def in_vmem(value):
    return pltpu.with_memory_space_constraint(value, pltpu.VMEM)


def in_hbm(value):
    return pltpu.with_memory_space_constraint(value, pltpu.HBM)


def params(mib):
    return pltpu.CompilerParams(vmem_limit_bytes=mib * MIB)


def cost(flops, nbytes, trans=0):
    return pl.CostEstimate(flops=int(flops), bytes_accessed=int(nbytes), transcendentals=int(trans))


def pick_piece(pieces, turn, j):
    count = len(pieces)
    place = lax.rem(turn - j - 1 + count, count)
    picked = pieces[0][...]
    for k in range(1, count):
        picked = jnp.where(place == k, pieces[k][...], picked)
    return picked


def slot_of(index, count):
    return lax.rem(index + 2 * count, count)


def pack_kernel(count, tokens_ref, seg_hbm, prompt_hbm, *refs):
    pieces, (block_ref, seg_ref, prompt_ref, wide_ref, sems) = refs[:count], refs[count:]
    ctx = lax.axis_index("ctx")
    copies = [
        pltpu.make_async_copy(tokens_ref.at[slot_of(ctx + k + 1, count)], pieces[k], sems.at[k]) for k in range(count)
    ]
    small = [
        pltpu.make_async_copy(seg_hbm, seg_ref, sems.at[count]),
        pltpu.make_async_copy(prompt_hbm, prompt_ref, sems.at[count + 1]),
    ]
    for copy in small + copies:
        copy.start()
    for copy in small:
        copy.wait()
    rows = prompt_ref.shape[0]
    wide_ref[...] = jnp.zeros_like(wide_ref)
    wide_ref[0:rows, :] = prompt_ref[...]
    for n in range(2):
        tally = jnp.sum((seg_ref[...] <= n).astype(f32), axis=1, keepdims=True)
        wide_ref[rows + n * count : rows + (n + 1) * count, :] = jnp.broadcast_to(tally, (count, prompt_ref.shape[1]))
    block_ref[...] = wide_ref[...].astype(bf16)
    for copy in copies:
        copy.wait()


def prepare_kernel(count, base_ref, gain_first_ref, gain_second_ref, cot_ref, *refs):
    weights, (tile_ref, table_ref, first_ref, second_ref) = refs[:3], refs[3:7]
    pieces, kept, sems = refs[7 : 7 + count], refs[7 + count : 10 + count], refs[10 + count]
    first_ref[...] = gain_first_ref[...]
    second_ref[...] = gain_second_ref[...]
    ctx = lax.axis_index("ctx")
    copies = [pltpu.make_async_copy(weights[n], kept[n], sems.at[n]) for n in range(3)] + [
        pltpu.make_async_copy(cot_ref.at[slot_of(ctx + k + 1, count)], pieces[k], sems.at[3 + k]) for k in range(count)
    ]
    for copy in copies:
        copy.start()
    heads = tile_ref.shape[0]
    for h in range(heads):
        row = jnp.broadcast_to(base_ref[h : h + 1, :], (BLK, 4 * BLK))
        spread = pltpu.roll(row, 0, 1, stride=1, stride_axis=0)
        low, mid, top = (spread[:, k * BLK : (k + 1) * BLK] for k in (3, 2, 1))
        tile_ref[h, 0] = low
        tile_ref[h, 1] = mid
        tile_ref[h, 2] = top
        rows = slice(h * BLK, (h + 1) * BLK)
        parts = [part for pair in zip(split_two(mid), split_two(low)) for part in pair]
        for k in range(4):
            table_ref[rows, k * BLK : (k + 1) * BLK] = parts[k]
    for copy in copies:
        copy.wait()


def plane_kernel(rows_own, *refs):
    parts, (out_ref, wide_ref) = refs[:-2], refs[-2:]
    core, chip = lax.rem(lax.axis_index("dp"), 2), lax.div(lax.axis_index("dp"), 2)
    high = rows_own + 8
    parts = [part[...].astype(f32) for part in parts]
    parts = [[jnp.where(core == c, part[:high], part[high:]) for c in range(2)] for part in parts]
    for place in range(len(parts)):
        for c in range(2):
            picked = parts[0][c]
            for n in range(1, len(parts)):
                picked = jnp.where((chip ^ n) == place, parts[n][c], picked)
            start = (2 * place + c) * rows_own
            wide_ref[start : start + rows_own, :] = picked[:rows_own]
    for c in range(2):
        wide_ref[SHOWN + 8 * c : SHOWN + 8 * (c + 1), :] = parts[0][c][rows_own:]
    out_ref[...] = wide_ref[0 : SHOWN + 16, :].astype(bf16)


def places(count):
    return lax.rem(lax.axis_index("dp"), 2), lax.rem(lax.axis_index("ctx"), count)


def first_kernel(count, piece, *refs):
    own, (gain_ref, norm_ref) = refs[:count], refs[count:]
    turn = places(count)[1]
    for j in range(count):
        tok = pick_piece(own, turn, j).astype(f32)
        norm_ref[j * piece : (j + 1) * piece, :] = (tok * inv_rms(tok) * gain_ref[...]).astype(bf16)


def forward_kernel(count, piece, rows_own, *refs):
    own, partner = refs[:count], refs[count : 2 * count]
    (
        normed_ref, gain_first_ref, gain_second_ref, wq_ref, wk_ref, wv_ref, tile_ref, table_ref,
    ) = refs[2 * count : 2 * count + 8]
    refs = refs[2 * count + 8 :]
    cols_of, later, refs = refs[: 2 * count], refs[2 * count : 2 * count + 3], refs[2 * count + 3 :]
    e_ref, marks_ref, prompt_ref, q_ref, kall_ref, vall_ref, mixed_ref, inv_ref, after_ref, act_ref = refs[:10]
    kept, refs = refs[10:13], refs[13:]
    wo_ref, wi_ref, wout_ref = kept
    going, refs = refs[:count], refs[count:]
    norm_ref, hid_ref, slot_bias_ref, score_ref, aug_ref, shown_ref, e_buf, sems, weight_sems = refs
    fetches = [pltpu.make_async_copy(later[n], kept[n], weight_sems.at[n]) for n in range(3)]
    for fetch in fetches:
        fetch.start()
    ctx = lax.axis_index("ctx")
    few = cols_of[0].shape[1]
    for place in range(2 * count):
        picked = cols_of[0][0:SHOWN]
        for n in range(1, 2 * count):
            picked = jnp.where((ctx ^ n) == place, cols_of[n][0:SHOWN], picked)
        shown_ref[0:SHOWN, place * few : (place + 1) * few] = picked.astype(f32)
    shown_ref[SHOWN:, :] = jnp.zeros((BLK - SHOWN, shown_ref.shape[1]), f32)
    prompt_ref[...] = shown_ref[...].astype(bf16)
    half, turn = places(count)
    half_len = count * piece
    width = q_ref.shape[1]
    tally = functools.reduce(jnp.add, [cols[SHOWN:].astype(f32) for cols in cols_of])
    tally_row = lax.broadcasted_iota(i32, (tally.shape[0], 1), 0)
    marks = []
    for n in range(2):
        here = tally_row == 8 * lax.div(ctx, count) + n * count + turn
        total = jnp.sum(jnp.where(here, tally, 0.0), axis=0, keepdims=True)[:, 0:1]
        marks.append((total + 0.5).astype(i32))
        marks_ref[n : n + 1, :] = jnp.broadcast_to(marks[n], (1, BLK))
    first, second = marks
    gain = gain_first_ref[...]
    slots = lax.broadcasted_iota(i32, (1, BLK), 1)
    for j in range(count):
        rows = slice(j * piece, (j + 1) * piece)
        place = half * half_len + j * piece + lax.broadcasted_iota(i32, (piece, 1), 0)
        inside = segment_of(place, first, second)[1]
        shown = inside < PROMPT
        choose = jnp.where((inside == slots) & shown, 1.0, 0.0).astype(bf16)
        picked = dot_nn(choose, prompt_ref[...])
        hidden = jnp.where(shown, picked, pick_piece(own, turn, j).astype(f32))
        hid_ref[rows, :] = hidden.astype(bf16)
        norm_ref[half_len + BLK + j * piece : half_len + BLK + (j + 1) * piece, :] = (
            hidden * inv_rms(hidden) * gain
        ).astype(bf16)
        tok = pick_piece(partner, turn, j).astype(f32)
        norm_ref[rows, :] = (tok * inv_rms(tok) * gain).astype(bf16)
    hidden = prompt_ref[...].astype(f32)
    norm_ref[half_len : half_len + BLK, :] = (hidden * inv_rms(hidden) * gain).astype(bf16)
    wide = 2 * BLK

    @pl.loop(0, width // wide)
    def _(t):
        cols = pl.ds(pl.multiple_of(t * wide, wide), wide)
        normed = jnp.concatenate([normed_ref[...], norm_ref[0 : half_len + BLK, :]], axis=0)
        kall_ref[:, cols] = dot_nn(normed, wk_ref[:, cols]).astype(bf16)
        vall_ref[:, cols] = dot_nn(normed, wv_ref[:, cols]).astype(bf16)
        q_ref[:, cols] = dot_nn(norm_ref[half_len + BLK :, :], wq_ref[:, cols]).astype(bf16)

    lane = lax.broadcasted_iota(i32, (1, PAIR), 1)
    low_lane = lane < HEAD
    lane_seg = lane
    spot = lax.broadcasted_iota(i32, (half_len, 1), 0)
    own_seg, own_inside = segment_of(half * half_len + spot, first, second)
    par_seg, par_inside = segment_of((1 - half) * half_len + spot, first, second)
    q_aug = jnp.where(own_seg == lane_seg, 1.0, 0.0).astype(bf16)

    def key_aug(seg, inside):
        closed = ((seg != lane_seg) | (inside < PROMPT)) & (lane_seg < 3)
        return jnp.where(closed, MASKED, 0.0).astype(bf16)

    slot = lax.broadcasted_iota(i32, (BLK, 1), 0)
    aug_ref[0:half_len] = key_aug(own_seg, own_inside)
    aug_ref[half_len : 2 * half_len] = key_aug(par_seg, par_inside)
    aug_ref[2 * half_len :] = jnp.where((slot >= PROMPT) & (lane_seg < 3), MASKED, 0.0).astype(bf16)
    across = segment_of(half * half_len + lax.broadcasted_iota(i32, (1, half_len), 1), first, second)[1]
    far = lax.rem(lax.broadcasted_iota(i32, (4 * BLK, 1), 0), 2 * BLK)
    spread = jnp.where(jnp.minimum(across, 2 * BLK - 1) == far, 1.0, 0.0).astype(bf16)
    slot_bias_ref[...] = dot_nn(table_ref[...], spread)
    blocks = half_len // BLK
    ones = jnp.ones((16, 2 * half_len + BLK), bf16)

    def e_copy(hp):
        at = lax.rem(hp, 2)
        return pltpu.make_async_copy(e_buf.at[at], e_ref.at[hp], sems.at[at])

    keys_all = 2 * half_len + BLK
    tiles_q = half_len // QCOLS
    chunk = keys_all // 3
    units = [(s, qt) for s in range(2) for qt in range(tiles_q)]

    def kept(s):
        return low_lane if s == 0 else jnp.logical_not(low_lane)

    def score_steps(hp, s, qt, slot):
        cols = pl.ds(pl.multiple_of(hp * PAIR, PAIR), PAIR)
        here = slice(qt * QCOLS, (qt + 1) * QCOLS)
        q_e = jnp.concatenate([jnp.where(kept(s), q_ref[here, cols], jnp.zeros((), bf16)), q_aug[here]], axis=1)

        def step(n):
            rows = slice(n * chunk, (n + 1) * chunk)
            score_ref[slot, rows, :] = dot_nt(jnp.concatenate([kall_ref[rows, cols], aug_ref[rows]], axis=1), q_e)

        return [functools.partial(step, n) for n in range(3)]

    for step in score_steps(0, 0, 0, 0):
        step()

    @pl.loop(0, width // PAIR)
    def _(hp):
        @pl.when(hp >= 2)
        def _():
            e_copy(hp - 2).wait()

        cols = pl.ds(pl.multiple_of(hp * PAIR, PAIR), PAIR)
        v_turned = vall_ref[:, cols].T
        for u, (s, qt) in enumerate(units):
            h = 2 * hp + s
            coming = units[(u + 1) % len(units)]
            at = hp if u + 1 < len(units) else jnp.minimum(hp + 1, width // PAIR - 1)
            steps = score_steps(at, *coming, (u + 1) % 2)
            back_far, ahead_far = tile_ref[h, 0, 0:1, BLK - 1 :], tile_ref[h, 2, BLK - 1 :, 0:1]
            other_far = jnp.where(half == 0, ahead_far, back_far)
            values = (back_far, ahead_far, other_far)
            columns = []
            for sub in range(QCOLS // BLK):
                qb = qt * (QCOLS // BLK) + sub
                here = slice(sub * BLK, (sub + 1) * BLK)

                def part_of(kb):
                    part = score_ref[u % 2, kb * BLK : (kb + 1) * BLK, here]
                    if kb == 2 * blocks:
                        slot_rows = pl.ds(pl.multiple_of(h * BLK, BLK), BLK)
                        return part + slot_bias_ref[slot_rows, qb * BLK : (qb + 1) * BLK], None
                    gap = kb - qb
                    if kb < blocks and abs(gap) <= 1:
                        return part + tile_ref[h, gap + 1], None
                    if kb < blocks:
                        return part, 0 if gap < 0 else 1
                    if qb == blocks - 1 and kb == blocks:
                        return part + jnp.where(half == 0, tile_ref[h, 2], back_far), None
                    if qb == 0 and kb == 2 * blocks - 1:
                        return part + jnp.where(half == 0, ahead_far, tile_ref[h, 0]), None
                    return part, 2

                tops, group = {}, {}
                for kb in range(2 * blocks + 1):
                    part, const = part_of(kb)
                    if const is None:
                        score_ref[u % 2, kb * BLK : (kb + 1) * BLK, here] = part
                    group[kb] = const
                    top = jnp.max(part.reshape(BLK // 8, 8, BLK), axis=0)
                    tops[const] = top if const not in tops else jnp.maximum(tops[const], top)
                    if steps and kb == 4:
                        steps.pop(0)()
                peak = functools.reduce(
                    jnp.maximum, [top if const is None else top + values[const] for const, top in tops.items()]
                )
                peak = jnp.max(peak, axis=0, keepdims=True)
                shifts = [peak - value for value in values]
                column = []
                for kb in range(2 * blocks + 1):
                    part = score_ref[u % 2, kb * BLK : (kb + 1) * BLK, here]
                    shift = peak if group[kb] is None else shifts[group[kb]]
                    column.append(jnp.exp(part - shift).astype(bf16))
                    if steps and kb == 4:
                        steps.pop(0)()
                columns.append(jnp.concatenate(column, axis=0))
            for step in steps:
                step()
            raised = jnp.concatenate(columns, axis=1)
            qcols = slice(qt * QCOLS, (qt + 1) * QCOLS)
            e_buf[lax.rem(hp, 2), s, :, qcols] = raised
            total = dot_nn(jnp.concatenate([v_turned[s * HEAD : (s + 1) * HEAD], ones], axis=0), raised)
            inv = 1.0 / total[HEAD : HEAD + 1]
            inv_ref[pl.ds(h, 1), qcols] = inv
            mixed_ref[pl.ds(pl.multiple_of(h * HEAD, HEAD), HEAD), qcols] = (total[:HEAD] * inv).astype(bf16)
        e_copy(hp).start()

    for fetch in fetches:
        fetch.wait()
    after_ref[...] = dot_tn(mixed_ref[...], wo_ref[...])

    @pl.loop(0, half_len // BLK)
    def _(t):
        rows = pl.ds(pl.multiple_of(t * BLK, BLK), BLK)
        after = hid_ref[rows, :].astype(f32) + after_ref[rows, :]
        after_ref[rows, :] = after
        norm_ref[rows, :] = (after * inv_rms(after) * gain_second_ref[...]).astype(bf16)

    @pl.loop(0, wi_ref.shape[1] // wide)
    def _(t):
        cols = pl.ds(pl.multiple_of(t * wide, wide), wide)
        act_ref[:, cols] = jnp.maximum(dot_nn(norm_ref[0:half_len, :], wi_ref[:, cols]), 0.0).astype(bf16)

    @pl.loop(0, width // wide)
    def _(t):
        cols = pl.ds(pl.multiple_of(t * wide, wide), wide)
        made = (after_ref[:, cols] + dot_nn(act_ref[...], wout_ref[:, cols])).astype(bf16)
        made = [made[j * piece : (j + 1) * piece] for j in range(count)]
        for k in range(count):
            place = slot_of(turn - k - 1, count)
            sent = made[0]
            for j in range(1, count):
                sent = jnp.where(place == j, made[j], sent)
            going[k][:, cols] = sent

    for hp in range(width // PAIR - 2, width // PAIR):
        e_copy(hp).wait()


def backward_kernel(count, piece, rows_own, *refs):
    cots = refs[:count]
    (
        marks_ref, act_ref, after_ref, mixed_ref, inv_ref, q_ref, kall_ref, vall_ref, prompt_ref, gain_first_ref, gain_second_ref,
        wout_ref, wi_ref, wo_ref, wq_ref, wk_ref, wv_ref, e_ref,
        kept_ref, sent_ref,
        cot_ref, acc_ref, low_ref, do_ref, dq_ref, gk_ref, gv_ref, cast_ref, e_buf, sems,
    ) = refs[count:]
    half, turn = places(count)
    first, second = marks_ref[0:1, 0:1], marks_ref[1:2, 0:1]
    half_len = count * piece
    width = q_ref.shape[1]
    pairs = width // PAIR

    def e_copy(hp):
        at = lax.rem(hp, 2)
        return pltpu.make_async_copy(e_ref.at[hp], e_buf.at[at], sems.at[at])

    for hp in range(2):
        e_copy(hp).start()
    for j in range(count):
        cot_ref[j * piece : (j + 1) * piece, :] = pick_piece(cots, turn, j)
    wide = 4 * BLK
    acc_ref[...] = jnp.zeros_like(acc_ref)

    @pl.loop(0, wi_ref.shape[1] // wide)
    def _(t):
        cols = pl.ds(pl.multiple_of(t * wide, wide), wide)
        grad_act = dot_nt(cot_ref[...], wout_ref[cols, :])
        grad_inner = jnp.where(act_ref[:, cols] > 0, grad_act, 0.0).astype(bf16)
        acc_ref[...] += dot_nt(grad_inner, wi_ref[:, cols])

    gain = gain_second_ref[...]

    @pl.loop(0, half_len // BLK)
    def _(t):
        rows = pl.ds(pl.multiple_of(t * BLK, BLK), BLK)
        after = after_ref[rows, :]
        scale = inv_rms(after)
        pulled = gain * acc_ref[rows, :]
        along = jnp.mean(after * pulled, axis=-1, keepdims=True)
        grad_after = cot_ref[rows, :].astype(f32) + scale * pulled - after * (scale * scale * scale * along)
        acc_ref[rows, :] = grad_after
        low_ref[rows, :] = grad_after.astype(bf16)

    do_ref[...] = dot_nt(wo_ref[...], low_ref[...])

    low_lane = lax.broadcasted_iota(i32, (1, PAIR), 1) < HEAD
    row = lax.broadcasted_iota(i32, (PAIR, 1), 0)
    ones = jnp.ones((2 * half_len + BLK, PAIR), bf16)

    @pl.loop(0, pairs)
    def _(hp):
        e_copy(hp).wait()
        cols = pl.ds(pl.multiple_of(hp * PAIR, PAIR), PAIR)
        q_pair, k_turned, v_pair = q_ref[:, cols], kall_ref[:, cols].T, vall_ref[:, cols]
        inv_both = jnp.where(row < HEAD, inv_ref[pl.ds(2 * hp, 1), :], inv_ref[pl.ds(2 * hp + 1, 1), :])
        do_pair = (do_ref[cols, :] * inv_both).astype(bf16)
        inner = do_pair.astype(f32) * mixed_ref[cols, :].astype(f32)
        slot_scores, slot_raised = [], []
        for s in range(2):
            mine = (row < HEAD) == (s == 0)
            high, low = split_two(-jnp.sum(inner[s * HEAD : (s + 1) * HEAD], axis=0, keepdims=True))
            zero = jnp.zeros((), bf16)
            shift = jnp.where(row == 0, high, jnp.where(row == 1, low, zero))
            do_e = jnp.concatenate([jnp.where(mine, do_pair, zero), shift], axis=0)
            raised = e_buf[lax.rem(hp, 2), s]
            grad_probs = dot_nn(jnp.concatenate([v_pair, ones], axis=1), do_e)
            grad_scores = (raised.astype(f32) * grad_probs).astype(bf16)
            made = dot_nn(k_turned[s * HEAD : (s + 1) * HEAD], grad_scores)
            dq_ref[pl.ds(pl.multiple_of(hp * PAIR + s * HEAD, HEAD), HEAD), :] = made.astype(bf16)
            slot_scores.append(grad_scores[2 * half_len :])
            slot_raised.append(raised[2 * half_len :])
        dk = dot_nn(jnp.concatenate(slot_scores, axis=0), q_pair)
        dv = dot_nt(jnp.concatenate(slot_raised, axis=0), do_pair)
        gk_ref[:, cols] = jnp.where(low_lane, dk[:BLK], dk[BLK:]).astype(bf16)
        gv_ref[:, cols] = jnp.where(low_lane, dv[:BLK], dv[BLK:]).astype(bf16)

        @pl.when(hp + 2 < pairs)
        def _():
            e_copy(hp + 2).start()

    spot = lax.broadcasted_iota(i32, (1, half_len), 1)
    inside = segment_of(half * half_len + spot, first, second)[1]
    slots = lax.broadcasted_iota(i32, (BLK, 1), 0)
    choose = jnp.where((inside == slots) & (inside < PROMPT), 1.0, 0.0).astype(bf16)
    gq = dot_nt(choose, dq_ref[...]).astype(bf16)
    pulled = dot_nt(gq, wq_ref[...]) + dot_nt(gk_ref[...], wk_ref[...]) + dot_nt(gv_ref[...], wv_ref[...])
    high, low = split_two(acc_ref[...])
    direct = dot_nn(choose, high) + dot_nn(choose, low)
    hidden = prompt_ref[...].astype(f32)
    scale = inv_rms(hidden)
    pulled = gain_first_ref[...] * pulled
    along = jnp.mean(hidden * pulled, axis=-1, keepdims=True)
    grad = direct + scale * pulled - hidden * (scale * scale * scale * along)
    for place in range(BLK // (2 * rows_own)):
        rows = slice(place * rows_own, (place + 1) * rows_own)
        low, high = (grad[(2 * place + c) * rows_own : (2 * place + c + 1) * rows_own] for c in range(2))
        kept_ref[rows, :] = jnp.where(half == 0, low, high)
        cast_ref[rows, :] = jnp.where(half == 0, high, low)
    sent_ref[...] = cast_ref[...].astype(bf16)


def share_kernel(rows_own, kept_ref, came_ref, mine_ref, *refs):
    parts, (total_ref,) = refs[:-1], refs[-1:]
    chip = lax.div(lax.axis_index("dp"), 2)
    total = kept_ref[...] + came_ref[...].astype(f32)
    for place in range(len(parts) + 1):
        total_ref[place] = total[place * rows_own : (place + 1) * rows_own]
    mine_ref[...] = total_ref[chip]
    for n in range(1, len(parts) + 1):
        parts[n - 1][...] = total_ref[chip ^ n].astype(bf16)


def square_kernel(total_ref, *refs):
    parts, (own_ref, square_ref) = refs[:-2], refs[-2:]
    total = total_ref[...]
    for part in parts:
        total = total + part[...].astype(f32)
    few = own_ref.shape[1]
    own = total[:, 0:few]
    for place in range(1, len(parts) + 1):
        own = jnp.where(lax.axis_index("ctx") == place, total[:, place * few : (place + 1) * few], own)
    own_ref[...] = own
    square = jnp.sum(jnp.sum(total * total, axis=1, keepdims=True), axis=0, keepdims=True)
    square_ref[...] = jnp.broadcast_to(square, square_ref.shape)


def update_kernel(max_norm, grad_ref, prompt_ref, first_ref, second_ref, *refs):
    squares, (prompt_out, first_out, second_out) = refs[:-3], refs[-3:]
    square = functools.reduce(jnp.add, [square[0:1, 0:1] for square in squares])
    clipped = grad_ref[...] * (max_norm / jnp.maximum(jnp.sqrt(square), max_norm))
    first_new = beta_first * first_ref[...] + (1.0 - beta_first) * clipped
    second_new = beta_second * second_ref[...] + (1.0 - beta_second) * clipped * clipped
    step = learn_rate * (first_new / first_fix) / (jnp.sqrt(second_new / second_fix) + adam_eps)
    prompt_out[...] = prompt_ref[...] - step
    first_out[...] = first_new
    second_out[...] = second_new


def on_device(
    sizes, tokens, segment_ids, prompt_slots, cotangent, w_query, w_key, w_value, w_output, w_inner, w_outer,
    gain_first, gain_second, bias_table, prompt, first_moment, second_moment,
):
    n_dp, n_ctx = sizes
    count, piece, width = tokens.shape
    half_len = count * piece
    heads = bias_table.shape[1]
    dp, ctx = lax.axis_index("dp"), lax.axis_index("ctx")
    core = lax.rem(dp, 2)

    def permute(value, target):
        pairs = []
        for d in range(n_dp):
            for z in range(n_ctx):
                d2, z2 = target(d, z)
                pairs.append((d * n_ctx + z, d2 * n_ctx + z2))
        return lax.ppermute(value, AXES, pairs)

    def swap_dp(value, bit):
        return permute(value, lambda d, z: (d ^ bit, z))

    def swap_ctx(value, bit):
        return permute(value, lambda d, z: (d, z ^ bit))

    def there(k):
        return lambda d, z: (2 * (d // 2) + z // count, (d % 2) * count + (z + k + 1) % count)

    rows_own, cols_own = prompt.shape
    piece_like = held((piece, width), bf16)
    packed = pl.pallas_call(
        functools.partial(pack_kernel, count),
        out_shape=[piece_like] * count + [held((rows_own + 8, cols_own), bf16)],
        in_specs=[any_spec()] * 3,
        out_specs=[vmem_spec()] * (count + 1),
        scratch_shapes=[
            pltpu.VMEM(segment_ids.shape, i32),
            pltpu.VMEM(prompt.shape, f32),
            pltpu.VMEM((rows_own + 8, cols_own), f32),
            pltpu.SemaphoreType.DMA((count + 2,)),
        ],
        compiler_params=params(4),
        cost_estimate=cost(1e5, 2e6),
    )(in_hbm(tokens), in_hbm(segment_ids), in_hbm(prompt))

    own = [permute(packed[k], there(k)) for k in range(count)]
    chip_rows = jnp.concatenate([packed[count], swap_dp(packed[count], 1)], axis=0)
    chip_parts = [chip_rows] + [swap_dp(chip_rows, 2 * n) for n in range(1, n_dp // 2)]
    plane = pl.pallas_call(
        functools.partial(plane_kernel, rows_own),
        out_shape=held((SHOWN + 16, cols_own), bf16),
        in_specs=[vmem_spec()] * len(chip_parts),
        out_specs=vmem_spec(),
        scratch_shapes=[pltpu.VMEM((BLK + 16, cols_own), f32)],
        compiler_params=params(4),
        cost_estimate=cost(1e5, 1e5),
    )(*chip_parts)

    choose = (np.arange(bias_table.shape[0])[:, None] == bucket_table(2 * BLK - np.arange(4 * BLK))[None]).astype(np.float32)
    base = lax.dot_general(
        bias_table, jnp.asarray(choose), (((0,), (0,)), ((), ())), precision=lax.Precision.HIGHEST
    )
    base, plane = lax.optimization_barrier((base, plane))
    cols_of = [plane] + [swap_ctx(plane, n) for n in range(1, n_ctx)]
    weights = (w_query, w_key, w_value)
    prepared = pl.pallas_call(
        functools.partial(prepare_kernel, count),
        out_shape=[held((heads, 3, BLK, BLK), f32), held((heads * BLK, 4 * BLK), bf16)]
        + [held((1, width), f32)] * 2
        + [piece_like] * count
        + [held(w.shape, bf16) for w in weights],
        in_specs=[vmem_spec()] * 3 + [any_spec()] * 4,
        out_specs=[vmem_spec()] * (7 + count),
        scratch_shapes=[pltpu.SemaphoreType.DMA((3 + count,))],
        compiler_params=params(4),
        cost_estimate=cost(1e6, 5e6),
    )(base, gain_first[None], gain_second[None], in_hbm(cotangent), *[in_hbm(w) for w in weights])
    tiles, table, gain_1, gain_2 = prepared[:4]
    cot_pieces = prepared[4 : 4 + count]
    w_q, w_k, w_v = prepared[4 + count :]

    keys_all = 2 * half_len + BLK
    hidden_ff = w_inner.shape[1]
    partner = [swap_dp(piece_rows, 1) for piece_rows in own]
    normed = pl.pallas_call(
        functools.partial(first_kernel, count, piece),
        out_shape=held((half_len, width), bf16),
        in_specs=[vmem_spec()] * (count + 1),
        out_specs=vmem_spec(),
        compiler_params=params(A_MIB),
        cost_estimate=cost(1e10, 8e6),
    )(*own, gain_1)
    cots = [permute(cot_pieces[k], there(k)) for k in range(count)]

    made = pl.pallas_call(
        functools.partial(forward_kernel, count, piece, rows_own),
        out_shape=[
            pltpu.HBM((heads // 2, 2, keys_all, half_len), bf16),
            held((8, BLK), i32),
            held((BLK, width), bf16),
            held((half_len, width), bf16),
            held((keys_all, width), bf16),
            held((keys_all, width), bf16),
            held((width, half_len), bf16),
            held((heads, half_len), f32),
            held((half_len, width), f32),
            held((half_len, hidden_ff), bf16),
        ]
        + [held(w.shape, bf16) for w in (w_output, w_inner, w_outer)]
        + [piece_like] * count,
        in_specs=[vmem_spec()] * (4 * count + 8) + [any_spec()] * 3,
        out_specs=[any_spec()] + [vmem_spec()] * (12 + count),
        scratch_shapes=[
            pltpu.VMEM((2 * half_len + BLK, width), bf16),
            pltpu.VMEM((half_len, width), bf16),
            pltpu.VMEM((heads * BLK, half_len), f32),
            pltpu.VMEM((2, keys_all, QCOLS), f32),
            pltpu.VMEM((keys_all, PAIR), bf16),
            pltpu.VMEM((BLK, width), f32),
            pltpu.VMEM((2, 2, keys_all, half_len), bf16),
            pltpu.SemaphoreType.DMA((2,)),
            pltpu.SemaphoreType.DMA((3,)),
        ],
        compiler_params=params(F_MIB),
        cost_estimate=cost(3e10, 4e7, heads * half_len * keys_all),
    )(
        *own, *partner, normed, gain_1, gain_2, w_q, w_k, w_v, tiles, table, *cols_of,
        *[in_hbm(w) for w in (w_output, w_inner, w_outer)],
    )
    got = [permute(made[13 + k], back_of(count, k)) for k in range(count)]
    w_o, w_i, w_out = made[10:13]
    e, marks, sent, q, kall, vall, mixed, inv, after, act = made[:10]

    half_rows = n_dp // 2 * rows_own
    kept, leaving = pl.pallas_call(
        functools.partial(backward_kernel, count, piece, rows_own),
        out_shape=[held((half_rows, width), f32), held((half_rows, width), bf16)],
        in_specs=[vmem_spec()] * (count + 17) + [any_spec()],
        out_specs=[vmem_spec()] * 2,
        scratch_shapes=[
            pltpu.VMEM((half_len, width), bf16),
            pltpu.VMEM((half_len, width), f32),
            pltpu.VMEM((half_len, width), bf16),
            pltpu.VMEM((width, half_len), f32),
            pltpu.VMEM((width, half_len), bf16),
            pltpu.VMEM((BLK, width), bf16),
            pltpu.VMEM((BLK, width), bf16),
            pltpu.VMEM((half_rows, width), f32),
            pltpu.VMEM((2, 2, keys_all, half_len), bf16),
            pltpu.SemaphoreType.DMA((2,)),
        ],
        compiler_params=params(B_MIB),
        cost_estimate=cost(3e10, 4e7),
    )(
        *cots, marks, act, after, mixed, inv, q, kall, vall, sent, gain_1, gain_2, w_out, w_i, w_o, w_q, w_k, w_v, in_hbm(e),
    )

    got, leaving = lax.optimization_barrier((got, leaving))
    order = [lax.rem(ctx + j + 1, count) for j in range(count)]
    output = jnp.stack(
        [functools.reduce(lambda a, k: jnp.where(order[k] == r, got[k], a), range(1, count), got[0]) for r in range(count)]
    )

    chips = n_dp // 2
    own_like = held((rows_own, width), f32)
    mine, *parts = pl.pallas_call(
        functools.partial(share_kernel, rows_own),
        out_shape=[own_like] + [held((rows_own, width), bf16)] * (chips - 1),
        in_specs=[vmem_spec()] * 2,
        out_specs=[vmem_spec()] * chips,
        scratch_shapes=[pltpu.VMEM((chips, rows_own, width), f32)],
        compiler_params=params(4),
        cost_estimate=cost(1e5, 1e5),
    )(kept, swap_dp(leaving, 1))
    for n in range(1, chips):
        mine = mine + swap_dp(parts[n - 1], 2 * n).astype(f32)
    line = mine.astype(bf16)
    line_parts = [swap_ctx(line, n) for n in range(1, n_ctx)]
    line_parts, output = lax.optimization_barrier((line_parts, output))
    grad_own, square = pl.pallas_call(
        square_kernel,
        out_shape=[held((rows_own, cols_own), f32), held((8, BLK), f32)],
        in_specs=[vmem_spec()] * n_ctx,
        out_specs=[vmem_spec()] * 2,
        compiler_params=params(4),
        cost_estimate=cost(1e5, 1e5),
    )(mine, *line_parts)
    square = square + swap_dp(square, 1)
    squares = [square] + [swap_dp(square, 2 * n) for n in range(1, chips)]
    own_out = out((rows_own, cols_own), f32)
    prompt_new, first_new, second_new = pl.pallas_call(
        functools.partial(update_kernel, float(0.5 * np.sqrt(np.float32(PROMPT * width)))),
        out_shape=[own_out] * 3,
        in_specs=[vmem_spec()] * (4 + chips),
        out_specs=[vmem_spec()] * 3,
        compiler_params=params(4),
        cost_estimate=cost(1e5, 1e5),
    )(grad_own, prompt, first_moment, second_moment, *squares)
    return (output, prompt_new, first_new, second_new)


def back_of(count, k):
    def target(d, z):
        half, c, r = d % 2, z // count, z % count
        return (2 * (d // 2) + c, half * count + (r - k - 1) % count)

    return target


def solution(mesh):
    rows, cols = P("dp", "ctx", None), P("dp", "ctx")
    placed = (rows, cols, cols, rows) + (P(),) * 9 + (cols,) * 3
    return jax.shard_map(
        functools.partial(on_device, (mesh.shape["dp"], mesh.shape["ctx"])),
        mesh=mesh,
        in_specs=placed,
        out_specs=(rows, cols, cols, cols),
        check_vma=False,
    )
```

```python
import functools

import jax
import jax.numpy as jnp
import numpy as np
from jax import lax
from jax.experimental import pallas as pl
from jax.experimental.pallas import tpu as pltpu
from jax.sharding import PartitionSpec as P

PROMPT = 100
HEAD = 64
PAIR = 2 * HEAD
BLK = 128
SHOWN = 112
HELD = (SHOWN + 16) // 2
QCOLS = 256
norm_eps = 1e-06
beta_first = 0.9
beta_second = 0.999
adam_eps = 1e-08
learn_rate = 0.1
first_fix = 1.0 - 0.9**8
second_fix = 1.0 - 0.999**8
far_marks = (12, 16, 23, 32, 46, 64, 91)
f32 = jnp.float32
bf16 = jnp.bfloat16
i32 = jnp.int32
MASKED = -float(2**30)
AXES = ("dp", "ctx")
MIB = 1 << 20
A_MIB, F_MIB, B_MIB = 6, 20, 18


def bucket_table(offset):
    distance = np.abs(offset)
    passed = sum((distance >= mark).astype(np.int32) for mark in far_marks)
    far_ids = np.minimum(8 + passed, 15)
    return np.where(distance < 8, distance, far_ids) + 16 * (offset > 0).astype(np.int32)


def dot_nn(a, b):
    return lax.dot_general(a, b, (((1,), (0,)), ((), ())), preferred_element_type=f32)


def dot_nt(a, b):
    return lax.dot_general(a, b, (((1,), (1,)), ((), ())), preferred_element_type=f32)


def dot_tn(a, b):
    return lax.dot_general(a, b, (((0,), (0,)), ((), ())), preferred_element_type=f32)


def split_two(values):
    high = values.astype(bf16)
    return high, (values - high.astype(f32)).astype(bf16)


def inv_rms(values):
    return lax.rsqrt(jnp.mean(values * values, axis=-1, keepdims=True) + norm_eps)


def segment_of(place, first, second):
    seg = (place >= first).astype(i32) + (place >= second).astype(i32)
    start = jnp.where(seg == 0, 0, jnp.where(seg == 1, first, second))
    return seg, place - start


def vmem_spec():
    return pl.BlockSpec(memory_space=pltpu.VMEM)


def smem_spec():
    return pl.BlockSpec(memory_space=pltpu.SMEM)


def any_spec():
    return pl.BlockSpec(memory_space=pl.ANY)


def out(shape, dtype):
    return jax.ShapeDtypeStruct(shape, dtype)


def held(shape, dtype):
    return pltpu.VMEM(shape, dtype)


def in_vmem(value):
    return pltpu.with_memory_space_constraint(value, pltpu.VMEM)


def in_hbm(value):
    return pltpu.with_memory_space_constraint(value, pltpu.HBM)


def params(mib):
    return pltpu.CompilerParams(vmem_limit_bytes=mib * MIB)


def cost(flops, nbytes, trans=0):
    return pl.CostEstimate(flops=int(flops), bytes_accessed=int(nbytes), transcendentals=int(trans))


def pick_piece(pieces, turn, j):
    count = len(pieces)
    place = lax.rem(turn - j - 1 + count, count)
    picked = pieces[0][...]
    for k in range(1, count):
        picked = jnp.where(place == k, pieces[k][...], picked)
    return picked


def slot_of(index, count):
    return lax.rem(index + 2 * count, count)


def pack_kernel(count, tokens_ref, seg_hbm, prompt_hbm, *refs):
    pieces, (block_ref, seg_ref, prompt_ref, wide_ref, sems) = refs[:count], refs[count:]
    ctx = lax.axis_index("ctx")
    copies = [
        pltpu.make_async_copy(tokens_ref.at[slot_of(ctx + k + 1, count)], pieces[k], sems.at[k]) for k in range(count)
    ]
    small = [
        pltpu.make_async_copy(seg_hbm, seg_ref, sems.at[count]),
        pltpu.make_async_copy(prompt_hbm, prompt_ref, sems.at[count + 1]),
    ]
    for copy in small + copies:
        copy.start()
    for copy in small:
        copy.wait()
    rows = prompt_ref.shape[0]
    wide_ref[...] = jnp.zeros_like(wide_ref)
    wide_ref[0:rows, :] = prompt_ref[...]
    for n in range(2):
        tally = jnp.sum((seg_ref[...] <= n).astype(f32), axis=1, keepdims=True)
        wide_ref[rows + n * count : rows + (n + 1) * count, :] = jnp.broadcast_to(tally, (count, prompt_ref.shape[1]))
    block_ref[...] = wide_ref[...].astype(bf16)
    for copy in copies:
        copy.wait()


def prepare_kernel(count, base_ref, gain_first_ref, gain_second_ref, cot_ref, *refs):
    weights, (tile_ref, table_ref, first_ref, second_ref) = refs[:3], refs[3:7]
    pieces, kept, sems = refs[7 : 7 + count], refs[7 + count : 10 + count], refs[10 + count]
    first_ref[...] = gain_first_ref[...]
    second_ref[...] = gain_second_ref[...]
    ctx = lax.axis_index("ctx")
    copies = [pltpu.make_async_copy(weights[n], kept[n], sems.at[n]) for n in range(3)] + [
        pltpu.make_async_copy(cot_ref.at[slot_of(ctx + k + 1, count)], pieces[k], sems.at[3 + k]) for k in range(count)
    ]
    for copy in copies:
        copy.start()
    heads = tile_ref.shape[0]
    for h in range(heads):
        row = jnp.broadcast_to(base_ref[h : h + 1, :], (BLK, 4 * BLK))
        spread = pltpu.roll(row, 0, 1, stride=1, stride_axis=0)
        low, mid, top = (spread[:, k * BLK : (k + 1) * BLK] for k in (3, 2, 1))
        tile_ref[h, 0] = low
        tile_ref[h, 1] = mid
        tile_ref[h, 2] = top
        rows = slice(h * BLK, (h + 1) * BLK)
        parts = [part for pair in zip(split_two(mid), split_two(low)) for part in pair]
        for k in range(4):
            table_ref[rows, k * BLK : (k + 1) * BLK] = parts[k]
    for copy in copies:
        copy.wait()


def plane_kernel(rows_own, *refs):
    parts, (out_ref, wide_ref) = refs[:-2], refs[-2:]
    core, chip = lax.rem(lax.axis_index("dp"), 2), lax.div(lax.axis_index("dp"), 2)
    high = rows_own + 8
    parts = [part[...].astype(f32) for part in parts]
    parts = [[jnp.where(core == c, part[:high], part[high:]) for c in range(2)] for part in parts]
    for place in range(len(parts)):
        for c in range(2):
            picked = parts[0][c]
            for n in range(1, len(parts)):
                picked = jnp.where((chip ^ n) == place, parts[n][c], picked)
            start = (2 * place + c) * rows_own
            wide_ref[start : start + rows_own, :] = picked[:rows_own]
    for c in range(2):
        wide_ref[SHOWN + 8 * c : SHOWN + 8 * (c + 1), :] = parts[0][c][rows_own:]
    out_ref[...] = jnp.where(core == 0, wide_ref[0:HELD, :], wide_ref[HELD : 2 * HELD, :]).astype(bf16)


def places(count):
    return lax.rem(lax.axis_index("dp"), 2), lax.rem(lax.axis_index("ctx"), count)


def first_kernel(count, piece, *refs):
    own, (gain_ref, norm_ref) = refs[:count], refs[count:]
    turn = places(count)[1]
    for j in range(count):
        tok = pick_piece(own, turn, j).astype(f32)
        norm_ref[j * piece : (j + 1) * piece, :] = (tok * inv_rms(tok) * gain_ref[...]).astype(bf16)


def forward_kernel(count, piece, rows_own, *refs):
    own, partner = refs[:count], refs[count : 2 * count]
    (
        normed_ref, gain_first_ref, gain_second_ref, wq_ref, wk_ref, wv_ref, tile_ref, table_ref,
    ) = refs[2 * count : 2 * count + 8]
    refs = refs[2 * count + 8 :]
    (mine_ref, other_ref), later, refs = refs[:2], refs[2:5], refs[5:]
    e_ref, marks_ref, prompt_ref, q_ref, kall_ref, vall_ref, mixed_ref, inv_ref, after_ref, act_ref = refs[:10]
    kept, refs = refs[10:13], refs[13:]
    wo_ref, wi_ref, wout_ref = kept
    going, refs = refs[:count], refs[count:]
    norm_ref, hid_ref, slot_bias_ref, score_ref, aug_ref, shown_ref, e_buf, sems, weight_sems = refs
    fetches = [pltpu.make_async_copy(later[n], kept[n], weight_sems.at[n]) for n in range(3)]
    for fetch in fetches:
        fetch.start()
    ctx = lax.axis_index("ctx")
    half, turn = places(count)
    few = mine_ref.shape[1]
    low = jnp.where(half == 0, mine_ref[...], other_ref[...]).astype(f32)
    high = jnp.where(half == 0, other_ref[...], mine_ref[...]).astype(f32)
    for place in range(2 * count):
        for part, start, stop in ((low, 0, HELD), (high, HELD, SHOWN)):
            picked = part[0 : stop - start]
            for n in range(1, 2 * count):
                picked = jnp.where((ctx ^ n) == place, part[n * HELD : n * HELD + stop - start], picked)
            shown_ref[start:stop, place * few : (place + 1) * few] = picked
    shown_ref[SHOWN:, :] = jnp.zeros((BLK - SHOWN, shown_ref.shape[1]), f32)
    prompt_ref[...] = shown_ref[...].astype(bf16)
    half_len = count * piece
    width = q_ref.shape[1]
    tally = functools.reduce(jnp.add, [high[(n + 1) * HELD - 16 : (n + 1) * HELD] for n in range(2 * count)])
    tally_row = lax.broadcasted_iota(i32, (tally.shape[0], 1), 0)
    marks = []
    for n in range(2):
        here = tally_row == 8 * lax.div(ctx, count) + n * count + turn
        total = jnp.sum(jnp.where(here, tally, 0.0), axis=0, keepdims=True)[:, 0:1]
        marks.append((total + 0.5).astype(i32))
        marks_ref[n : n + 1, :] = jnp.broadcast_to(marks[n], (1, BLK))
    first, second = marks
    gain = gain_first_ref[...]
    slots = lax.broadcasted_iota(i32, (1, BLK), 1)
    for j in range(count):
        rows = slice(j * piece, (j + 1) * piece)
        place = half * half_len + j * piece + lax.broadcasted_iota(i32, (piece, 1), 0)
        inside = segment_of(place, first, second)[1]
        shown = inside < PROMPT
        choose = jnp.where((inside == slots) & shown, 1.0, 0.0).astype(bf16)
        picked = dot_nn(choose, prompt_ref[...])
        hidden = jnp.where(shown, picked, pick_piece(own, turn, j).astype(f32))
        hid_ref[rows, :] = hidden.astype(bf16)
        norm_ref[half_len + BLK + j * piece : half_len + BLK + (j + 1) * piece, :] = (
            hidden * inv_rms(hidden) * gain
        ).astype(bf16)
        tok = pick_piece(partner, turn, j).astype(f32)
        norm_ref[rows, :] = (tok * inv_rms(tok) * gain).astype(bf16)
    hidden = prompt_ref[...].astype(f32)
    norm_ref[half_len : half_len + BLK, :] = (hidden * inv_rms(hidden) * gain).astype(bf16)
    wide = 2 * BLK

    @pl.loop(0, width // wide)
    def _(t):
        cols = pl.ds(pl.multiple_of(t * wide, wide), wide)
        normed = jnp.concatenate([normed_ref[...], norm_ref[0 : half_len + BLK, :]], axis=0)
        kall_ref[:, cols] = dot_nn(normed, wk_ref[:, cols]).astype(bf16)
        vall_ref[:, cols] = dot_nn(normed, wv_ref[:, cols]).astype(bf16)
        q_ref[:, cols] = dot_nn(norm_ref[half_len + BLK :, :], wq_ref[:, cols]).astype(bf16)

    lane = lax.broadcasted_iota(i32, (1, PAIR), 1)
    low_lane = lane < HEAD
    lane_seg = lane
    spot = lax.broadcasted_iota(i32, (half_len, 1), 0)
    own_seg, own_inside = segment_of(half * half_len + spot, first, second)
    par_seg, par_inside = segment_of((1 - half) * half_len + spot, first, second)
    q_aug = jnp.where(own_seg == lane_seg, 1.0, 0.0).astype(bf16)

    def key_aug(seg, inside):
        closed = ((seg != lane_seg) | (inside < PROMPT)) & (lane_seg < 3)
        return jnp.where(closed, MASKED, 0.0).astype(bf16)

    slot = lax.broadcasted_iota(i32, (BLK, 1), 0)
    aug_ref[0:half_len] = key_aug(own_seg, own_inside)
    aug_ref[half_len : 2 * half_len] = key_aug(par_seg, par_inside)
    aug_ref[2 * half_len :] = jnp.where((slot >= PROMPT) & (lane_seg < 3), MASKED, 0.0).astype(bf16)
    across = segment_of(half * half_len + lax.broadcasted_iota(i32, (1, half_len), 1), first, second)[1]
    far = lax.rem(lax.broadcasted_iota(i32, (4 * BLK, 1), 0), 2 * BLK)
    spread = jnp.where(jnp.minimum(across, 2 * BLK - 1) == far, 1.0, 0.0).astype(bf16)
    slot_bias_ref[...] = dot_nn(table_ref[...], spread)
    blocks = half_len // BLK
    ones = jnp.ones((16, 2 * half_len + BLK), bf16)

    def e_copy(hp):
        at = lax.rem(hp, 2)
        return pltpu.make_async_copy(e_buf.at[at], e_ref.at[hp], sems.at[at])

    keys_all = 2 * half_len + BLK
    tiles_q = half_len // QCOLS
    chunk = keys_all // 3
    units = [(s, qt) for s in range(2) for qt in range(tiles_q)]

    def kept(s):
        return low_lane if s == 0 else jnp.logical_not(low_lane)

    def score_steps(hp, s, qt, slot):
        cols = pl.ds(pl.multiple_of(hp * PAIR, PAIR), PAIR)
        here = slice(qt * QCOLS, (qt + 1) * QCOLS)
        q_e = jnp.concatenate([jnp.where(kept(s), q_ref[here, cols], jnp.zeros((), bf16)), q_aug[here]], axis=1)

        def step(n):
            rows = slice(n * chunk, (n + 1) * chunk)
            score_ref[slot, rows, :] = dot_nt(jnp.concatenate([kall_ref[rows, cols], aug_ref[rows]], axis=1), q_e)

        return [functools.partial(step, n) for n in range(3)]

    for step in score_steps(0, 0, 0, 0):
        step()

    @pl.loop(0, width // PAIR)
    def _(hp):
        @pl.when(hp >= 2)
        def _():
            e_copy(hp - 2).wait()

        cols = pl.ds(pl.multiple_of(hp * PAIR, PAIR), PAIR)
        v_turned = vall_ref[:, cols].T
        for u, (s, qt) in enumerate(units):
            h = 2 * hp + s
            coming = units[(u + 1) % len(units)]
            at = hp if u + 1 < len(units) else jnp.minimum(hp + 1, width // PAIR - 1)
            steps = score_steps(at, *coming, (u + 1) % 2)
            back_far, ahead_far = tile_ref[h, 0, 0:1, BLK - 1 :], tile_ref[h, 2, BLK - 1 :, 0:1]
            other_far = jnp.where(half == 0, ahead_far, back_far)
            values = (back_far, ahead_far, other_far)
            columns = []
            for sub in range(QCOLS // BLK):
                qb = qt * (QCOLS // BLK) + sub
                here = slice(sub * BLK, (sub + 1) * BLK)

                def part_of(kb):
                    part = score_ref[u % 2, kb * BLK : (kb + 1) * BLK, here]
                    if kb == 2 * blocks:
                        slot_rows = pl.ds(pl.multiple_of(h * BLK, BLK), BLK)
                        return part + slot_bias_ref[slot_rows, qb * BLK : (qb + 1) * BLK], None
                    gap = kb - qb
                    if kb < blocks and abs(gap) <= 1:
                        return part + tile_ref[h, gap + 1], None
                    if kb < blocks:
                        return part, 0 if gap < 0 else 1
                    if qb == blocks - 1 and kb == blocks:
                        return part + jnp.where(half == 0, tile_ref[h, 2], back_far), None
                    if qb == 0 and kb == 2 * blocks - 1:
                        return part + jnp.where(half == 0, ahead_far, tile_ref[h, 0]), None
                    return part, 2

                tops, group = {}, {}
                for kb in range(2 * blocks + 1):
                    part, const = part_of(kb)
                    if const is None:
                        score_ref[u % 2, kb * BLK : (kb + 1) * BLK, here] = part
                    group[kb] = const
                    top = jnp.max(part.reshape(BLK // 8, 8, BLK), axis=0)
                    tops[const] = top if const not in tops else jnp.maximum(tops[const], top)
                    if steps and kb == 4:
                        steps.pop(0)()
                peak = functools.reduce(
                    jnp.maximum, [top if const is None else top + values[const] for const, top in tops.items()]
                )
                peak = jnp.max(peak, axis=0, keepdims=True)
                shifts = [peak - value for value in values]
                column = []
                for kb in range(2 * blocks + 1):
                    part = score_ref[u % 2, kb * BLK : (kb + 1) * BLK, here]
                    shift = peak if group[kb] is None else shifts[group[kb]]
                    column.append(jnp.exp(part - shift).astype(bf16))
                    if steps and kb == 4:
                        steps.pop(0)()
                columns.append(jnp.concatenate(column, axis=0))
            for step in steps:
                step()
            raised = jnp.concatenate(columns, axis=1)
            qcols = slice(qt * QCOLS, (qt + 1) * QCOLS)
            e_buf[lax.rem(hp, 2), s, :, qcols] = raised
            total = dot_nn(jnp.concatenate([v_turned[s * HEAD : (s + 1) * HEAD], ones], axis=0), raised)
            inv = 1.0 / total[HEAD : HEAD + 1]
            inv_ref[pl.ds(h, 1), qcols] = inv
            mixed_ref[pl.ds(pl.multiple_of(h * HEAD, HEAD), HEAD), qcols] = (total[:HEAD] * inv).astype(bf16)
        e_copy(hp).start()

    for fetch in fetches:
        fetch.wait()
    after_ref[...] = dot_tn(mixed_ref[...], wo_ref[...])

    @pl.loop(0, half_len // BLK)
    def _(t):
        rows = pl.ds(pl.multiple_of(t * BLK, BLK), BLK)
        after = hid_ref[rows, :].astype(f32) + after_ref[rows, :]
        after_ref[rows, :] = after
        norm_ref[rows, :] = (after * inv_rms(after) * gain_second_ref[...]).astype(bf16)

    @pl.loop(0, wi_ref.shape[1] // wide)
    def _(t):
        cols = pl.ds(pl.multiple_of(t * wide, wide), wide)
        act_ref[:, cols] = jnp.maximum(dot_nn(norm_ref[0:half_len, :], wi_ref[:, cols]), 0.0).astype(bf16)

    @pl.loop(0, width // wide)
    def _(t):
        cols = pl.ds(pl.multiple_of(t * wide, wide), wide)
        made = (after_ref[:, cols] + dot_nn(act_ref[...], wout_ref[:, cols])).astype(bf16)
        made = [made[j * piece : (j + 1) * piece] for j in range(count)]
        for k in range(count):
            place = slot_of(turn - k - 1, count)
            sent = made[0]
            for j in range(1, count):
                sent = jnp.where(place == j, made[j], sent)
            going[k][:, cols] = sent

    for hp in range(width // PAIR - 2, width // PAIR):
        e_copy(hp).wait()


def backward_kernel(count, piece, rows_own, *refs):
    cots = refs[:count]
    (
        marks_ref, act_ref, after_ref, mixed_ref, inv_ref, q_ref, kall_ref, vall_ref, prompt_ref, gain_first_ref, gain_second_ref,
        wout_ref, wi_ref, wo_ref, wq_ref, wk_ref, wv_ref, e_ref,
        kept_ref, sent_ref,
        cot_ref, acc_ref, low_ref, do_ref, dq_ref, gk_ref, gv_ref, cast_ref, e_buf, sems,
    ) = refs[count:]
    half, turn = places(count)
    first, second = marks_ref[0:1, 0:1], marks_ref[1:2, 0:1]
    half_len = count * piece
    width = q_ref.shape[1]
    pairs = width // PAIR

    def e_copy(hp):
        at = lax.rem(hp, 2)
        return pltpu.make_async_copy(e_ref.at[hp], e_buf.at[at], sems.at[at])

    for hp in range(2):
        e_copy(hp).start()
    for j in range(count):
        cot_ref[j * piece : (j + 1) * piece, :] = pick_piece(cots, turn, j)
    wide = 4 * BLK
    acc_ref[...] = jnp.zeros_like(acc_ref)

    @pl.loop(0, wi_ref.shape[1] // wide)
    def _(t):
        cols = pl.ds(pl.multiple_of(t * wide, wide), wide)
        grad_act = dot_nt(cot_ref[...], wout_ref[cols, :])
        grad_inner = jnp.where(act_ref[:, cols] > 0, grad_act, 0.0).astype(bf16)
        acc_ref[...] += dot_nt(grad_inner, wi_ref[:, cols])

    gain = gain_second_ref[...]

    @pl.loop(0, half_len // BLK)
    def _(t):
        rows = pl.ds(pl.multiple_of(t * BLK, BLK), BLK)
        after = after_ref[rows, :]
        scale = inv_rms(after)
        pulled = gain * acc_ref[rows, :]
        along = jnp.mean(after * pulled, axis=-1, keepdims=True)
        grad_after = cot_ref[rows, :].astype(f32) + scale * pulled - after * (scale * scale * scale * along)
        acc_ref[rows, :] = grad_after
        low_ref[rows, :] = grad_after.astype(bf16)

    do_ref[...] = dot_nt(wo_ref[...], low_ref[...])

    low_lane = lax.broadcasted_iota(i32, (1, PAIR), 1) < HEAD
    row = lax.broadcasted_iota(i32, (PAIR, 1), 0)
    ones = jnp.ones((2 * half_len + BLK, PAIR), bf16)

    @pl.loop(0, pairs)
    def _(hp):
        e_copy(hp).wait()
        cols = pl.ds(pl.multiple_of(hp * PAIR, PAIR), PAIR)
        q_pair, k_turned, v_pair = q_ref[:, cols], kall_ref[:, cols].T, vall_ref[:, cols]
        inv_both = jnp.where(row < HEAD, inv_ref[pl.ds(2 * hp, 1), :], inv_ref[pl.ds(2 * hp + 1, 1), :])
        do_pair = (do_ref[cols, :] * inv_both).astype(bf16)
        inner = do_pair.astype(f32) * mixed_ref[cols, :].astype(f32)
        slot_scores, slot_raised = [], []
        for s in range(2):
            mine = (row < HEAD) == (s == 0)
            high, low = split_two(-jnp.sum(inner[s * HEAD : (s + 1) * HEAD], axis=0, keepdims=True))
            zero = jnp.zeros((), bf16)
            shift = jnp.where(row == 0, high, jnp.where(row == 1, low, zero))
            do_e = jnp.concatenate([jnp.where(mine, do_pair, zero), shift], axis=0)
            raised = e_buf[lax.rem(hp, 2), s]
            grad_probs = dot_nn(jnp.concatenate([v_pair, ones], axis=1), do_e)
            grad_scores = (raised.astype(f32) * grad_probs).astype(bf16)
            made = dot_nn(k_turned[s * HEAD : (s + 1) * HEAD], grad_scores)
            dq_ref[pl.ds(pl.multiple_of(hp * PAIR + s * HEAD, HEAD), HEAD), :] = made.astype(bf16)
            slot_scores.append(grad_scores[2 * half_len :])
            slot_raised.append(raised[2 * half_len :])
        dk = dot_nn(jnp.concatenate(slot_scores, axis=0), q_pair)
        dv = dot_nt(jnp.concatenate(slot_raised, axis=0), do_pair)
        gk_ref[:, cols] = jnp.where(low_lane, dk[:BLK], dk[BLK:]).astype(bf16)
        gv_ref[:, cols] = jnp.where(low_lane, dv[:BLK], dv[BLK:]).astype(bf16)

        @pl.when(hp + 2 < pairs)
        def _():
            e_copy(hp + 2).start()

    spot = lax.broadcasted_iota(i32, (1, half_len), 1)
    inside = segment_of(half * half_len + spot, first, second)[1]
    slots = lax.broadcasted_iota(i32, (BLK, 1), 0)
    choose = jnp.where((inside == slots) & (inside < PROMPT), 1.0, 0.0).astype(bf16)
    gq = dot_nt(choose, dq_ref[...]).astype(bf16)
    pulled = dot_nt(gq, wq_ref[...]) + dot_nt(gk_ref[...], wk_ref[...]) + dot_nt(gv_ref[...], wv_ref[...])
    high, low = split_two(acc_ref[...])
    direct = dot_nn(choose, high) + dot_nn(choose, low)
    hidden = prompt_ref[...].astype(f32)
    scale = inv_rms(hidden)
    pulled = gain_first_ref[...] * pulled
    along = jnp.mean(hidden * pulled, axis=-1, keepdims=True)
    grad = direct + scale * pulled - hidden * (scale * scale * scale * along)
    for place in range(BLK // (2 * rows_own)):
        rows = slice(place * rows_own, (place + 1) * rows_own)
        low, high = (grad[(2 * place + c) * rows_own : (2 * place + c + 1) * rows_own] for c in range(2))
        kept_ref[rows, :] = jnp.where(half == 0, low, high)
        cast_ref[rows, :] = jnp.where(half == 0, high, low)
    sent_ref[...] = cast_ref[...].astype(bf16)


def share_kernel(rows_own, kept_ref, came_ref, mine_ref, *refs):
    parts, (total_ref,) = refs[:-1], refs[-1:]
    chip = lax.div(lax.axis_index("dp"), 2)
    total = kept_ref[...] + came_ref[...].astype(f32)
    for place in range(len(parts) + 1):
        total_ref[place] = total[place * rows_own : (place + 1) * rows_own]
    mine_ref[...] = total_ref[chip]
    for n in range(1, len(parts) + 1):
        parts[n - 1][...] = total_ref[chip ^ n].astype(bf16)


def square_kernel(total_ref, *refs):
    parts, (own_ref, square_ref) = refs[:-2], refs[-2:]
    total = total_ref[...]
    for part in parts:
        total = total + part[...].astype(f32)
    few = own_ref.shape[1]
    own = total[:, 0:few]
    for place in range(1, len(parts) + 1):
        own = jnp.where(lax.axis_index("ctx") == place, total[:, place * few : (place + 1) * few], own)
    own_ref[...] = own
    square = jnp.sum(jnp.sum(total * total, axis=1, keepdims=True), axis=0, keepdims=True)
    square_ref[...] = jnp.broadcast_to(square, square_ref.shape)


def update_kernel(max_norm, grad_ref, prompt_ref, first_ref, second_ref, *refs):
    squares, (prompt_out, first_out, second_out) = refs[:-3], refs[-3:]
    square = functools.reduce(jnp.add, [square[0:1, 0:1] for square in squares])
    clipped = grad_ref[...] * (max_norm / jnp.maximum(jnp.sqrt(square), max_norm))
    first_new = beta_first * first_ref[...] + (1.0 - beta_first) * clipped
    second_new = beta_second * second_ref[...] + (1.0 - beta_second) * clipped * clipped
    step = learn_rate * (first_new / first_fix) / (jnp.sqrt(second_new / second_fix) + adam_eps)
    prompt_out[...] = prompt_ref[...] - step
    first_out[...] = first_new
    second_out[...] = second_new


def on_device(
    sizes, tokens, segment_ids, prompt_slots, cotangent, w_query, w_key, w_value, w_output, w_inner, w_outer,
    gain_first, gain_second, bias_table, prompt, first_moment, second_moment,
):
    n_dp, n_ctx = sizes
    count, piece, width = tokens.shape
    half_len = count * piece
    heads = bias_table.shape[1]
    dp, ctx = lax.axis_index("dp"), lax.axis_index("ctx")
    core = lax.rem(dp, 2)

    def permute(value, target):
        pairs = []
        for d in range(n_dp):
            for z in range(n_ctx):
                d2, z2 = target(d, z)
                pairs.append((d * n_ctx + z, d2 * n_ctx + z2))
        return lax.ppermute(value, AXES, pairs)

    def swap_dp(value, bit):
        return permute(value, lambda d, z: (d ^ bit, z))

    def swap_ctx(value, bit):
        return permute(value, lambda d, z: (d, z ^ bit))

    def there(k):
        return lambda d, z: (2 * (d // 2) + z // count, (d % 2) * count + (z + k + 1) % count)

    rows_own, cols_own = prompt.shape
    piece_like = held((piece, width), bf16)
    packed = pl.pallas_call(
        functools.partial(pack_kernel, count),
        out_shape=[piece_like] * count + [held((rows_own + 8, cols_own), bf16)],
        in_specs=[any_spec()] * 3,
        out_specs=[vmem_spec()] * (count + 1),
        scratch_shapes=[
            pltpu.VMEM(segment_ids.shape, i32),
            pltpu.VMEM(prompt.shape, f32),
            pltpu.VMEM((rows_own + 8, cols_own), f32),
            pltpu.SemaphoreType.DMA((count + 2,)),
        ],
        compiler_params=params(4),
        cost_estimate=cost(1e5, 2e6),
    )(in_hbm(tokens), in_hbm(segment_ids), in_hbm(prompt))

    own = [permute(packed[k], there(k)) for k in range(count)]
    chip_rows = jnp.concatenate([packed[count], swap_dp(packed[count], 1)], axis=0)
    chip_parts = [chip_rows] + [swap_dp(chip_rows, 2 * n) for n in range(1, n_dp // 2)]
    plane = pl.pallas_call(
        functools.partial(plane_kernel, rows_own),
        out_shape=held((HELD, cols_own), bf16),
        in_specs=[vmem_spec()] * len(chip_parts),
        out_specs=vmem_spec(),
        scratch_shapes=[pltpu.VMEM((BLK + 16, cols_own), f32)],
        compiler_params=params(4),
        cost_estimate=cost(1e5, 1e5),
    )(*chip_parts)

    choose = (np.arange(bias_table.shape[0])[:, None] == bucket_table(2 * BLK - np.arange(4 * BLK))[None]).astype(np.float32)
    base = lax.dot_general(
        bias_table, jnp.asarray(choose), (((0,), (0,)), ((), ())), precision=lax.Precision.HIGHEST
    )
    base, plane = lax.optimization_barrier((base, plane))
    cols_mine = jnp.concatenate([plane] + [swap_ctx(plane, n) for n in range(1, n_ctx)], axis=0)
    cols_other = swap_dp(cols_mine, 1)
    weights = (w_query, w_key, w_value)
    prepared = pl.pallas_call(
        functools.partial(prepare_kernel, count),
        out_shape=[held((heads, 3, BLK, BLK), f32), held((heads * BLK, 4 * BLK), bf16)]
        + [held((1, width), f32)] * 2
        + [piece_like] * count
        + [held(w.shape, bf16) for w in weights],
        in_specs=[vmem_spec()] * 3 + [any_spec()] * 4,
        out_specs=[vmem_spec()] * (7 + count),
        scratch_shapes=[pltpu.SemaphoreType.DMA((3 + count,))],
        compiler_params=params(4),
        cost_estimate=cost(1e6, 5e6),
    )(base, gain_first[None], gain_second[None], in_hbm(cotangent), *[in_hbm(w) for w in weights])
    tiles, table, gain_1, gain_2 = prepared[:4]
    cot_pieces = prepared[4 : 4 + count]
    w_q, w_k, w_v = prepared[4 + count :]

    keys_all = 2 * half_len + BLK
    hidden_ff = w_inner.shape[1]
    partner = [swap_dp(piece_rows, 1) for piece_rows in own]
    normed = pl.pallas_call(
        functools.partial(first_kernel, count, piece),
        out_shape=held((half_len, width), bf16),
        in_specs=[vmem_spec()] * (count + 1),
        out_specs=vmem_spec(),
        compiler_params=params(A_MIB),
        cost_estimate=cost(1e10, 8e6),
    )(*own, gain_1)
    cots = [permute(cot_pieces[k], there(k)) for k in range(count)]

    made = pl.pallas_call(
        functools.partial(forward_kernel, count, piece, rows_own),
        out_shape=[
            pltpu.HBM((heads // 2, 2, keys_all, half_len), bf16),
            held((8, BLK), i32),
            held((BLK, width), bf16),
            held((half_len, width), bf16),
            held((keys_all, width), bf16),
            held((keys_all, width), bf16),
            held((width, half_len), bf16),
            held((heads, half_len), f32),
            held((half_len, width), f32),
            held((half_len, hidden_ff), bf16),
        ]
        + [held(w.shape, bf16) for w in (w_output, w_inner, w_outer)]
        + [piece_like] * count,
        in_specs=[vmem_spec()] * (2 * count + 10) + [any_spec()] * 3,
        out_specs=[any_spec()] + [vmem_spec()] * (12 + count),
        scratch_shapes=[
            pltpu.VMEM((2 * half_len + BLK, width), bf16),
            pltpu.VMEM((half_len, width), bf16),
            pltpu.VMEM((heads * BLK, half_len), f32),
            pltpu.VMEM((2, keys_all, QCOLS), f32),
            pltpu.VMEM((keys_all, PAIR), bf16),
            pltpu.VMEM((BLK, width), f32),
            pltpu.VMEM((2, 2, keys_all, half_len), bf16),
            pltpu.SemaphoreType.DMA((2,)),
            pltpu.SemaphoreType.DMA((3,)),
        ],
        compiler_params=params(F_MIB),
        cost_estimate=cost(3e10, 4e7, heads * half_len * keys_all),
    )(
        *own, *partner, normed, gain_1, gain_2, w_q, w_k, w_v, tiles, table, cols_mine, cols_other,
        *[in_hbm(w) for w in (w_output, w_inner, w_outer)],
    )
    got = [permute(made[13 + k], back_of(count, k)) for k in range(count)]
    w_o, w_i, w_out = made[10:13]
    e, marks, sent, q, kall, vall, mixed, inv, after, act = made[:10]

    half_rows = n_dp // 2 * rows_own
    kept, leaving = pl.pallas_call(
        functools.partial(backward_kernel, count, piece, rows_own),
        out_shape=[held((half_rows, width), f32), held((half_rows, width), bf16)],
        in_specs=[vmem_spec()] * (count + 17) + [any_spec()],
        out_specs=[vmem_spec()] * 2,
        scratch_shapes=[
            pltpu.VMEM((half_len, width), bf16),
            pltpu.VMEM((half_len, width), f32),
            pltpu.VMEM((half_len, width), bf16),
            pltpu.VMEM((width, half_len), f32),
            pltpu.VMEM((width, half_len), bf16),
            pltpu.VMEM((BLK, width), bf16),
            pltpu.VMEM((BLK, width), bf16),
            pltpu.VMEM((half_rows, width), f32),
            pltpu.VMEM((2, 2, keys_all, half_len), bf16),
            pltpu.SemaphoreType.DMA((2,)),
        ],
        compiler_params=params(B_MIB),
        cost_estimate=cost(3e10, 4e7),
    )(
        *cots, marks, act, after, mixed, inv, q, kall, vall, sent, gain_1, gain_2, w_out, w_i, w_o, w_q, w_k, w_v, in_hbm(e),
    )

    got, leaving = lax.optimization_barrier((got, leaving))
    order = [lax.rem(ctx + j + 1, count) for j in range(count)]
    output = jnp.stack(
        [functools.reduce(lambda a, k: jnp.where(order[k] == r, got[k], a), range(1, count), got[0]) for r in range(count)]
    )

    chips = n_dp // 2
    own_like = held((rows_own, width), f32)
    mine, *parts = pl.pallas_call(
        functools.partial(share_kernel, rows_own),
        out_shape=[own_like] + [held((rows_own, width), bf16)] * (chips - 1),
        in_specs=[vmem_spec()] * 2,
        out_specs=[vmem_spec()] * chips,
        scratch_shapes=[pltpu.VMEM((chips, rows_own, width), f32)],
        compiler_params=params(4),
        cost_estimate=cost(1e5, 1e5),
    )(kept, swap_dp(leaving, 1))
    for n in range(1, chips):
        mine = mine + swap_dp(parts[n - 1], 2 * n).astype(f32)
    line = mine.astype(bf16)
    line_parts = [swap_ctx(line, n) for n in range(1, n_ctx)]
    line_parts, output = lax.optimization_barrier((line_parts, output))
    grad_own, square = pl.pallas_call(
        square_kernel,
        out_shape=[held((rows_own, cols_own), f32), held((8, BLK), f32)],
        in_specs=[vmem_spec()] * n_ctx,
        out_specs=[vmem_spec()] * 2,
        compiler_params=params(4),
        cost_estimate=cost(1e5, 1e5),
    )(mine, *line_parts)
    square = square + swap_dp(square, 1)
    squares = [square] + [swap_dp(square, 2 * n) for n in range(1, chips)]
    own_out = out((rows_own, cols_own), f32)
    prompt_new, first_new, second_new = pl.pallas_call(
        functools.partial(update_kernel, float(0.5 * np.sqrt(np.float32(PROMPT * width)))),
        out_shape=[own_out] * 3,
        in_specs=[vmem_spec()] * (4 + chips),
        out_specs=[vmem_spec()] * 3,
        compiler_params=params(4),
        cost_estimate=cost(1e5, 1e5),
    )(grad_own, prompt, first_moment, second_moment, *squares)
    return (output, prompt_new, first_new, second_new)


def back_of(count, k):
    def target(d, z):
        half, c, r = d % 2, z // count, z % count
        return (2 * (d // 2) + c, half * count + (r - k - 1) % count)

    return target


def solution(mesh):
    rows, cols = P("dp", "ctx", None), P("dp", "ctx")
    placed = (rows, cols, cols, rows) + (P(),) * 9 + (cols,) * 3
    return jax.shard_map(
        functools.partial(on_device, (mesh.shape["dp"], mesh.shape["ctx"])),
        mesh=mesh,
        in_specs=placed,
        out_specs=(rows, cols, cols, cols),
        check_vma=False,
    )
```

```python
import functools

import jax
import jax.numpy as jnp
import numpy as np
from jax import lax
from jax.experimental import pallas as pl
from jax.experimental.pallas import tpu as pltpu
from jax.sharding import PartitionSpec as P

PROMPT = 100
HEAD = 64
PAIR = 2 * HEAD
BLK = 128
SHOWN = 112
HELD = (SHOWN + 16) // 2
QCOLS = 256
UNITS = 1536
norm_eps = 1e-06
beta_first = 0.9
beta_second = 0.999
adam_eps = 1e-08
learn_rate = 0.1
first_fix = 1.0 - 0.9**8
second_fix = 1.0 - 0.999**8
far_marks = (12, 16, 23, 32, 46, 64, 91)
f32 = jnp.float32
bf16 = jnp.bfloat16
i32 = jnp.int32
MASKED = -float(2**30)
AXES = ("dp", "ctx")
MIB = 1 << 20
A_MIB, F_MIB, B_MIB = 6, 20, 18


def bucket_table(offset):
    distance = np.abs(offset)
    passed = sum((distance >= mark).astype(np.int32) for mark in far_marks)
    far_ids = np.minimum(8 + passed, 15)
    return np.where(distance < 8, distance, far_ids) + 16 * (offset > 0).astype(np.int32)


def dot_nn(a, b):
    return lax.dot_general(a, b, (((1,), (0,)), ((), ())), preferred_element_type=f32)


def dot_nt(a, b):
    return lax.dot_general(a, b, (((1,), (1,)), ((), ())), preferred_element_type=f32)


def dot_tn(a, b):
    return lax.dot_general(a, b, (((0,), (0,)), ((), ())), preferred_element_type=f32)


def split_two(values):
    high = values.astype(bf16)
    return high, (values - high.astype(f32)).astype(bf16)


def inv_rms(values):
    return lax.rsqrt(jnp.mean(values * values, axis=-1, keepdims=True) + norm_eps)


def segment_of(place, first, second):
    seg = (place >= first).astype(i32) + (place >= second).astype(i32)
    start = jnp.where(seg == 0, 0, jnp.where(seg == 1, first, second))
    return seg, place - start


def vmem_spec():
    return pl.BlockSpec(memory_space=pltpu.VMEM)


def smem_spec():
    return pl.BlockSpec(memory_space=pltpu.SMEM)


def any_spec():
    return pl.BlockSpec(memory_space=pl.ANY)


def out(shape, dtype):
    return jax.ShapeDtypeStruct(shape, dtype)


def held(shape, dtype):
    return pltpu.VMEM(shape, dtype)


def in_vmem(value):
    return pltpu.with_memory_space_constraint(value, pltpu.VMEM)


def in_hbm(value):
    return pltpu.with_memory_space_constraint(value, pltpu.HBM)


def params(mib):
    return pltpu.CompilerParams(vmem_limit_bytes=mib * MIB)


def cost(flops, nbytes, trans=0):
    return pl.CostEstimate(flops=int(flops), bytes_accessed=int(nbytes), transcendentals=int(trans))


def pick_piece(pieces, turn, j):
    count = len(pieces)
    place = lax.rem(turn - j - 1 + count, count)
    picked = pieces[0][...]
    for k in range(1, count):
        picked = jnp.where(place == k, pieces[k][...], picked)
    return picked


def slot_of(index, count):
    return lax.rem(index + 2 * count, count)


def pack_kernel(count, tokens_ref, seg_hbm, prompt_hbm, *refs):
    pieces, (block_ref, seg_ref, prompt_ref, wide_ref, sems) = refs[:count], refs[count:]
    ctx = lax.axis_index("ctx")
    copies = [
        pltpu.make_async_copy(tokens_ref.at[slot_of(ctx + k + 1, count)], pieces[k], sems.at[k]) for k in range(count)
    ]
    small = [
        pltpu.make_async_copy(seg_hbm, seg_ref, sems.at[count]),
        pltpu.make_async_copy(prompt_hbm, prompt_ref, sems.at[count + 1]),
    ]
    for copy in small + copies:
        copy.start()
    for copy in small:
        copy.wait()
    rows = prompt_ref.shape[0]
    wide_ref[...] = jnp.zeros_like(wide_ref)
    wide_ref[0:rows, :] = prompt_ref[...]
    for n in range(2):
        tally = jnp.sum((seg_ref[...] <= n).astype(f32), axis=1, keepdims=True)
        wide_ref[rows + n * count : rows + (n + 1) * count, :] = jnp.broadcast_to(tally, (count, prompt_ref.shape[1]))
    block_ref[...] = wide_ref[...].astype(bf16)
    for copy in copies:
        copy.wait()


def prepare_kernel(count, base_ref, gain_first_ref, gain_second_ref, cot_ref, *refs):
    weights, (tile_ref, table_ref, first_ref, second_ref) = refs[:3], refs[3:7]
    pieces, kept, sems = refs[7 : 7 + count], refs[7 + count : 10 + count], refs[10 + count]
    first_ref[...] = gain_first_ref[...]
    second_ref[...] = gain_second_ref[...]
    ctx = lax.axis_index("ctx")
    copies = [pltpu.make_async_copy(weights[n], kept[n], sems.at[n]) for n in range(3)] + [
        pltpu.make_async_copy(cot_ref.at[slot_of(ctx + k + 1, count)], pieces[k], sems.at[3 + k]) for k in range(count)
    ]
    for copy in copies:
        copy.start()
    heads = tile_ref.shape[0]
    for h in range(heads):
        row = jnp.broadcast_to(base_ref[h : h + 1, :], (BLK, 4 * BLK))
        spread = pltpu.roll(row, 0, 1, stride=1, stride_axis=0)
        low, mid, top = (spread[:, k * BLK : (k + 1) * BLK] for k in (3, 2, 1))
        tile_ref[h, 0] = low
        tile_ref[h, 1] = mid
        tile_ref[h, 2] = top
        rows = slice(h * BLK, (h + 1) * BLK)
        parts = [part for pair in zip(split_two(mid), split_two(low)) for part in pair]
        for k in range(4):
            table_ref[rows, k * BLK : (k + 1) * BLK] = parts[k]
    for copy in copies:
        copy.wait()


def plane_kernel(rows_own, *refs):
    parts, (out_ref, wide_ref) = refs[:-2], refs[-2:]
    core, chip = lax.rem(lax.axis_index("dp"), 2), lax.div(lax.axis_index("dp"), 2)
    high = rows_own + 8
    parts = [part[...].astype(f32) for part in parts]
    parts = [[jnp.where(core == c, part[:high], part[high:]) for c in range(2)] for part in parts]
    for place in range(len(parts)):
        for c in range(2):
            picked = parts[0][c]
            for n in range(1, len(parts)):
                picked = jnp.where((chip ^ n) == place, parts[n][c], picked)
            start = (2 * place + c) * rows_own
            wide_ref[start : start + rows_own, :] = picked[:rows_own]
    for c in range(2):
        wide_ref[SHOWN + 8 * c : SHOWN + 8 * (c + 1), :] = parts[0][c][rows_own:]
    out_ref[...] = jnp.where(core == 0, wide_ref[0:HELD, :], wide_ref[HELD : 2 * HELD, :]).astype(bf16)


def places(count):
    return lax.rem(lax.axis_index("dp"), 2), lax.rem(lax.axis_index("ctx"), count)


def first_kernel(count, piece, *refs):
    own, (gain_ref, norm_ref) = refs[:count], refs[count:]
    turn = places(count)[1]
    for j in range(count):
        tok = pick_piece(own, turn, j).astype(f32)
        norm_ref[j * piece : (j + 1) * piece, :] = (tok * inv_rms(tok) * gain_ref[...]).astype(bf16)


def forward_kernel(count, piece, rows_own, *refs):
    own, partner = refs[:count], refs[count : 2 * count]
    (
        normed_ref, gain_first_ref, gain_second_ref, wq_ref, wk_ref, wv_ref, tile_ref, table_ref,
    ) = refs[2 * count : 2 * count + 8]
    refs = refs[2 * count + 8 :]
    (mine_ref, other_ref), later, refs = refs[:2], refs[2:5], refs[5:]
    e_ref, marks_ref, prompt_ref, q_ref, kall_ref, vall_ref, mixed_ref, inv_ref, after_ref, act_ref = refs[:10]
    kept, refs = refs[10:13], refs[13:]
    wo_ref, wi_ref, wout_ref = kept
    going, refs = refs[:count], refs[count:]
    norm_ref, hid_ref, slot_bias_ref, score_ref, aug_ref, shown_ref, e_buf, sems, weight_sems = refs
    fetches = [pltpu.make_async_copy(later[n], kept[n], weight_sems.at[n]) for n in range(3)]
    for fetch in fetches:
        fetch.start()
    ctx = lax.axis_index("ctx")
    half, turn = places(count)
    few = mine_ref.shape[1]
    low = jnp.where(half == 0, mine_ref[...], other_ref[...]).astype(f32)
    high = jnp.where(half == 0, other_ref[...], mine_ref[...]).astype(f32)
    for place in range(2 * count):
        for part, start, stop in ((low, 0, HELD), (high, HELD, SHOWN)):
            picked = part[0 : stop - start]
            for n in range(1, 2 * count):
                picked = jnp.where((ctx ^ n) == place, part[n * HELD : n * HELD + stop - start], picked)
            shown_ref[start:stop, place * few : (place + 1) * few] = picked
    shown_ref[SHOWN:, :] = jnp.zeros((BLK - SHOWN, shown_ref.shape[1]), f32)
    prompt_ref[...] = shown_ref[...].astype(bf16)
    half_len = count * piece
    width = q_ref.shape[1]
    tally = functools.reduce(jnp.add, [high[(n + 1) * HELD - 16 : (n + 1) * HELD] for n in range(2 * count)])
    tally_row = lax.broadcasted_iota(i32, (tally.shape[0], 1), 0)
    marks = []
    for n in range(2):
        here = tally_row == 8 * lax.div(ctx, count) + n * count + turn
        total = jnp.sum(jnp.where(here, tally, 0.0), axis=0, keepdims=True)[:, 0:1]
        marks.append((total + 0.5).astype(i32))
        marks_ref[n : n + 1, :] = jnp.broadcast_to(marks[n], (1, BLK))
    first, second = marks
    gain = gain_first_ref[...]
    slots = lax.broadcasted_iota(i32, (1, BLK), 1)
    for j in range(count):
        rows = slice(j * piece, (j + 1) * piece)
        place = half * half_len + j * piece + lax.broadcasted_iota(i32, (piece, 1), 0)
        inside = segment_of(place, first, second)[1]
        shown = inside < PROMPT
        choose = jnp.where((inside == slots) & shown, 1.0, 0.0).astype(bf16)
        picked = dot_nn(choose, prompt_ref[...])
        hidden = jnp.where(shown, picked, pick_piece(own, turn, j).astype(f32))
        hid_ref[rows, :] = hidden.astype(bf16)
        norm_ref[half_len + BLK + j * piece : half_len + BLK + (j + 1) * piece, :] = (
            hidden * inv_rms(hidden) * gain
        ).astype(bf16)
        tok = pick_piece(partner, turn, j).astype(f32)
        norm_ref[rows, :] = (tok * inv_rms(tok) * gain).astype(bf16)
    hidden = prompt_ref[...].astype(f32)
    norm_ref[half_len : half_len + BLK, :] = (hidden * inv_rms(hidden) * gain).astype(bf16)
    wide = 2 * BLK

    @pl.loop(0, width // wide)
    def _(t):
        cols = pl.ds(pl.multiple_of(t * wide, wide), wide)
        normed = jnp.concatenate([normed_ref[...], norm_ref[0 : half_len + BLK, :]], axis=0)
        kall_ref[:, cols] = dot_nn(normed, wk_ref[:, cols]).astype(bf16)
        vall_ref[:, cols] = dot_nn(normed, wv_ref[:, cols]).astype(bf16)
        q_ref[:, cols] = dot_nn(norm_ref[half_len + BLK :, :], wq_ref[:, cols]).astype(bf16)

    lane = lax.broadcasted_iota(i32, (1, PAIR), 1)
    low_lane = lane < HEAD
    lane_seg = lane
    spot = lax.broadcasted_iota(i32, (half_len, 1), 0)
    own_seg, own_inside = segment_of(half * half_len + spot, first, second)
    par_seg, par_inside = segment_of((1 - half) * half_len + spot, first, second)
    q_aug = jnp.where(own_seg == lane_seg, 1.0, 0.0).astype(bf16)

    def key_aug(seg, inside):
        closed = ((seg != lane_seg) | (inside < PROMPT)) & (lane_seg < 3)
        return jnp.where(closed, MASKED, 0.0).astype(bf16)

    slot = lax.broadcasted_iota(i32, (BLK, 1), 0)
    aug_ref[0:half_len] = key_aug(own_seg, own_inside)
    aug_ref[half_len : 2 * half_len] = key_aug(par_seg, par_inside)
    aug_ref[2 * half_len :] = jnp.where((slot >= PROMPT) & (lane_seg < 3), MASKED, 0.0).astype(bf16)
    across = segment_of(half * half_len + lax.broadcasted_iota(i32, (1, half_len), 1), first, second)[1]
    far = lax.rem(lax.broadcasted_iota(i32, (4 * BLK, 1), 0), 2 * BLK)
    spread = jnp.where(jnp.minimum(across, 2 * BLK - 1) == far, 1.0, 0.0).astype(bf16)
    slot_bias_ref[...] = dot_nn(table_ref[...], spread)
    blocks = half_len // BLK
    ones = jnp.ones((16, 2 * half_len + BLK), bf16)

    def e_copy(hp):
        at = lax.rem(hp, 2)
        return pltpu.make_async_copy(e_buf.at[at], e_ref.at[hp], sems.at[at])

    keys_all = 2 * half_len + BLK
    tiles_q = half_len // QCOLS
    chunk = keys_all // 3
    units = [(s, qt) for s in range(2) for qt in range(tiles_q)]

    def kept(s):
        return low_lane if s == 0 else jnp.logical_not(low_lane)

    def score_steps(hp, s, qt, slot):
        cols = pl.ds(pl.multiple_of(hp * PAIR, PAIR), PAIR)
        here = slice(qt * QCOLS, (qt + 1) * QCOLS)
        q_e = jnp.concatenate([jnp.where(kept(s), q_ref[here, cols], jnp.zeros((), bf16)), q_aug[here]], axis=1)

        def step(n):
            rows = slice(n * chunk, (n + 1) * chunk)
            score_ref[slot, rows, :] = dot_nt(jnp.concatenate([kall_ref[rows, cols], aug_ref[rows]], axis=1), q_e)

        return [functools.partial(step, n) for n in range(3)]

    for step in score_steps(0, 0, 0, 0):
        step()

    @pl.loop(0, width // PAIR)
    def _(hp):
        @pl.when(hp >= 2)
        def _():
            e_copy(hp - 2).wait()

        cols = pl.ds(pl.multiple_of(hp * PAIR, PAIR), PAIR)
        v_turned = vall_ref[:, cols].T
        for u, (s, qt) in enumerate(units):
            h = 2 * hp + s
            coming = units[(u + 1) % len(units)]
            at = hp if u + 1 < len(units) else jnp.minimum(hp + 1, width // PAIR - 1)
            steps = score_steps(at, *coming, (u + 1) % 2)
            back_far, ahead_far = tile_ref[h, 0, 0:1, BLK - 1 :], tile_ref[h, 2, BLK - 1 :, 0:1]
            other_far = jnp.where(half == 0, ahead_far, back_far)
            values = (back_far, ahead_far, other_far)
            columns = []
            for sub in range(QCOLS // BLK):
                qb = qt * (QCOLS // BLK) + sub
                here = slice(sub * BLK, (sub + 1) * BLK)

                def part_of(kb):
                    part = score_ref[u % 2, kb * BLK : (kb + 1) * BLK, here]
                    if kb == 2 * blocks:
                        slot_rows = pl.ds(pl.multiple_of(h * BLK, BLK), BLK)
                        return part + slot_bias_ref[slot_rows, qb * BLK : (qb + 1) * BLK], None
                    gap = kb - qb
                    if kb < blocks and abs(gap) <= 1:
                        return part + tile_ref[h, gap + 1], None
                    if kb < blocks:
                        return part, 0 if gap < 0 else 1
                    if qb == blocks - 1 and kb == blocks:
                        return part + jnp.where(half == 0, tile_ref[h, 2], back_far), None
                    if qb == 0 and kb == 2 * blocks - 1:
                        return part + jnp.where(half == 0, ahead_far, tile_ref[h, 0]), None
                    return part, 2

                tops, group = {}, {}
                for kb in range(2 * blocks + 1):
                    part, const = part_of(kb)
                    if const is None:
                        score_ref[u % 2, kb * BLK : (kb + 1) * BLK, here] = part
                    group[kb] = const
                    top = jnp.max(part.reshape(BLK // 8, 8, BLK), axis=0)
                    tops[const] = top if const not in tops else jnp.maximum(tops[const], top)
                    if steps and kb == 4:
                        steps.pop(0)()
                peak = functools.reduce(
                    jnp.maximum, [top if const is None else top + values[const] for const, top in tops.items()]
                )
                peak = jnp.max(peak, axis=0, keepdims=True)
                shifts = [peak - value for value in values]
                column = []
                for kb in range(2 * blocks + 1):
                    part = score_ref[u % 2, kb * BLK : (kb + 1) * BLK, here]
                    shift = peak if group[kb] is None else shifts[group[kb]]
                    column.append(jnp.exp(part - shift).astype(bf16))
                    if steps and kb == 4:
                        steps.pop(0)()
                columns.append(jnp.concatenate(column, axis=0))
            for step in steps:
                step()
            raised = jnp.concatenate(columns, axis=1)
            qcols = slice(qt * QCOLS, (qt + 1) * QCOLS)
            e_buf[lax.rem(hp, 2), s, :, qcols] = raised
            total = dot_nn(jnp.concatenate([v_turned[s * HEAD : (s + 1) * HEAD], ones], axis=0), raised)
            inv = 1.0 / total[HEAD : HEAD + 1]
            inv_ref[pl.ds(h, 1), qcols] = inv
            mixed_ref[pl.ds(pl.multiple_of(h * HEAD, HEAD), HEAD), qcols] = (total[:HEAD] * inv).astype(bf16)
        e_copy(hp).start()

    for fetch in fetches:
        fetch.wait()
    after_ref[...] = dot_tn(mixed_ref[...], wo_ref[...])

    @pl.loop(0, half_len // BLK)
    def _(t):
        rows = pl.ds(pl.multiple_of(t * BLK, BLK), BLK)
        after = hid_ref[rows, :].astype(f32) + after_ref[rows, :]
        after_ref[rows, :] = after
        norm_ref[rows, :] = (after * inv_rms(after) * gain_second_ref[...]).astype(bf16)

    @pl.loop(0, wi_ref.shape[1] // UNITS)
    def _(t):
        units = pl.ds(pl.multiple_of(t * UNITS, UNITS), UNITS)
        inner = lax.dot_general(
            wi_ref[:, units], norm_ref[0:half_len, :], (((0,), (1,)), ((), ())), preferred_element_type=f32
        )
        act_ref[units, :] = jnp.maximum(inner, 0.0).astype(bf16)

    made = (after_ref[...] + dot_tn(act_ref[...], wout_ref[...])).astype(bf16)
    made = [made[j * piece : (j + 1) * piece] for j in range(count)]
    for k in range(count):
        place = slot_of(turn - k - 1, count)
        sent = made[0]
        for j in range(1, count):
            sent = jnp.where(place == j, made[j], sent)
        going[k][...] = sent

    for hp in range(width // PAIR - 2, width // PAIR):
        e_copy(hp).wait()


def backward_kernel(count, piece, rows_own, *refs):
    cots = refs[:count]
    (
        marks_ref, act_ref, after_ref, mixed_ref, inv_ref, q_ref, kall_ref, vall_ref, prompt_ref, gain_first_ref, gain_second_ref,
        wout_ref, wi_ref, wo_ref, wq_ref, wk_ref, wv_ref, e_ref,
        kept_ref, sent_ref,
        cot_ref, acc_ref, low_ref, do_ref, dq_ref, gk_ref, gv_ref, cast_ref, e_buf, sems,
    ) = refs[count:]
    half, turn = places(count)
    first, second = marks_ref[0:1, 0:1], marks_ref[1:2, 0:1]
    half_len = count * piece
    width = q_ref.shape[1]
    pairs = width // PAIR

    def e_copy(hp):
        at = lax.rem(hp, 2)
        return pltpu.make_async_copy(e_ref.at[hp], e_buf.at[at], sems.at[at])

    for hp in range(2):
        e_copy(hp).start()
    for j in range(count):
        cot_ref[j * piece : (j + 1) * piece, :] = pick_piece(cots, turn, j)
    do_ref[...] = jnp.zeros_like(do_ref)

    @pl.loop(0, wi_ref.shape[1] // UNITS)
    def _(t):
        units = pl.ds(pl.multiple_of(t * UNITS, UNITS), UNITS)
        grad_act = dot_nt(wout_ref[units, :], cot_ref[...])
        grad_inner = jnp.where(act_ref[units, :] > 0, grad_act, 0.0).astype(bf16)
        do_ref[...] += dot_nn(wi_ref[:, units], grad_inner)

    acc_ref[...] = do_ref[...].T
    gain = gain_second_ref[...]

    @pl.loop(0, half_len // BLK)
    def _(t):
        rows = pl.ds(pl.multiple_of(t * BLK, BLK), BLK)
        after = after_ref[rows, :]
        scale = inv_rms(after)
        pulled = gain * acc_ref[rows, :]
        along = jnp.mean(after * pulled, axis=-1, keepdims=True)
        grad_after = cot_ref[rows, :].astype(f32) + scale * pulled - after * (scale * scale * scale * along)
        acc_ref[rows, :] = grad_after
        low_ref[rows, :] = grad_after.astype(bf16)

    do_ref[...] = dot_nt(wo_ref[...], low_ref[...])

    low_lane = lax.broadcasted_iota(i32, (1, PAIR), 1) < HEAD
    row = lax.broadcasted_iota(i32, (PAIR, 1), 0)
    ones = jnp.ones((2 * half_len + BLK, PAIR), bf16)

    @pl.loop(0, pairs)
    def _(hp):
        e_copy(hp).wait()
        cols = pl.ds(pl.multiple_of(hp * PAIR, PAIR), PAIR)
        q_pair, k_turned, v_pair = q_ref[:, cols], kall_ref[:, cols].T, vall_ref[:, cols]
        inv_both = jnp.where(row < HEAD, inv_ref[pl.ds(2 * hp, 1), :], inv_ref[pl.ds(2 * hp + 1, 1), :])
        do_pair = (do_ref[cols, :] * inv_both).astype(bf16)
        inner = do_pair.astype(f32) * mixed_ref[cols, :].astype(f32)
        slot_scores, slot_raised = [], []
        for s in range(2):
            mine = (row < HEAD) == (s == 0)
            high, low = split_two(-jnp.sum(inner[s * HEAD : (s + 1) * HEAD], axis=0, keepdims=True))
            zero = jnp.zeros((), bf16)
            shift = jnp.where(row == 0, high, jnp.where(row == 1, low, zero))
            do_e = jnp.concatenate([jnp.where(mine, do_pair, zero), shift], axis=0)
            raised = e_buf[lax.rem(hp, 2), s]
            grad_probs = dot_nn(jnp.concatenate([v_pair, ones], axis=1), do_e)
            grad_scores = (raised.astype(f32) * grad_probs).astype(bf16)
            made = dot_nn(k_turned[s * HEAD : (s + 1) * HEAD], grad_scores)
            dq_ref[pl.ds(pl.multiple_of(hp * PAIR + s * HEAD, HEAD), HEAD), :] = made.astype(bf16)
            slot_scores.append(grad_scores[2 * half_len :])
            slot_raised.append(raised[2 * half_len :])
        dk = dot_nn(jnp.concatenate(slot_scores, axis=0), q_pair)
        dv = dot_nt(jnp.concatenate(slot_raised, axis=0), do_pair)
        gk_ref[:, cols] = jnp.where(low_lane, dk[:BLK], dk[BLK:]).astype(bf16)
        gv_ref[:, cols] = jnp.where(low_lane, dv[:BLK], dv[BLK:]).astype(bf16)

        @pl.when(hp + 2 < pairs)
        def _():
            e_copy(hp + 2).start()

    spot = lax.broadcasted_iota(i32, (1, half_len), 1)
    inside = segment_of(half * half_len + spot, first, second)[1]
    slots = lax.broadcasted_iota(i32, (BLK, 1), 0)
    choose = jnp.where((inside == slots) & (inside < PROMPT), 1.0, 0.0).astype(bf16)
    gq = dot_nt(choose, dq_ref[...]).astype(bf16)
    pulled = dot_nt(gq, wq_ref[...]) + dot_nt(gk_ref[...], wk_ref[...]) + dot_nt(gv_ref[...], wv_ref[...])
    high, low = split_two(acc_ref[...])
    direct = dot_nn(choose, high) + dot_nn(choose, low)
    hidden = prompt_ref[...].astype(f32)
    scale = inv_rms(hidden)
    pulled = gain_first_ref[...] * pulled
    along = jnp.mean(hidden * pulled, axis=-1, keepdims=True)
    grad = direct + scale * pulled - hidden * (scale * scale * scale * along)
    for place in range(BLK // (2 * rows_own)):
        rows = slice(place * rows_own, (place + 1) * rows_own)
        low, high = (grad[(2 * place + c) * rows_own : (2 * place + c + 1) * rows_own] for c in range(2))
        kept_ref[rows, :] = jnp.where(half == 0, low, high)
        cast_ref[rows, :] = jnp.where(half == 0, high, low)
    sent_ref[...] = cast_ref[...].astype(bf16)


def share_kernel(rows_own, kept_ref, came_ref, mine_ref, *refs):
    parts, (total_ref,) = refs[:-1], refs[-1:]
    chip = lax.div(lax.axis_index("dp"), 2)
    total = kept_ref[...] + came_ref[...].astype(f32)
    for place in range(len(parts) + 1):
        total_ref[place] = total[place * rows_own : (place + 1) * rows_own]
    mine_ref[...] = total_ref[chip]
    for n in range(1, len(parts) + 1):
        parts[n - 1][...] = total_ref[chip ^ n].astype(bf16)


def square_kernel(total_ref, *refs):
    parts, (own_ref, square_ref) = refs[:-2], refs[-2:]
    total = total_ref[...]
    for part in parts:
        total = total + part[...].astype(f32)
    few = own_ref.shape[1]
    own = total[:, 0:few]
    for place in range(1, len(parts) + 1):
        own = jnp.where(lax.axis_index("ctx") == place, total[:, place * few : (place + 1) * few], own)
    own_ref[...] = own
    square = jnp.sum(jnp.sum(total * total, axis=1, keepdims=True), axis=0, keepdims=True)
    square_ref[...] = jnp.broadcast_to(square, square_ref.shape)


def update_kernel(max_norm, grad_ref, prompt_ref, first_ref, second_ref, *refs):
    squares, (prompt_out, first_out, second_out) = refs[:-3], refs[-3:]
    square = functools.reduce(jnp.add, [square[0:1, 0:1] for square in squares])
    clipped = grad_ref[...] * (max_norm / jnp.maximum(jnp.sqrt(square), max_norm))
    first_new = beta_first * first_ref[...] + (1.0 - beta_first) * clipped
    second_new = beta_second * second_ref[...] + (1.0 - beta_second) * clipped * clipped
    step = learn_rate * (first_new / first_fix) / (jnp.sqrt(second_new / second_fix) + adam_eps)
    prompt_out[...] = prompt_ref[...] - step
    first_out[...] = first_new
    second_out[...] = second_new


def on_device(
    sizes, tokens, segment_ids, prompt_slots, cotangent, w_query, w_key, w_value, w_output, w_inner, w_outer,
    gain_first, gain_second, bias_table, prompt, first_moment, second_moment,
):
    n_dp, n_ctx = sizes
    count, piece, width = tokens.shape
    half_len = count * piece
    heads = bias_table.shape[1]
    dp, ctx = lax.axis_index("dp"), lax.axis_index("ctx")
    core = lax.rem(dp, 2)

    def permute(value, target):
        pairs = []
        for d in range(n_dp):
            for z in range(n_ctx):
                d2, z2 = target(d, z)
                pairs.append((d * n_ctx + z, d2 * n_ctx + z2))
        return lax.ppermute(value, AXES, pairs)

    def swap_dp(value, bit):
        return permute(value, lambda d, z: (d ^ bit, z))

    def swap_ctx(value, bit):
        return permute(value, lambda d, z: (d, z ^ bit))

    def there(k):
        return lambda d, z: (2 * (d // 2) + z // count, (d % 2) * count + (z + k + 1) % count)

    rows_own, cols_own = prompt.shape
    piece_like = held((piece, width), bf16)
    packed = pl.pallas_call(
        functools.partial(pack_kernel, count),
        out_shape=[piece_like] * count + [held((rows_own + 8, cols_own), bf16)],
        in_specs=[any_spec()] * 3,
        out_specs=[vmem_spec()] * (count + 1),
        scratch_shapes=[
            pltpu.VMEM(segment_ids.shape, i32),
            pltpu.VMEM(prompt.shape, f32),
            pltpu.VMEM((rows_own + 8, cols_own), f32),
            pltpu.SemaphoreType.DMA((count + 2,)),
        ],
        compiler_params=params(4),
        cost_estimate=cost(1e5, 2e6),
    )(in_hbm(tokens), in_hbm(segment_ids), in_hbm(prompt))

    own = [permute(packed[k], there(k)) for k in range(count)]
    chip_rows = jnp.concatenate([packed[count], swap_dp(packed[count], 1)], axis=0)
    chip_parts = [chip_rows] + [swap_dp(chip_rows, 2 * n) for n in range(1, n_dp // 2)]
    plane = pl.pallas_call(
        functools.partial(plane_kernel, rows_own),
        out_shape=held((HELD, cols_own), bf16),
        in_specs=[vmem_spec()] * len(chip_parts),
        out_specs=vmem_spec(),
        scratch_shapes=[pltpu.VMEM((BLK + 16, cols_own), f32)],
        compiler_params=params(4),
        cost_estimate=cost(1e5, 1e5),
    )(*chip_parts)

    choose = (np.arange(bias_table.shape[0])[:, None] == bucket_table(2 * BLK - np.arange(4 * BLK))[None]).astype(np.float32)
    base = lax.dot_general(
        bias_table, jnp.asarray(choose), (((0,), (0,)), ((), ())), precision=lax.Precision.HIGHEST
    )
    base, plane = lax.optimization_barrier((base, plane))
    cols_mine = jnp.concatenate([plane] + [swap_ctx(plane, n) for n in range(1, n_ctx)], axis=0)
    cols_other = swap_dp(cols_mine, 1)
    weights = (w_query, w_key, w_value)
    prepared = pl.pallas_call(
        functools.partial(prepare_kernel, count),
        out_shape=[held((heads, 3, BLK, BLK), f32), held((heads * BLK, 4 * BLK), bf16)]
        + [held((1, width), f32)] * 2
        + [piece_like] * count
        + [held(w.shape, bf16) for w in weights],
        in_specs=[vmem_spec()] * 3 + [any_spec()] * 4,
        out_specs=[vmem_spec()] * (7 + count),
        scratch_shapes=[pltpu.SemaphoreType.DMA((3 + count,))],
        compiler_params=params(4),
        cost_estimate=cost(1e6, 5e6),
    )(base, gain_first[None], gain_second[None], in_hbm(cotangent), *[in_hbm(w) for w in weights])
    tiles, table, gain_1, gain_2 = prepared[:4]
    cot_pieces = prepared[4 : 4 + count]
    w_q, w_k, w_v = prepared[4 + count :]

    keys_all = 2 * half_len + BLK
    hidden_ff = w_inner.shape[1]
    partner = [swap_dp(piece_rows, 1) for piece_rows in own]
    normed = pl.pallas_call(
        functools.partial(first_kernel, count, piece),
        out_shape=held((half_len, width), bf16),
        in_specs=[vmem_spec()] * (count + 1),
        out_specs=vmem_spec(),
        compiler_params=params(A_MIB),
        cost_estimate=cost(1e10, 8e6),
    )(*own, gain_1)
    cots = [permute(cot_pieces[k], there(k)) for k in range(count)]

    made = pl.pallas_call(
        functools.partial(forward_kernel, count, piece, rows_own),
        out_shape=[
            pltpu.HBM((heads // 2, 2, keys_all, half_len), bf16),
            held((8, BLK), i32),
            held((BLK, width), bf16),
            held((half_len, width), bf16),
            held((keys_all, width), bf16),
            held((keys_all, width), bf16),
            held((width, half_len), bf16),
            held((heads, half_len), f32),
            held((half_len, width), f32),
            held((hidden_ff, half_len), bf16),
        ]
        + [held(w.shape, bf16) for w in (w_output, w_inner, w_outer)]
        + [piece_like] * count,
        in_specs=[vmem_spec()] * (2 * count + 10) + [any_spec()] * 3,
        out_specs=[any_spec()] + [vmem_spec()] * (12 + count),
        scratch_shapes=[
            pltpu.VMEM((2 * half_len + BLK, width), bf16),
            pltpu.VMEM((half_len, width), bf16),
            pltpu.VMEM((heads * BLK, half_len), f32),
            pltpu.VMEM((2, keys_all, QCOLS), f32),
            pltpu.VMEM((keys_all, PAIR), bf16),
            pltpu.VMEM((BLK, width), f32),
            pltpu.VMEM((2, 2, keys_all, half_len), bf16),
            pltpu.SemaphoreType.DMA((2,)),
            pltpu.SemaphoreType.DMA((3,)),
        ],
        compiler_params=params(F_MIB),
        cost_estimate=cost(3e10, 4e7, heads * half_len * keys_all),
    )(
        *own, *partner, normed, gain_1, gain_2, w_q, w_k, w_v, tiles, table, cols_mine, cols_other,
        *[in_hbm(w) for w in (w_output, w_inner, w_outer)],
    )
    got = [permute(made[13 + k], back_of(count, k)) for k in range(count)]
    w_o, w_i, w_out = made[10:13]
    e, marks, sent, q, kall, vall, mixed, inv, after, act = made[:10]

    half_rows = n_dp // 2 * rows_own
    kept, leaving = pl.pallas_call(
        functools.partial(backward_kernel, count, piece, rows_own),
        out_shape=[held((half_rows, width), f32), held((half_rows, width), bf16)],
        in_specs=[vmem_spec()] * (count + 17) + [any_spec()],
        out_specs=[vmem_spec()] * 2,
        scratch_shapes=[
            pltpu.VMEM((half_len, width), bf16),
            pltpu.VMEM((half_len, width), f32),
            pltpu.VMEM((half_len, width), bf16),
            pltpu.VMEM((width, half_len), f32),
            pltpu.VMEM((width, half_len), bf16),
            pltpu.VMEM((BLK, width), bf16),
            pltpu.VMEM((BLK, width), bf16),
            pltpu.VMEM((half_rows, width), f32),
            pltpu.VMEM((2, 2, keys_all, half_len), bf16),
            pltpu.SemaphoreType.DMA((2,)),
        ],
        compiler_params=params(B_MIB),
        cost_estimate=cost(3e10, 4e7),
    )(
        *cots, marks, act, after, mixed, inv, q, kall, vall, sent, gain_1, gain_2, w_out, w_i, w_o, w_q, w_k, w_v, in_hbm(e),
    )

    got, leaving = lax.optimization_barrier((got, leaving))
    order = [lax.rem(ctx + j + 1, count) for j in range(count)]
    output = jnp.stack(
        [functools.reduce(lambda a, k: jnp.where(order[k] == r, got[k], a), range(1, count), got[0]) for r in range(count)]
    )

    chips = n_dp // 2
    own_like = held((rows_own, width), f32)
    mine, *parts = pl.pallas_call(
        functools.partial(share_kernel, rows_own),
        out_shape=[own_like] + [held((rows_own, width), bf16)] * (chips - 1),
        in_specs=[vmem_spec()] * 2,
        out_specs=[vmem_spec()] * chips,
        scratch_shapes=[pltpu.VMEM((chips, rows_own, width), f32)],
        compiler_params=params(4),
        cost_estimate=cost(1e5, 1e5),
    )(kept, swap_dp(leaving, 1))
    for n in range(1, chips):
        mine = mine + swap_dp(parts[n - 1], 2 * n).astype(f32)
    line = mine.astype(bf16)
    line_parts = [swap_ctx(line, n) for n in range(1, n_ctx)]
    line_parts, output = lax.optimization_barrier((line_parts, output))
    grad_own, square = pl.pallas_call(
        square_kernel,
        out_shape=[held((rows_own, cols_own), f32), held((8, BLK), f32)],
        in_specs=[vmem_spec()] * n_ctx,
        out_specs=[vmem_spec()] * 2,
        compiler_params=params(4),
        cost_estimate=cost(1e5, 1e5),
    )(mine, *line_parts)
    square = square + swap_dp(square, 1)
    squares = [square] + [swap_dp(square, 2 * n) for n in range(1, chips)]
    own_out = out((rows_own, cols_own), f32)
    prompt_new, first_new, second_new = pl.pallas_call(
        functools.partial(update_kernel, float(0.5 * np.sqrt(np.float32(PROMPT * width)))),
        out_shape=[own_out] * 3,
        in_specs=[vmem_spec()] * (4 + chips),
        out_specs=[vmem_spec()] * 3,
        compiler_params=params(4),
        cost_estimate=cost(1e5, 1e5),
    )(grad_own, prompt, first_moment, second_moment, *squares)
    return (output, prompt_new, first_new, second_new)


def back_of(count, k):
    def target(d, z):
        half, c, r = d % 2, z // count, z % count
        return (2 * (d // 2) + c, half * count + (r - k - 1) % count)

    return target


def solution(mesh):
    rows, cols = P("dp", "ctx", None), P("dp", "ctx")
    placed = (rows, cols, cols, rows) + (P(),) * 9 + (cols,) * 3
    return jax.shard_map(
        functools.partial(on_device, (mesh.shape["dp"], mesh.shape["ctx"])),
        mesh=mesh,
        in_specs=placed,
        out_specs=(rows, cols, cols, cols),
        check_vma=False,
    )
```

```python
import functools

import jax
import jax.numpy as jnp
import numpy as np
from jax import lax
from jax.experimental import pallas as pl
from jax.experimental.pallas import tpu as pltpu
from jax.sharding import PartitionSpec as P

PROMPT = 100
HEAD = 64
PAIR = 2 * HEAD
BLK = 128
SHOWN = 112
HELD = (SHOWN + 16) // 2
QCOLS = 256
UNITS = 1536
norm_eps = 1e-06
beta_first = 0.9
beta_second = 0.999
adam_eps = 1e-08
learn_rate = 0.1
first_fix = 1.0 - 0.9**8
second_fix = 1.0 - 0.999**8
far_marks = (12, 16, 23, 32, 46, 64, 91)
f32 = jnp.float32
bf16 = jnp.bfloat16
i32 = jnp.int32
MASKED = -float(2**30)
AXES = ("dp", "ctx")
MIB = 1 << 20
A_MIB, F_MIB, B_MIB = 6, 20, 18


def bucket_table(offset):
    distance = np.abs(offset)
    passed = sum((distance >= mark).astype(np.int32) for mark in far_marks)
    far_ids = np.minimum(8 + passed, 15)
    return np.where(distance < 8, distance, far_ids) + 16 * (offset > 0).astype(np.int32)


def dot_nn(a, b):
    return lax.dot_general(a, b, (((1,), (0,)), ((), ())), preferred_element_type=f32)


def dot_nt(a, b):
    return lax.dot_general(a, b, (((1,), (1,)), ((), ())), preferred_element_type=f32)


def dot_tn(a, b):
    return lax.dot_general(a, b, (((0,), (0,)), ((), ())), preferred_element_type=f32)


def split_two(values):
    high = values.astype(bf16)
    return high, (values - high.astype(f32)).astype(bf16)


def inv_rms(values):
    return lax.rsqrt(jnp.mean(values * values, axis=-1, keepdims=True) + norm_eps)


def segment_of(place, first, second):
    seg = (place >= first).astype(i32) + (place >= second).astype(i32)
    start = jnp.where(seg == 0, 0, jnp.where(seg == 1, first, second))
    return seg, place - start


def vmem_spec():
    return pl.BlockSpec(memory_space=pltpu.VMEM)


def smem_spec():
    return pl.BlockSpec(memory_space=pltpu.SMEM)


def any_spec():
    return pl.BlockSpec(memory_space=pl.ANY)


def out(shape, dtype):
    return jax.ShapeDtypeStruct(shape, dtype)


def held(shape, dtype):
    return pltpu.VMEM(shape, dtype)


def in_vmem(value):
    return pltpu.with_memory_space_constraint(value, pltpu.VMEM)


def in_hbm(value):
    return pltpu.with_memory_space_constraint(value, pltpu.HBM)


def params(mib):
    return pltpu.CompilerParams(vmem_limit_bytes=mib * MIB)


def cost(flops, nbytes, trans=0):
    return pl.CostEstimate(flops=int(flops), bytes_accessed=int(nbytes), transcendentals=int(trans))


def pick_piece(pieces, turn, j):
    count = len(pieces)
    place = lax.rem(turn - j - 1 + count, count)
    picked = pieces[0][...]
    for k in range(1, count):
        picked = jnp.where(place == k, pieces[k][...], picked)
    return picked


def slot_of(index, count):
    return lax.rem(index + 2 * count, count)


def pack_kernel(count, tokens_ref, seg_hbm, prompt_hbm, *refs):
    pieces, (block_ref, seg_ref, prompt_ref, wide_ref, sems) = refs[:count], refs[count:]
    ctx = lax.axis_index("ctx")
    copies = [
        pltpu.make_async_copy(tokens_ref.at[slot_of(ctx + k + 1, count)], pieces[k], sems.at[k]) for k in range(count)
    ]
    small = [
        pltpu.make_async_copy(seg_hbm, seg_ref, sems.at[count]),
        pltpu.make_async_copy(prompt_hbm, prompt_ref, sems.at[count + 1]),
    ]
    for copy in small + copies:
        copy.start()
    for copy in small:
        copy.wait()
    rows = prompt_ref.shape[0]
    wide_ref[...] = jnp.zeros_like(wide_ref)
    wide_ref[0:rows, :] = prompt_ref[...]
    for n in range(2):
        tally = jnp.sum((seg_ref[...] <= n).astype(f32), axis=1, keepdims=True)
        wide_ref[rows + n * count : rows + (n + 1) * count, :] = jnp.broadcast_to(tally, (count, prompt_ref.shape[1]))
    block_ref[...] = wide_ref[...].astype(bf16)
    for copy in copies:
        copy.wait()


def prepare_kernel(count, base_ref, gain_first_ref, gain_second_ref, cot_ref, *refs):
    weights, (tile_ref, table_ref, first_ref, second_ref) = refs[:3], refs[3:7]
    pieces, kept, sems = refs[7 : 7 + count], refs[7 + count : 10 + count], refs[10 + count]
    first_ref[...] = gain_first_ref[...]
    second_ref[...] = gain_second_ref[...]
    ctx = lax.axis_index("ctx")
    copies = [pltpu.make_async_copy(weights[n], kept[n], sems.at[n]) for n in range(3)] + [
        pltpu.make_async_copy(cot_ref.at[slot_of(ctx + k + 1, count)], pieces[k], sems.at[3 + k]) for k in range(count)
    ]
    for copy in copies:
        copy.start()
    heads = tile_ref.shape[0]
    for h in range(heads):
        row = jnp.broadcast_to(base_ref[h : h + 1, :], (BLK, 4 * BLK))
        spread = pltpu.roll(row, 0, 1, stride=1, stride_axis=0)
        low, mid, top = (spread[:, k * BLK : (k + 1) * BLK] for k in (3, 2, 1))
        tile_ref[h, 0] = low
        tile_ref[h, 1] = mid
        tile_ref[h, 2] = top
        rows = slice(h * BLK, (h + 1) * BLK)
        parts = [part for pair in zip(split_two(mid), split_two(low)) for part in pair]
        for k in range(4):
            table_ref[rows, k * BLK : (k + 1) * BLK] = parts[k]
    for copy in copies:
        copy.wait()


def plane_kernel(rows_own, *refs):
    parts, (out_ref, wide_ref) = refs[:-2], refs[-2:]
    core, chip = lax.rem(lax.axis_index("dp"), 2), lax.div(lax.axis_index("dp"), 2)
    high = rows_own + 8
    parts = [part[...].astype(f32) for part in parts]
    parts = [[jnp.where(core == c, part[:high], part[high:]) for c in range(2)] for part in parts]
    for place in range(len(parts)):
        for c in range(2):
            picked = parts[0][c]
            for n in range(1, len(parts)):
                picked = jnp.where((chip ^ n) == place, parts[n][c], picked)
            start = (2 * place + c) * rows_own
            wide_ref[start : start + rows_own, :] = picked[:rows_own]
    for c in range(2):
        wide_ref[SHOWN + 8 * c : SHOWN + 8 * (c + 1), :] = parts[0][c][rows_own:]
    out_ref[...] = jnp.where(core == 0, wide_ref[0:HELD, :], wide_ref[HELD : 2 * HELD, :]).astype(bf16)


def places(count):
    return lax.rem(lax.axis_index("dp"), 2), lax.rem(lax.axis_index("ctx"), count)


def first_kernel(count, piece, *refs):
    own, (gain_ref, norm_ref) = refs[:count], refs[count:]
    turn = places(count)[1]
    for j in range(count):
        tok = pick_piece(own, turn, j).astype(f32)
        norm_ref[j * piece : (j + 1) * piece, :] = (tok * inv_rms(tok) * gain_ref[...]).astype(bf16)


def forward_kernel(count, piece, rows_own, *refs):
    own, partner = refs[:count], refs[count : 2 * count]
    (
        normed_ref, gain_first_ref, gain_second_ref, wq_ref, wk_ref, wv_ref, tile_ref, table_ref,
    ) = refs[2 * count : 2 * count + 8]
    refs = refs[2 * count + 8 :]
    (mine_ref, other_ref), later, refs = refs[:2], refs[2:5], refs[5:]
    e_ref, marks_ref, prompt_ref, q_ref, kall_ref, vall_ref, mixed_ref, inv_ref, after_ref, act_ref = refs[:10]
    kept, refs = refs[10:13], refs[13:]
    wo_ref, wi_ref, wout_ref = kept
    going, refs = refs[:count], refs[count:]
    norm_ref, hid_ref, slot_bias_ref, score_ref, aug_ref, shown_ref, e_buf, sems, weight_sems = refs
    fetches = [pltpu.make_async_copy(later[n], kept[n], weight_sems.at[n]) for n in range(3)]
    for fetch in fetches:
        fetch.start()
    ctx = lax.axis_index("ctx")
    half, turn = places(count)
    few = mine_ref.shape[1]
    low = jnp.where(half == 0, mine_ref[...], other_ref[...]).astype(f32)
    high = jnp.where(half == 0, other_ref[...], mine_ref[...]).astype(f32)
    for place in range(2 * count):
        for part, start, stop in ((low, 0, HELD), (high, HELD, SHOWN)):
            picked = part[0 : stop - start]
            for n in range(1, 2 * count):
                picked = jnp.where((ctx ^ n) == place, part[n * HELD : n * HELD + stop - start], picked)
            shown_ref[start:stop, place * few : (place + 1) * few] = picked
    shown_ref[SHOWN:, :] = jnp.zeros((BLK - SHOWN, shown_ref.shape[1]), f32)
    prompt_ref[...] = shown_ref[...].astype(bf16)
    half_len = count * piece
    width = q_ref.shape[1]
    tally = functools.reduce(jnp.add, [high[(n + 1) * HELD - 16 : (n + 1) * HELD] for n in range(2 * count)])
    tally_row = lax.broadcasted_iota(i32, (tally.shape[0], 1), 0)
    marks = []
    for n in range(2):
        here = tally_row == 8 * lax.div(ctx, count) + n * count + turn
        total = jnp.sum(jnp.where(here, tally, 0.0), axis=0, keepdims=True)[:, 0:1]
        marks.append((total + 0.5).astype(i32))
        marks_ref[n : n + 1, :] = jnp.broadcast_to(marks[n], (1, BLK))
    first, second = marks
    gain = gain_first_ref[...]
    slots = lax.broadcasted_iota(i32, (1, BLK), 1)
    for j in range(count):
        rows = slice(j * piece, (j + 1) * piece)
        place = half * half_len + j * piece + lax.broadcasted_iota(i32, (piece, 1), 0)
        inside = segment_of(place, first, second)[1]
        shown = inside < PROMPT
        choose = jnp.where((inside == slots) & shown, 1.0, 0.0).astype(bf16)
        picked = dot_nn(choose, prompt_ref[...])
        hidden = jnp.where(shown, picked, pick_piece(own, turn, j).astype(f32))
        hid_ref[rows, :] = hidden.astype(bf16)
        norm_ref[half_len + BLK + j * piece : half_len + BLK + (j + 1) * piece, :] = (
            hidden * inv_rms(hidden) * gain
        ).astype(bf16)
        tok = pick_piece(partner, turn, j).astype(f32)
        norm_ref[rows, :] = (tok * inv_rms(tok) * gain).astype(bf16)
    hidden = prompt_ref[...].astype(f32)
    norm_ref[half_len : half_len + BLK, :] = (hidden * inv_rms(hidden) * gain).astype(bf16)
    wide = 2 * BLK
    for t in range(width // wide):
        cols = slice(t * wide, (t + 1) * wide)
        normed = jnp.concatenate([normed_ref[...], norm_ref[0 : half_len + BLK, :]], axis=0)
        kall_ref[:, cols] = dot_nn(normed, wk_ref[:, cols]).astype(bf16)
        vall_ref[:, cols] = dot_nn(normed, wv_ref[:, cols]).astype(bf16)
        q_ref[:, cols] = dot_nn(norm_ref[half_len + BLK :, :], wq_ref[:, cols]).astype(bf16)

    lane = lax.broadcasted_iota(i32, (1, PAIR), 1)
    low_lane = lane < HEAD
    lane_seg = lane
    spot = lax.broadcasted_iota(i32, (half_len, 1), 0)
    own_seg, own_inside = segment_of(half * half_len + spot, first, second)
    par_seg, par_inside = segment_of((1 - half) * half_len + spot, first, second)
    q_aug = jnp.where(own_seg == lane_seg, 1.0, 0.0).astype(bf16)

    def key_aug(seg, inside):
        closed = ((seg != lane_seg) | (inside < PROMPT)) & (lane_seg < 3)
        return jnp.where(closed, MASKED, 0.0).astype(bf16)

    slot = lax.broadcasted_iota(i32, (BLK, 1), 0)
    aug_ref[0:half_len] = key_aug(own_seg, own_inside)
    aug_ref[half_len : 2 * half_len] = key_aug(par_seg, par_inside)
    aug_ref[2 * half_len :] = jnp.where((slot >= PROMPT) & (lane_seg < 3), MASKED, 0.0).astype(bf16)
    across = segment_of(half * half_len + lax.broadcasted_iota(i32, (1, half_len), 1), first, second)[1]
    far = lax.rem(lax.broadcasted_iota(i32, (4 * BLK, 1), 0), 2 * BLK)
    spread = jnp.where(jnp.minimum(across, 2 * BLK - 1) == far, 1.0, 0.0).astype(bf16)
    slot_bias_ref[...] = dot_nn(table_ref[...], spread)
    blocks = half_len // BLK
    ones = jnp.ones((16, 2 * half_len + BLK), bf16)

    def e_copy(hp):
        at = lax.rem(hp, 2)
        return pltpu.make_async_copy(e_buf.at[at], e_ref.at[hp], sems.at[at])

    keys_all = 2 * half_len + BLK
    tiles_q = half_len // QCOLS
    chunk = keys_all // 3
    units = [(s, qt) for s in range(2) for qt in range(tiles_q)]

    def kept(s):
        return low_lane if s == 0 else jnp.logical_not(low_lane)

    def score_steps(hp, s, qt, slot):
        cols = pl.ds(pl.multiple_of(hp * PAIR, PAIR), PAIR)
        here = slice(qt * QCOLS, (qt + 1) * QCOLS)
        q_e = jnp.concatenate([jnp.where(kept(s), q_ref[here, cols], jnp.zeros((), bf16)), q_aug[here]], axis=1)

        def step(n):
            rows = slice(n * chunk, (n + 1) * chunk)
            score_ref[slot, rows, :] = dot_nt(jnp.concatenate([kall_ref[rows, cols], aug_ref[rows]], axis=1), q_e)

        return [functools.partial(step, n) for n in range(3)]

    for step in score_steps(0, 0, 0, 0):
        step()

    @pl.loop(0, width // PAIR)
    def _(hp):
        @pl.when(hp >= 2)
        def _():
            e_copy(hp - 2).wait()

        cols = pl.ds(pl.multiple_of(hp * PAIR, PAIR), PAIR)
        v_turned = vall_ref[:, cols].T
        for u, (s, qt) in enumerate(units):
            h = 2 * hp + s
            coming = units[(u + 1) % len(units)]
            at = hp if u + 1 < len(units) else jnp.minimum(hp + 1, width // PAIR - 1)
            steps = score_steps(at, *coming, (u + 1) % 2)
            back_far, ahead_far = tile_ref[h, 0, 0:1, BLK - 1 :], tile_ref[h, 2, BLK - 1 :, 0:1]
            other_far = jnp.where(half == 0, ahead_far, back_far)
            values = (back_far, ahead_far, other_far)
            columns = []
            for sub in range(QCOLS // BLK):
                qb = qt * (QCOLS // BLK) + sub
                here = slice(sub * BLK, (sub + 1) * BLK)

                def part_of(kb):
                    part = score_ref[u % 2, kb * BLK : (kb + 1) * BLK, here]
                    if kb == 2 * blocks:
                        slot_rows = pl.ds(pl.multiple_of(h * BLK, BLK), BLK)
                        return part + slot_bias_ref[slot_rows, qb * BLK : (qb + 1) * BLK], None
                    gap = kb - qb
                    if kb < blocks and abs(gap) <= 1:
                        return part + tile_ref[h, gap + 1], None
                    if kb < blocks:
                        return part, 0 if gap < 0 else 1
                    if qb == blocks - 1 and kb == blocks:
                        return part + jnp.where(half == 0, tile_ref[h, 2], back_far), None
                    if qb == 0 and kb == 2 * blocks - 1:
                        return part + jnp.where(half == 0, ahead_far, tile_ref[h, 0]), None
                    return part, 2

                tops, group = {}, {}
                for kb in range(2 * blocks + 1):
                    part, const = part_of(kb)
                    if const is None:
                        score_ref[u % 2, kb * BLK : (kb + 1) * BLK, here] = part
                    group[kb] = const
                    top = jnp.max(part.reshape(BLK // 8, 8, BLK), axis=0)
                    tops[const] = top if const not in tops else jnp.maximum(tops[const], top)
                    if steps and kb == 4:
                        steps.pop(0)()
                peak = functools.reduce(
                    jnp.maximum, [top if const is None else top + values[const] for const, top in tops.items()]
                )
                peak = jnp.max(peak, axis=0, keepdims=True)
                shifts = [peak - value for value in values]
                column = []
                for kb in range(2 * blocks + 1):
                    part = score_ref[u % 2, kb * BLK : (kb + 1) * BLK, here]
                    shift = peak if group[kb] is None else shifts[group[kb]]
                    column.append(jnp.exp(part - shift).astype(bf16))
                    if steps and kb == 4:
                        steps.pop(0)()
                columns.append(jnp.concatenate(column, axis=0))
            for step in steps:
                step()
            raised = jnp.concatenate(columns, axis=1)
            qcols = slice(qt * QCOLS, (qt + 1) * QCOLS)
            e_buf[lax.rem(hp, 2), s, :, qcols] = raised
            total = dot_nn(jnp.concatenate([v_turned[s * HEAD : (s + 1) * HEAD], ones], axis=0), raised)
            inv = 1.0 / total[HEAD : HEAD + 1]
            inv_ref[pl.ds(h, 1), qcols] = inv
            mixed_ref[pl.ds(pl.multiple_of(h * HEAD, HEAD), HEAD), qcols] = (total[:HEAD] * inv).astype(bf16)
        e_copy(hp).start()

    for fetch in fetches:
        fetch.wait()
    after_ref[...] = dot_tn(mixed_ref[...], wo_ref[...])

    for t in range(half_len // BLK):
        rows = slice(t * BLK, (t + 1) * BLK)
        after = hid_ref[rows, :].astype(f32) + after_ref[rows, :]
        after_ref[rows, :] = after
        norm_ref[rows, :] = (after * inv_rms(after) * gain_second_ref[...]).astype(bf16)

    @pl.loop(0, wi_ref.shape[1] // UNITS)
    def _(t):
        units = pl.ds(pl.multiple_of(t * UNITS, UNITS), UNITS)
        inner = lax.dot_general(
            wi_ref[:, units], norm_ref[0:half_len, :], (((0,), (1,)), ((), ())), preferred_element_type=f32
        )
        act_ref[units, :] = jnp.maximum(inner, 0.0).astype(bf16)

    made = (after_ref[...] + dot_tn(act_ref[...], wout_ref[...])).astype(bf16)
    made = [made[j * piece : (j + 1) * piece] for j in range(count)]
    for k in range(count):
        place = slot_of(turn - k - 1, count)
        sent = made[0]
        for j in range(1, count):
            sent = jnp.where(place == j, made[j], sent)
        going[k][...] = sent

    for hp in range(width // PAIR - 2, width // PAIR):
        e_copy(hp).wait()


def backward_kernel(count, piece, rows_own, *refs):
    cots = refs[:count]
    (
        marks_ref, act_ref, after_ref, mixed_ref, inv_ref, q_ref, kall_ref, vall_ref, prompt_ref, gain_first_ref, gain_second_ref,
        wout_ref, wi_ref, wo_ref, wq_ref, wk_ref, wv_ref, e_ref,
        kept_ref, sent_ref,
        cot_ref, acc_ref, low_ref, do_ref, dq_ref, gk_ref, gv_ref, cast_ref, e_buf, sems,
    ) = refs[count:]
    half, turn = places(count)
    first, second = marks_ref[0:1, 0:1], marks_ref[1:2, 0:1]
    half_len = count * piece
    width = q_ref.shape[1]
    pairs = width // PAIR

    def e_copy(hp):
        at = lax.rem(hp, 2)
        return pltpu.make_async_copy(e_ref.at[hp], e_buf.at[at], sems.at[at])

    for hp in range(2):
        e_copy(hp).start()
    for j in range(count):
        cot_ref[j * piece : (j + 1) * piece, :] = pick_piece(cots, turn, j)
    do_ref[...] = jnp.zeros_like(do_ref)

    for t in range(wi_ref.shape[1] // UNITS):
        units = slice(t * UNITS, (t + 1) * UNITS)
        grad_act = dot_nt(wout_ref[units, :], cot_ref[...])
        grad_inner = jnp.where(act_ref[units, :] > 0, grad_act, 0.0).astype(bf16)
        do_ref[...] += dot_nn(wi_ref[:, units], grad_inner)

    acc_ref[...] = do_ref[...].T
    gain = gain_second_ref[...]

    for t in range(half_len // BLK):
        rows = slice(t * BLK, (t + 1) * BLK)
        after = after_ref[rows, :]
        scale = inv_rms(after)
        pulled = gain * acc_ref[rows, :]
        along = jnp.mean(after * pulled, axis=-1, keepdims=True)
        grad_after = cot_ref[rows, :].astype(f32) + scale * pulled - after * (scale * scale * scale * along)
        acc_ref[rows, :] = grad_after
        low_ref[rows, :] = grad_after.astype(bf16)

    do_ref[...] = dot_nt(wo_ref[...], low_ref[...])

    low_lane = lax.broadcasted_iota(i32, (1, PAIR), 1) < HEAD
    row = lax.broadcasted_iota(i32, (PAIR, 1), 0)
    ones = jnp.ones((2 * half_len + BLK, PAIR), bf16)

    @pl.loop(0, pairs)
    def _(hp):
        e_copy(hp).wait()
        cols = pl.ds(pl.multiple_of(hp * PAIR, PAIR), PAIR)
        q_pair, k_turned, v_pair = q_ref[:, cols], kall_ref[:, cols].T, vall_ref[:, cols]
        inv_both = jnp.where(row < HEAD, inv_ref[pl.ds(2 * hp, 1), :], inv_ref[pl.ds(2 * hp + 1, 1), :])
        do_pair = (do_ref[cols, :] * inv_both).astype(bf16)
        inner = do_pair.astype(f32) * mixed_ref[cols, :].astype(f32)
        slot_scores, slot_raised = [], []
        for s in range(2):
            mine = (row < HEAD) == (s == 0)
            high, low = split_two(-jnp.sum(inner[s * HEAD : (s + 1) * HEAD], axis=0, keepdims=True))
            zero = jnp.zeros((), bf16)
            shift = jnp.where(row == 0, high, jnp.where(row == 1, low, zero))
            do_e = jnp.concatenate([jnp.where(mine, do_pair, zero), shift], axis=0)
            raised = e_buf[lax.rem(hp, 2), s]
            grad_probs = dot_nn(jnp.concatenate([v_pair, ones], axis=1), do_e)
            grad_scores = (raised.astype(f32) * grad_probs).astype(bf16)
            made = dot_nn(k_turned[s * HEAD : (s + 1) * HEAD], grad_scores)
            dq_ref[pl.ds(pl.multiple_of(hp * PAIR + s * HEAD, HEAD), HEAD), :] = made.astype(bf16)
            slot_scores.append(grad_scores[2 * half_len :])
            slot_raised.append(raised[2 * half_len :])
        dk = dot_nn(jnp.concatenate(slot_scores, axis=0), q_pair)
        dv = dot_nt(jnp.concatenate(slot_raised, axis=0), do_pair)
        gk_ref[:, cols] = jnp.where(low_lane, dk[:BLK], dk[BLK:]).astype(bf16)
        gv_ref[:, cols] = jnp.where(low_lane, dv[:BLK], dv[BLK:]).astype(bf16)

        @pl.when(hp + 2 < pairs)
        def _():
            e_copy(hp + 2).start()

    spot = lax.broadcasted_iota(i32, (1, half_len), 1)
    inside = segment_of(half * half_len + spot, first, second)[1]
    slots = lax.broadcasted_iota(i32, (BLK, 1), 0)
    choose = jnp.where((inside == slots) & (inside < PROMPT), 1.0, 0.0).astype(bf16)
    gq = dot_nt(choose, dq_ref[...]).astype(bf16)
    pulled = dot_nt(gq, wq_ref[...]) + dot_nt(gk_ref[...], wk_ref[...]) + dot_nt(gv_ref[...], wv_ref[...])
    high, low = split_two(acc_ref[...])
    direct = dot_nn(choose, high) + dot_nn(choose, low)
    hidden = prompt_ref[...].astype(f32)
    scale = inv_rms(hidden)
    pulled = gain_first_ref[...] * pulled
    along = jnp.mean(hidden * pulled, axis=-1, keepdims=True)
    grad = direct + scale * pulled - hidden * (scale * scale * scale * along)
    for place in range(BLK // (2 * rows_own)):
        rows = slice(place * rows_own, (place + 1) * rows_own)
        low, high = (grad[(2 * place + c) * rows_own : (2 * place + c + 1) * rows_own] for c in range(2))
        kept_ref[rows, :] = jnp.where(half == 0, low, high)
        cast_ref[rows, :] = jnp.where(half == 0, high, low)
    sent_ref[...] = cast_ref[...].astype(bf16)


def share_kernel(rows_own, kept_ref, came_ref, mine_ref, *refs):
    parts, (total_ref,) = refs[:-1], refs[-1:]
    chip = lax.div(lax.axis_index("dp"), 2)
    total = kept_ref[...] + came_ref[...].astype(f32)
    for place in range(len(parts) + 1):
        total_ref[place] = total[place * rows_own : (place + 1) * rows_own]
    mine_ref[...] = total_ref[chip]
    for n in range(1, len(parts) + 1):
        parts[n - 1][...] = total_ref[chip ^ n].astype(bf16)


def square_kernel(total_ref, *refs):
    parts, (own_ref, square_ref) = refs[:-2], refs[-2:]
    total = total_ref[...]
    for part in parts:
        total = total + part[...].astype(f32)
    few = own_ref.shape[1]
    own = total[:, 0:few]
    for place in range(1, len(parts) + 1):
        own = jnp.where(lax.axis_index("ctx") == place, total[:, place * few : (place + 1) * few], own)
    own_ref[...] = own
    square = jnp.sum(jnp.sum(total * total, axis=1, keepdims=True), axis=0, keepdims=True)
    square_ref[...] = jnp.broadcast_to(square, square_ref.shape)


def update_kernel(max_norm, grad_ref, prompt_ref, first_ref, second_ref, *refs):
    squares, (prompt_out, first_out, second_out) = refs[:-3], refs[-3:]
    square = functools.reduce(jnp.add, [square[0:1, 0:1] for square in squares])
    clipped = grad_ref[...] * (max_norm / jnp.maximum(jnp.sqrt(square), max_norm))
    first_new = beta_first * first_ref[...] + (1.0 - beta_first) * clipped
    second_new = beta_second * second_ref[...] + (1.0 - beta_second) * clipped * clipped
    step = learn_rate * (first_new / first_fix) / (jnp.sqrt(second_new / second_fix) + adam_eps)
    prompt_out[...] = prompt_ref[...] - step
    first_out[...] = first_new
    second_out[...] = second_new


def on_device(
    sizes, tokens, segment_ids, prompt_slots, cotangent, w_query, w_key, w_value, w_output, w_inner, w_outer,
    gain_first, gain_second, bias_table, prompt, first_moment, second_moment,
):
    n_dp, n_ctx = sizes
    count, piece, width = tokens.shape
    half_len = count * piece
    heads = bias_table.shape[1]
    dp, ctx = lax.axis_index("dp"), lax.axis_index("ctx")
    core = lax.rem(dp, 2)

    def permute(value, target):
        pairs = []
        for d in range(n_dp):
            for z in range(n_ctx):
                d2, z2 = target(d, z)
                pairs.append((d * n_ctx + z, d2 * n_ctx + z2))
        return lax.ppermute(value, AXES, pairs)

    def swap_dp(value, bit):
        return permute(value, lambda d, z: (d ^ bit, z))

    def swap_ctx(value, bit):
        return permute(value, lambda d, z: (d, z ^ bit))

    def there(k):
        return lambda d, z: (2 * (d // 2) + z // count, (d % 2) * count + (z + k + 1) % count)

    rows_own, cols_own = prompt.shape
    piece_like = held((piece, width), bf16)
    packed = pl.pallas_call(
        functools.partial(pack_kernel, count),
        out_shape=[piece_like] * count + [held((rows_own + 8, cols_own), bf16)],
        in_specs=[any_spec()] * 3,
        out_specs=[vmem_spec()] * (count + 1),
        scratch_shapes=[
            pltpu.VMEM(segment_ids.shape, i32),
            pltpu.VMEM(prompt.shape, f32),
            pltpu.VMEM((rows_own + 8, cols_own), f32),
            pltpu.SemaphoreType.DMA((count + 2,)),
        ],
        compiler_params=params(4),
        cost_estimate=cost(1e5, 2e6),
    )(in_hbm(tokens), in_hbm(segment_ids), in_hbm(prompt))

    own = [permute(packed[k], there(k)) for k in range(count)]
    chip_rows = jnp.concatenate([packed[count], swap_dp(packed[count], 1)], axis=0)
    chip_parts = [chip_rows] + [swap_dp(chip_rows, 2 * n) for n in range(1, n_dp // 2)]
    plane = pl.pallas_call(
        functools.partial(plane_kernel, rows_own),
        out_shape=held((HELD, cols_own), bf16),
        in_specs=[vmem_spec()] * len(chip_parts),
        out_specs=vmem_spec(),
        scratch_shapes=[pltpu.VMEM((BLK + 16, cols_own), f32)],
        compiler_params=params(4),
        cost_estimate=cost(1e5, 1e5),
    )(*chip_parts)

    choose = (np.arange(bias_table.shape[0])[:, None] == bucket_table(2 * BLK - np.arange(4 * BLK))[None]).astype(np.float32)
    base = lax.dot_general(
        bias_table, jnp.asarray(choose), (((0,), (0,)), ((), ())), precision=lax.Precision.HIGHEST
    )
    base, plane = lax.optimization_barrier((base, plane))
    cols_mine = jnp.concatenate([plane] + [swap_ctx(plane, n) for n in range(1, n_ctx)], axis=0)
    cols_other = swap_dp(cols_mine, 1)
    weights = (w_query, w_key, w_value)
    prepared = pl.pallas_call(
        functools.partial(prepare_kernel, count),
        out_shape=[held((heads, 3, BLK, BLK), f32), held((heads * BLK, 4 * BLK), bf16)]
        + [held((1, width), f32)] * 2
        + [piece_like] * count
        + [held(w.shape, bf16) for w in weights],
        in_specs=[vmem_spec()] * 3 + [any_spec()] * 4,
        out_specs=[vmem_spec()] * (7 + count),
        scratch_shapes=[pltpu.SemaphoreType.DMA((3 + count,))],
        compiler_params=params(4),
        cost_estimate=cost(1e6, 5e6),
    )(base, gain_first[None], gain_second[None], in_hbm(cotangent), *[in_hbm(w) for w in weights])
    tiles, table, gain_1, gain_2 = prepared[:4]
    cot_pieces = prepared[4 : 4 + count]
    w_q, w_k, w_v = prepared[4 + count :]

    keys_all = 2 * half_len + BLK
    hidden_ff = w_inner.shape[1]
    partner = [swap_dp(piece_rows, 1) for piece_rows in own]
    normed = pl.pallas_call(
        functools.partial(first_kernel, count, piece),
        out_shape=held((half_len, width), bf16),
        in_specs=[vmem_spec()] * (count + 1),
        out_specs=vmem_spec(),
        compiler_params=params(A_MIB),
        cost_estimate=cost(1e10, 8e6),
    )(*own, gain_1)
    cots = [permute(cot_pieces[k], there(k)) for k in range(count)]

    made = pl.pallas_call(
        functools.partial(forward_kernel, count, piece, rows_own),
        out_shape=[
            pltpu.HBM((heads // 2, 2, keys_all, half_len), bf16),
            held((8, BLK), i32),
            held((BLK, width), bf16),
            held((half_len, width), bf16),
            held((keys_all, width), bf16),
            held((keys_all, width), bf16),
            held((width, half_len), bf16),
            held((heads, half_len), f32),
            held((half_len, width), f32),
            held((hidden_ff, half_len), bf16),
        ]
        + [held(w.shape, bf16) for w in (w_output, w_inner, w_outer)]
        + [piece_like] * count,
        in_specs=[vmem_spec()] * (2 * count + 10) + [any_spec()] * 3,
        out_specs=[any_spec()] + [vmem_spec()] * (12 + count),
        scratch_shapes=[
            pltpu.VMEM((2 * half_len + BLK, width), bf16),
            pltpu.VMEM((half_len, width), bf16),
            pltpu.VMEM((heads * BLK, half_len), f32),
            pltpu.VMEM((2, keys_all, QCOLS), f32),
            pltpu.VMEM((keys_all, PAIR), bf16),
            pltpu.VMEM((BLK, width), f32),
            pltpu.VMEM((2, 2, keys_all, half_len), bf16),
            pltpu.SemaphoreType.DMA((2,)),
            pltpu.SemaphoreType.DMA((3,)),
        ],
        compiler_params=params(F_MIB),
        cost_estimate=cost(3e10, 4e7, heads * half_len * keys_all),
    )(
        *own, *partner, normed, gain_1, gain_2, w_q, w_k, w_v, tiles, table, cols_mine, cols_other,
        *[in_hbm(w) for w in (w_output, w_inner, w_outer)],
    )
    got = [permute(made[13 + k], back_of(count, k)) for k in range(count)]
    w_o, w_i, w_out = made[10:13]
    e, marks, sent, q, kall, vall, mixed, inv, after, act = made[:10]

    half_rows = n_dp // 2 * rows_own
    kept, leaving = pl.pallas_call(
        functools.partial(backward_kernel, count, piece, rows_own),
        out_shape=[held((half_rows, width), f32), held((half_rows, width), bf16)],
        in_specs=[vmem_spec()] * (count + 17) + [any_spec()],
        out_specs=[vmem_spec()] * 2,
        scratch_shapes=[
            pltpu.VMEM((half_len, width), bf16),
            pltpu.VMEM((half_len, width), f32),
            pltpu.VMEM((half_len, width), bf16),
            pltpu.VMEM((width, half_len), f32),
            pltpu.VMEM((width, half_len), bf16),
            pltpu.VMEM((BLK, width), bf16),
            pltpu.VMEM((BLK, width), bf16),
            pltpu.VMEM((half_rows, width), f32),
            pltpu.VMEM((2, 2, keys_all, half_len), bf16),
            pltpu.SemaphoreType.DMA((2,)),
        ],
        compiler_params=params(B_MIB),
        cost_estimate=cost(3e10, 4e7),
    )(
        *cots, marks, act, after, mixed, inv, q, kall, vall, sent, gain_1, gain_2, w_out, w_i, w_o, w_q, w_k, w_v, in_hbm(e),
    )

    got, leaving = lax.optimization_barrier((got, leaving))
    order = [lax.rem(ctx + j + 1, count) for j in range(count)]
    output = jnp.stack(
        [functools.reduce(lambda a, k: jnp.where(order[k] == r, got[k], a), range(1, count), got[0]) for r in range(count)]
    )

    chips = n_dp // 2
    own_like = held((rows_own, width), f32)
    mine, *parts = pl.pallas_call(
        functools.partial(share_kernel, rows_own),
        out_shape=[own_like] + [held((rows_own, width), bf16)] * (chips - 1),
        in_specs=[vmem_spec()] * 2,
        out_specs=[vmem_spec()] * chips,
        scratch_shapes=[pltpu.VMEM((chips, rows_own, width), f32)],
        compiler_params=params(4),
        cost_estimate=cost(1e5, 1e5),
    )(kept, swap_dp(leaving, 1))
    for n in range(1, chips):
        mine = mine + swap_dp(parts[n - 1], 2 * n).astype(f32)
    line = mine.astype(bf16)
    line_parts = [swap_ctx(line, n) for n in range(1, n_ctx)]
    line_parts, output = lax.optimization_barrier((line_parts, output))
    grad_own, square = pl.pallas_call(
        square_kernel,
        out_shape=[held((rows_own, cols_own), f32), held((8, BLK), f32)],
        in_specs=[vmem_spec()] * n_ctx,
        out_specs=[vmem_spec()] * 2,
        compiler_params=params(4),
        cost_estimate=cost(1e5, 1e5),
    )(mine, *line_parts)
    square = square + swap_dp(square, 1)
    squares = [square] + [swap_dp(square, 2 * n) for n in range(1, chips)]
    own_out = out((rows_own, cols_own), f32)
    prompt_new, first_new, second_new = pl.pallas_call(
        functools.partial(update_kernel, float(0.5 * np.sqrt(np.float32(PROMPT * width)))),
        out_shape=[own_out] * 3,
        in_specs=[vmem_spec()] * (4 + chips),
        out_specs=[vmem_spec()] * 3,
        compiler_params=params(4),
        cost_estimate=cost(1e5, 1e5),
    )(grad_own, prompt, first_moment, second_moment, *squares)
    return (output, prompt_new, first_new, second_new)


def back_of(count, k):
    def target(d, z):
        half, c, r = d % 2, z // count, z % count
        return (2 * (d // 2) + c, half * count + (r - k - 1) % count)

    return target


def solution(mesh):
    rows, cols = P("dp", "ctx", None), P("dp", "ctx")
    placed = (rows, cols, cols, rows) + (P(),) * 9 + (cols,) * 3
    return jax.shard_map(
        functools.partial(on_device, (mesh.shape["dp"], mesh.shape["ctx"])),
        mesh=mesh,
        in_specs=placed,
        out_specs=(rows, cols, cols, cols),
        check_vma=False,
    )
```

```python
import functools

import jax
import jax.numpy as jnp
import numpy as np
from jax import lax
from jax.experimental import pallas as pl
from jax.experimental.pallas import tpu as pltpu
from jax.sharding import PartitionSpec as P

PROMPT = 100
HEAD = 64
PAIR = 2 * HEAD
BLK = 128
SHOWN = 112
HELD = (SHOWN + 16) // 2
QCOLS = 256
UNITS = 1536
norm_eps = 1e-06
beta_first = 0.9
beta_second = 0.999
adam_eps = 1e-08
learn_rate = 0.1
first_fix = 1.0 - 0.9**8
second_fix = 1.0 - 0.999**8
far_marks = (12, 16, 23, 32, 46, 64, 91)
f32 = jnp.float32
bf16 = jnp.bfloat16
i32 = jnp.int32
MASKED = -float(2**30)
AXES = ("dp", "ctx")
MIB = 1 << 20
A_MIB, F_MIB, B_MIB = 6, 20, 18


def bucket_table(offset):
    distance = np.abs(offset)
    passed = sum((distance >= mark).astype(np.int32) for mark in far_marks)
    far_ids = np.minimum(8 + passed, 15)
    return np.where(distance < 8, distance, far_ids) + 16 * (offset > 0).astype(np.int32)


def dot_nn(a, b):
    return lax.dot_general(a, b, (((1,), (0,)), ((), ())), preferred_element_type=f32)


def dot_nt(a, b):
    return lax.dot_general(a, b, (((1,), (1,)), ((), ())), preferred_element_type=f32)


def dot_tn(a, b):
    return lax.dot_general(a, b, (((0,), (0,)), ((), ())), preferred_element_type=f32)


def split_two(values):
    high = values.astype(bf16)
    return high, (values - high.astype(f32)).astype(bf16)


def inv_rms(values):
    return lax.rsqrt(jnp.mean(values * values, axis=-1, keepdims=True) + norm_eps)


def segment_of(place, first, second):
    seg = (place >= first).astype(i32) + (place >= second).astype(i32)
    start = jnp.where(seg == 0, 0, jnp.where(seg == 1, first, second))
    return seg, place - start


def vmem_spec():
    return pl.BlockSpec(memory_space=pltpu.VMEM)


def smem_spec():
    return pl.BlockSpec(memory_space=pltpu.SMEM)


def any_spec():
    return pl.BlockSpec(memory_space=pl.ANY)


def out(shape, dtype):
    return jax.ShapeDtypeStruct(shape, dtype)


def held(shape, dtype):
    return pltpu.VMEM(shape, dtype)


def in_vmem(value):
    return pltpu.with_memory_space_constraint(value, pltpu.VMEM)


def in_hbm(value):
    return pltpu.with_memory_space_constraint(value, pltpu.HBM)


def params(mib):
    return pltpu.CompilerParams(vmem_limit_bytes=mib * MIB)


def cost(flops, nbytes, trans=0):
    return pl.CostEstimate(flops=int(flops), bytes_accessed=int(nbytes), transcendentals=int(trans))


def pick_piece(pieces, turn, j):
    count = len(pieces)
    place = lax.rem(turn - j - 1 + count, count)
    picked = pieces[0][...]
    for k in range(1, count):
        picked = jnp.where(place == k, pieces[k][...], picked)
    return picked


def slot_of(index, count):
    return lax.rem(index + 2 * count, count)


def pack_kernel(count, tokens_ref, seg_hbm, prompt_hbm, *refs):
    pieces, (block_ref, seg_ref, prompt_ref, wide_ref, sems) = refs[:count], refs[count:]
    ctx = lax.axis_index("ctx")
    copies = [
        pltpu.make_async_copy(tokens_ref.at[slot_of(ctx + k + 1, count)], pieces[k], sems.at[k]) for k in range(count)
    ]
    small = [
        pltpu.make_async_copy(seg_hbm, seg_ref, sems.at[count]),
        pltpu.make_async_copy(prompt_hbm, prompt_ref, sems.at[count + 1]),
    ]
    for copy in small + copies:
        copy.start()
    for copy in small:
        copy.wait()
    rows = prompt_ref.shape[0]
    wide_ref[...] = jnp.zeros_like(wide_ref)
    wide_ref[0:rows, :] = prompt_ref[...]
    for n in range(2):
        tally = jnp.sum((seg_ref[...] <= n).astype(f32), axis=1, keepdims=True)
        wide_ref[rows + n * count : rows + (n + 1) * count, :] = jnp.broadcast_to(tally, (count, prompt_ref.shape[1]))
    block_ref[...] = wide_ref[...].astype(bf16)
    for copy in copies:
        copy.wait()


def prepare_kernel(count, base_ref, gain_first_ref, gain_second_ref, cot_ref, *refs):
    weights, (tile_ref, table_ref, first_ref, second_ref) = refs[:3], refs[3:7]
    pieces, kept, sems = refs[7 : 7 + count], refs[7 + count : 10 + count], refs[10 + count]
    first_ref[0, :] = gain_first_ref[...]
    second_ref[0, :] = gain_second_ref[...]
    ctx = lax.axis_index("ctx")
    copies = [pltpu.make_async_copy(weights[n], kept[n], sems.at[n]) for n in range(3)] + [
        pltpu.make_async_copy(cot_ref.at[slot_of(ctx + k + 1, count)], pieces[k], sems.at[3 + k]) for k in range(count)
    ]
    for copy in copies:
        copy.start()
    heads = tile_ref.shape[0]
    for h in range(heads):
        row = jnp.broadcast_to(base_ref[h : h + 1, :], (BLK, 4 * BLK))
        spread = pltpu.roll(row, 0, 1, stride=1, stride_axis=0)
        low, mid, top = (spread[:, k * BLK : (k + 1) * BLK] for k in (3, 2, 1))
        tile_ref[h, 0] = low
        tile_ref[h, 1] = mid
        tile_ref[h, 2] = top
        rows = slice(h * BLK, (h + 1) * BLK)
        parts = [part for pair in zip(split_two(mid), split_two(low)) for part in pair]
        for k in range(4):
            table_ref[rows, k * BLK : (k + 1) * BLK] = parts[k]
    for copy in copies:
        copy.wait()


def plane_kernel(rows_own, *refs):
    parts, (out_ref, wide_ref) = refs[:-2], refs[-2:]
    core, chip = lax.rem(lax.axis_index("dp"), 2), lax.div(lax.axis_index("dp"), 2)
    high = rows_own + 8
    parts = [part[...].astype(f32) for part in parts]
    parts = [[jnp.where(core == c, part[:high], part[high:]) for c in range(2)] for part in parts]
    for place in range(len(parts)):
        for c in range(2):
            picked = parts[0][c]
            for n in range(1, len(parts)):
                picked = jnp.where((chip ^ n) == place, parts[n][c], picked)
            start = (2 * place + c) * rows_own
            wide_ref[start : start + rows_own, :] = picked[:rows_own]
    for c in range(2):
        wide_ref[SHOWN + 8 * c : SHOWN + 8 * (c + 1), :] = parts[0][c][rows_own:]
    out_ref[...] = jnp.where(core == 0, wide_ref[0:HELD, :], wide_ref[HELD : 2 * HELD, :]).astype(bf16)


def places(count):
    return lax.rem(lax.axis_index("dp"), 2), lax.rem(lax.axis_index("ctx"), count)


def first_kernel(count, piece, *refs):
    own, (gain_ref, norm_ref) = refs[:count], refs[count:]
    turn = places(count)[1]
    for j in range(count):
        tok = pick_piece(own, turn, j).astype(f32)
        norm_ref[j * piece : (j + 1) * piece, :] = (tok * inv_rms(tok) * gain_ref[...]).astype(bf16)


def forward_kernel(count, piece, rows_own, *refs):
    own, partner = refs[:count], refs[count : 2 * count]
    (
        normed_ref, gain_first_ref, gain_second_ref, wq_ref, wk_ref, wv_ref, tile_ref, table_ref,
    ) = refs[2 * count : 2 * count + 8]
    refs = refs[2 * count + 8 :]
    (mine_ref, other_ref), later, refs = refs[:2], refs[2:5], refs[5:]
    e_ref, marks_ref, prompt_ref, q_ref, kall_ref, vall_ref, mixed_ref, inv_ref, after_ref, act_ref = refs[:10]
    kept, refs = refs[10:13], refs[13:]
    wo_ref, wi_ref, wout_ref = kept
    going, refs = refs[:count], refs[count:]
    norm_ref, hid_ref, slot_bias_ref, score_ref, aug_ref, shown_ref, e_buf, sems, weight_sems = refs
    fetches = [pltpu.make_async_copy(later[n], kept[n], weight_sems.at[n]) for n in range(3)]
    for fetch in fetches:
        fetch.start()
    ctx = lax.axis_index("ctx")
    half, turn = places(count)
    few = mine_ref.shape[1]
    low = jnp.where(half == 0, mine_ref[...], other_ref[...]).astype(f32)
    high = jnp.where(half == 0, other_ref[...], mine_ref[...]).astype(f32)
    for place in range(2 * count):
        for part, start, stop in ((low, 0, HELD), (high, HELD, SHOWN)):
            picked = part[0 : stop - start]
            for n in range(1, 2 * count):
                picked = jnp.where((ctx ^ n) == place, part[n * HELD : n * HELD + stop - start], picked)
            shown_ref[start:stop, place * few : (place + 1) * few] = picked
    shown_ref[SHOWN:, :] = jnp.zeros((BLK - SHOWN, shown_ref.shape[1]), f32)
    prompt_ref[...] = shown_ref[...].astype(bf16)
    half_len = count * piece
    width = q_ref.shape[1]
    tally = functools.reduce(jnp.add, [high[(n + 1) * HELD - 16 : (n + 1) * HELD] for n in range(2 * count)])
    tally_row = lax.broadcasted_iota(i32, (tally.shape[0], 1), 0)
    marks = []
    for n in range(2):
        here = tally_row == 8 * lax.div(ctx, count) + n * count + turn
        total = jnp.sum(jnp.where(here, tally, 0.0), axis=0, keepdims=True)[:, 0:1]
        marks.append((total + 0.5).astype(i32))
        marks_ref[n : n + 1, :] = jnp.broadcast_to(marks[n], (1, BLK))
    first, second = marks
    gain = gain_first_ref[...]
    slots = lax.broadcasted_iota(i32, (1, BLK), 1)
    for j in range(count):
        rows = slice(j * piece, (j + 1) * piece)
        place = half * half_len + j * piece + lax.broadcasted_iota(i32, (piece, 1), 0)
        inside = segment_of(place, first, second)[1]
        shown = inside < PROMPT
        choose = jnp.where((inside == slots) & shown, 1.0, 0.0).astype(bf16)
        picked = dot_nn(choose, prompt_ref[...])
        hidden = jnp.where(shown, picked, pick_piece(own, turn, j).astype(f32))
        hid_ref[rows, :] = hidden.astype(bf16)
        norm_ref[half_len + BLK + j * piece : half_len + BLK + (j + 1) * piece, :] = (
            hidden * inv_rms(hidden) * gain
        ).astype(bf16)
        tok = pick_piece(partner, turn, j).astype(f32)
        norm_ref[rows, :] = (tok * inv_rms(tok) * gain).astype(bf16)
    hidden = prompt_ref[...].astype(f32)
    norm_ref[half_len : half_len + BLK, :] = (hidden * inv_rms(hidden) * gain).astype(bf16)
    wide = 2 * BLK
    for t in range(width // wide):
        cols = slice(t * wide, (t + 1) * wide)
        normed = jnp.concatenate([normed_ref[...], norm_ref[0 : half_len + BLK, :]], axis=0)
        kall_ref[:, cols] = dot_nn(normed, wk_ref[:, cols]).astype(bf16)
        vall_ref[:, cols] = dot_nn(normed, wv_ref[:, cols]).astype(bf16)
    for t in range(width // wide):
        cols = slice(t * wide, (t + 1) * wide)
        q_ref[:, cols] = dot_nn(norm_ref[half_len + BLK :, :], wq_ref[:, cols]).astype(bf16)

    lane = lax.broadcasted_iota(i32, (1, PAIR), 1)
    low_lane = lane < HEAD
    lane_seg = lane
    spot = lax.broadcasted_iota(i32, (half_len, 1), 0)
    own_seg, own_inside = segment_of(half * half_len + spot, first, second)
    par_seg, par_inside = segment_of((1 - half) * half_len + spot, first, second)
    q_aug = jnp.where(own_seg == lane_seg, 1.0, 0.0).astype(bf16)

    def key_aug(seg, inside):
        closed = ((seg != lane_seg) | (inside < PROMPT)) & (lane_seg < 3)
        return jnp.where(closed, MASKED, 0.0).astype(bf16)

    slot = lax.broadcasted_iota(i32, (BLK, 1), 0)
    aug_ref[0:half_len] = key_aug(own_seg, own_inside)
    aug_ref[half_len : 2 * half_len] = key_aug(par_seg, par_inside)
    aug_ref[2 * half_len :] = jnp.where((slot >= PROMPT) & (lane_seg < 3), MASKED, 0.0).astype(bf16)
    across = segment_of(half * half_len + lax.broadcasted_iota(i32, (1, half_len), 1), first, second)[1]
    far = lax.rem(lax.broadcasted_iota(i32, (4 * BLK, 1), 0), 2 * BLK)
    spread = jnp.where(jnp.minimum(across, 2 * BLK - 1) == far, 1.0, 0.0).astype(bf16)
    slot_bias_ref[...] = dot_nn(table_ref[...], spread)
    blocks = half_len // BLK
    ones = jnp.ones((16, 2 * half_len + BLK), bf16)

    def e_copy(hp):
        at = lax.rem(hp, 2)
        return pltpu.make_async_copy(e_buf.at[at], e_ref.at[hp], sems.at[at])

    keys_all = 2 * half_len + BLK
    tiles_q = half_len // QCOLS
    chunk = keys_all // 3
    units = [(s, qt) for s in range(2) for qt in range(tiles_q)]

    def kept(s):
        return low_lane if s == 0 else jnp.logical_not(low_lane)

    def score_steps(hp, s, qt, slot):
        cols = pl.ds(pl.multiple_of(hp * PAIR, PAIR), PAIR)
        here = slice(qt * QCOLS, (qt + 1) * QCOLS)
        q_e = jnp.concatenate([jnp.where(kept(s), q_ref[here, cols], jnp.zeros((), bf16)), q_aug[here]], axis=1)

        def step(n):
            rows = slice(n * chunk, (n + 1) * chunk)
            score_ref[slot, rows, :] = dot_nt(jnp.concatenate([kall_ref[rows, cols], aug_ref[rows]], axis=1), q_e)

        return [functools.partial(step, n) for n in range(3)]

    for step in score_steps(0, 0, 0, 0):
        step()

    @pl.loop(0, width // PAIR)
    def _(hp):
        @pl.when(hp >= 2)
        def _():
            e_copy(hp - 2).wait()

        cols = pl.ds(pl.multiple_of(hp * PAIR, PAIR), PAIR)
        v_turned = vall_ref[:, cols].T
        for u, (s, qt) in enumerate(units):
            h = 2 * hp + s
            coming = units[(u + 1) % len(units)]
            at = hp if u + 1 < len(units) else jnp.minimum(hp + 1, width // PAIR - 1)
            steps = score_steps(at, *coming, (u + 1) % 2)
            back_far, ahead_far = tile_ref[h, 0, 0:1, BLK - 1 :], tile_ref[h, 2, BLK - 1 :, 0:1]
            other_far = jnp.where(half == 0, ahead_far, back_far)
            values = (back_far, ahead_far, other_far)
            columns = []
            for sub in range(QCOLS // BLK):
                qb = qt * (QCOLS // BLK) + sub
                here = slice(sub * BLK, (sub + 1) * BLK)

                def part_of(kb):
                    part = score_ref[u % 2, kb * BLK : (kb + 1) * BLK, here]
                    if kb == 2 * blocks:
                        slot_rows = pl.ds(pl.multiple_of(h * BLK, BLK), BLK)
                        return part + slot_bias_ref[slot_rows, qb * BLK : (qb + 1) * BLK], None
                    gap = kb - qb
                    if kb < blocks and abs(gap) <= 1:
                        return part + tile_ref[h, gap + 1], None
                    if kb < blocks:
                        return part, 0 if gap < 0 else 1
                    if qb == blocks - 1 and kb == blocks:
                        return part + jnp.where(half == 0, tile_ref[h, 2], back_far), None
                    if qb == 0 and kb == 2 * blocks - 1:
                        return part + jnp.where(half == 0, ahead_far, tile_ref[h, 0]), None
                    return part, 2

                tops, group = {}, {}
                for kb in range(2 * blocks + 1):
                    part, const = part_of(kb)
                    if const is None:
                        score_ref[u % 2, kb * BLK : (kb + 1) * BLK, here] = part
                    group[kb] = const
                    top = jnp.max(part.reshape(BLK // 8, 8, BLK), axis=0)
                    tops[const] = top if const not in tops else jnp.maximum(tops[const], top)
                    if steps and kb == 4:
                        steps.pop(0)()
                peak = functools.reduce(
                    jnp.maximum, [top if const is None else top + values[const] for const, top in tops.items()]
                )
                peak = jnp.max(peak, axis=0, keepdims=True)
                shifts = [peak - value for value in values]
                column = []
                for kb in range(2 * blocks + 1):
                    part = score_ref[u % 2, kb * BLK : (kb + 1) * BLK, here]
                    shift = peak if group[kb] is None else shifts[group[kb]]
                    column.append(jnp.exp(part - shift).astype(bf16))
                    if steps and kb == 4:
                        steps.pop(0)()
                columns.append(jnp.concatenate(column, axis=0))
            for step in steps:
                step()
            raised = jnp.concatenate(columns, axis=1)
            qcols = slice(qt * QCOLS, (qt + 1) * QCOLS)
            e_buf[lax.rem(hp, 2), s, :, qcols] = raised
            total = dot_nn(jnp.concatenate([v_turned[s * HEAD : (s + 1) * HEAD], ones], axis=0), raised)
            inv = 1.0 / total[HEAD : HEAD + 1]
            inv_ref[pl.ds(h, 1), qcols] = inv
            mixed_ref[pl.ds(pl.multiple_of(h * HEAD, HEAD), HEAD), qcols] = (total[:HEAD] * inv).astype(bf16)
        e_copy(hp).start()

    for fetch in fetches:
        fetch.wait()
    after_ref[...] = dot_tn(mixed_ref[...], wo_ref[...])

    for t in range(half_len // BLK):
        rows = slice(t * BLK, (t + 1) * BLK)
        after = hid_ref[rows, :].astype(f32) + after_ref[rows, :]
        after_ref[rows, :] = after
        norm_ref[rows, :] = (after * inv_rms(after) * gain_second_ref[...]).astype(bf16)

    @pl.loop(0, wi_ref.shape[1] // UNITS)
    def _(t):
        units = pl.ds(pl.multiple_of(t * UNITS, UNITS), UNITS)
        inner = lax.dot_general(
            wi_ref[:, units], norm_ref[0:half_len, :], (((0,), (1,)), ((), ())), preferred_element_type=f32
        )
        act_ref[units, :] = jnp.maximum(inner, 0.0).astype(bf16)

    made = (after_ref[...] + dot_tn(act_ref[...], wout_ref[...])).astype(bf16)
    made = [made[j * piece : (j + 1) * piece] for j in range(count)]
    for k in range(count):
        place = slot_of(turn - k - 1, count)
        sent = made[0]
        for j in range(1, count):
            sent = jnp.where(place == j, made[j], sent)
        going[k][...] = sent

    for hp in range(width // PAIR - 2, width // PAIR):
        e_copy(hp).wait()


def backward_kernel(count, piece, rows_own, *refs):
    cots = refs[:count]
    (
        marks_ref, act_ref, after_ref, mixed_ref, inv_ref, q_ref, kall_ref, vall_ref, prompt_ref, gain_first_ref, gain_second_ref,
        wout_ref, wi_ref, wo_ref, wq_ref, wk_ref, wv_ref, e_ref,
        kept_ref, sent_ref,
        cot_ref, acc_ref, low_ref, do_ref, dq_ref, gk_ref, gv_ref, cast_ref, e_buf, sems,
    ) = refs[count:]
    half, turn = places(count)
    first, second = marks_ref[0:1, 0:1], marks_ref[1:2, 0:1]
    half_len = count * piece
    width = q_ref.shape[1]
    pairs = width // PAIR

    def e_copy(hp):
        at = lax.rem(hp, 2)
        return pltpu.make_async_copy(e_ref.at[hp], e_buf.at[at], sems.at[at])

    for hp in range(2):
        e_copy(hp).start()
    for j in range(count):
        cot_ref[j * piece : (j + 1) * piece, :] = pick_piece(cots, turn, j)
    do_ref[...] = jnp.zeros_like(do_ref)

    for t in range(wi_ref.shape[1] // UNITS):
        units = slice(t * UNITS, (t + 1) * UNITS)
        grad_act = dot_nt(wout_ref[units, :], cot_ref[...])
        grad_inner = jnp.where(act_ref[units, :] > 0, grad_act, 0.0).astype(bf16)
        do_ref[...] += dot_nn(wi_ref[:, units], grad_inner)

    acc_ref[...] = do_ref[...].T
    gain = gain_second_ref[...]

    for t in range(half_len // BLK):
        rows = slice(t * BLK, (t + 1) * BLK)
        after = after_ref[rows, :]
        scale = inv_rms(after)
        pulled = gain * acc_ref[rows, :]
        along = jnp.mean(after * pulled, axis=-1, keepdims=True)
        grad_after = cot_ref[rows, :].astype(f32) + scale * pulled - after * (scale * scale * scale * along)
        acc_ref[rows, :] = grad_after
        low_ref[rows, :] = grad_after.astype(bf16)

    do_ref[...] = dot_nt(wo_ref[...], low_ref[...])

    low_lane = lax.broadcasted_iota(i32, (1, PAIR), 1) < HEAD
    row = lax.broadcasted_iota(i32, (PAIR, 1), 0)
    ones = jnp.ones((2 * half_len + BLK, PAIR), bf16)

    @pl.loop(0, pairs)
    def _(hp):
        e_copy(hp).wait()
        cols = pl.ds(pl.multiple_of(hp * PAIR, PAIR), PAIR)
        q_pair, k_turned, v_pair = q_ref[:, cols], kall_ref[:, cols].T, vall_ref[:, cols]
        inv_both = jnp.where(row < HEAD, inv_ref[pl.ds(2 * hp, 1), :], inv_ref[pl.ds(2 * hp + 1, 1), :])
        do_pair = (do_ref[cols, :] * inv_both).astype(bf16)
        inner = do_pair.astype(f32) * mixed_ref[cols, :].astype(f32)
        slot_scores, slot_raised = [], []
        for s in range(2):
            mine = (row < HEAD) == (s == 0)
            high, low = split_two(-jnp.sum(inner[s * HEAD : (s + 1) * HEAD], axis=0, keepdims=True))
            zero = jnp.zeros((), bf16)
            shift = jnp.where(row == 0, high, jnp.where(row == 1, low, zero))
            do_e = jnp.concatenate([jnp.where(mine, do_pair, zero), shift], axis=0)
            raised = e_buf[lax.rem(hp, 2), s]
            grad_probs = dot_nn(jnp.concatenate([v_pair, ones], axis=1), do_e)
            grad_scores = (raised.astype(f32) * grad_probs).astype(bf16)
            made = dot_nn(k_turned[s * HEAD : (s + 1) * HEAD], grad_scores)
            dq_ref[pl.ds(pl.multiple_of(hp * PAIR + s * HEAD, HEAD), HEAD), :] = made.astype(bf16)
            slot_scores.append(grad_scores[2 * half_len :])
            slot_raised.append(raised[2 * half_len :])
        dk = dot_nn(jnp.concatenate(slot_scores, axis=0), q_pair)
        dv = dot_nt(jnp.concatenate(slot_raised, axis=0), do_pair)
        gk_ref[:, cols] = jnp.where(low_lane, dk[:BLK], dk[BLK:]).astype(bf16)
        gv_ref[:, cols] = jnp.where(low_lane, dv[:BLK], dv[BLK:]).astype(bf16)

        @pl.when(hp + 2 < pairs)
        def _():
            e_copy(hp + 2).start()

    spot = lax.broadcasted_iota(i32, (1, half_len), 1)
    inside = segment_of(half * half_len + spot, first, second)[1]
    slots = lax.broadcasted_iota(i32, (BLK, 1), 0)
    choose = jnp.where((inside == slots) & (inside < PROMPT), 1.0, 0.0).astype(bf16)
    gq = dot_nt(choose, dq_ref[...]).astype(bf16)
    pulled = dot_nt(gq, wq_ref[...]) + dot_nt(gk_ref[...], wk_ref[...]) + dot_nt(gv_ref[...], wv_ref[...])
    high, low = split_two(acc_ref[...])
    direct = dot_nn(choose, high) + dot_nn(choose, low)
    hidden = prompt_ref[...].astype(f32)
    scale = inv_rms(hidden)
    pulled = gain_first_ref[...] * pulled
    along = jnp.mean(hidden * pulled, axis=-1, keepdims=True)
    grad = direct + scale * pulled - hidden * (scale * scale * scale * along)
    for place in range(BLK // (2 * rows_own)):
        rows = slice(place * rows_own, (place + 1) * rows_own)
        low, high = (grad[(2 * place + c) * rows_own : (2 * place + c + 1) * rows_own] for c in range(2))
        kept_ref[rows, :] = jnp.where(half == 0, low, high)
        cast_ref[rows, :] = jnp.where(half == 0, high, low)
    sent_ref[...] = cast_ref[...].astype(bf16)


def share_kernel(rows_own, kept_ref, came_ref, mine_ref, *refs):
    parts, (total_ref,) = refs[:-1], refs[-1:]
    chip = lax.div(lax.axis_index("dp"), 2)
    total = kept_ref[...] + came_ref[...].astype(f32)
    for place in range(len(parts) + 1):
        total_ref[place] = total[place * rows_own : (place + 1) * rows_own]
    mine_ref[...] = total_ref[chip]
    for n in range(1, len(parts) + 1):
        parts[n - 1][...] = total_ref[chip ^ n].astype(bf16)


def square_kernel(total_ref, *refs):
    parts, (own_ref, square_ref) = refs[:-2], refs[-2:]
    total = total_ref[...]
    for part in parts:
        total = total + part[...].astype(f32)
    few = own_ref.shape[1]
    own = total[:, 0:few]
    for place in range(1, len(parts) + 1):
        own = jnp.where(lax.axis_index("ctx") == place, total[:, place * few : (place + 1) * few], own)
    own_ref[...] = own
    square = jnp.sum(jnp.sum(total * total, axis=1, keepdims=True), axis=0, keepdims=True)
    square_ref[...] = jnp.broadcast_to(square, square_ref.shape)


def update_kernel(max_norm, grad_ref, prompt_ref, first_ref, second_ref, *refs):
    squares, (prompt_out, first_out, second_out) = refs[:-3], refs[-3:]
    square = functools.reduce(jnp.add, [square[0:1, 0:1] for square in squares])
    clipped = grad_ref[...] * (max_norm / jnp.maximum(jnp.sqrt(square), max_norm))
    first_new = beta_first * first_ref[...] + (1.0 - beta_first) * clipped
    second_new = beta_second * second_ref[...] + (1.0 - beta_second) * clipped * clipped
    step = learn_rate * (first_new / first_fix) / (jnp.sqrt(second_new / second_fix) + adam_eps)
    prompt_out[...] = prompt_ref[...] - step
    first_out[...] = first_new
    second_out[...] = second_new


def on_device(
    sizes, tokens, segment_ids, prompt_slots, cotangent, w_query, w_key, w_value, w_output, w_inner, w_outer,
    gain_first, gain_second, bias_table, prompt, first_moment, second_moment,
):
    n_dp, n_ctx = sizes
    count, piece, width = tokens.shape
    half_len = count * piece
    heads = bias_table.shape[1]
    dp, ctx = lax.axis_index("dp"), lax.axis_index("ctx")
    core = lax.rem(dp, 2)

    def permute(value, target):
        pairs = []
        for d in range(n_dp):
            for z in range(n_ctx):
                d2, z2 = target(d, z)
                pairs.append((d * n_ctx + z, d2 * n_ctx + z2))
        return lax.ppermute(value, AXES, pairs)

    def swap_dp(value, bit):
        return permute(value, lambda d, z: (d ^ bit, z))

    def swap_ctx(value, bit):
        return permute(value, lambda d, z: (d, z ^ bit))

    def there(k):
        return lambda d, z: (2 * (d // 2) + z // count, (d % 2) * count + (z + k + 1) % count)

    rows_own, cols_own = prompt.shape
    piece_like = held((piece, width), bf16)
    packed = pl.pallas_call(
        functools.partial(pack_kernel, count),
        out_shape=[piece_like] * count + [held((rows_own + 8, cols_own), bf16)],
        in_specs=[any_spec()] * 3,
        out_specs=[vmem_spec()] * (count + 1),
        scratch_shapes=[
            pltpu.VMEM(segment_ids.shape, i32),
            pltpu.VMEM(prompt.shape, f32),
            pltpu.VMEM((rows_own + 8, cols_own), f32),
            pltpu.SemaphoreType.DMA((count + 2,)),
        ],
        compiler_params=params(4),
        cost_estimate=cost(1e5, 2e6),
    )(in_hbm(tokens), in_hbm(segment_ids), in_hbm(prompt))

    own = [permute(packed[k], there(k)) for k in range(count)]
    chip_rows = jnp.concatenate([packed[count], swap_dp(packed[count], 1)], axis=0)
    chip_parts = [chip_rows] + [swap_dp(chip_rows, 2 * n) for n in range(1, n_dp // 2)]
    plane = pl.pallas_call(
        functools.partial(plane_kernel, rows_own),
        out_shape=held((HELD, cols_own), bf16),
        in_specs=[vmem_spec()] * len(chip_parts),
        out_specs=vmem_spec(),
        scratch_shapes=[pltpu.VMEM((BLK + 16, cols_own), f32)],
        compiler_params=params(4),
        cost_estimate=cost(1e5, 1e5),
    )(*chip_parts)

    choose = (np.arange(bias_table.shape[0])[:, None] == bucket_table(2 * BLK - np.arange(4 * BLK))[None]).astype(np.float32)
    base = lax.dot_general(
        bias_table, jnp.asarray(choose), (((0,), (0,)), ((), ())), precision=lax.Precision.HIGHEST
    )
    base, plane = lax.optimization_barrier((base, plane))
    cols_mine = jnp.concatenate([plane] + [swap_ctx(plane, n) for n in range(1, n_ctx)], axis=0)
    cols_other = swap_dp(cols_mine, 1)
    weights = (w_query, w_key, w_value)
    prepared = pl.pallas_call(
        functools.partial(prepare_kernel, count),
        out_shape=[held((heads, 3, BLK, BLK), f32), held((heads * BLK, 4 * BLK), bf16)]
        + [held((1, width), f32)] * 2
        + [piece_like] * count
        + [held(w.shape, bf16) for w in weights],
        in_specs=[vmem_spec()] * 3 + [any_spec()] * 4,
        out_specs=[vmem_spec()] * (7 + count),
        scratch_shapes=[pltpu.SemaphoreType.DMA((3 + count,))],
        compiler_params=params(4),
        cost_estimate=cost(1e6, 5e6),
    )(base, gain_first, gain_second, in_hbm(cotangent), *[in_hbm(w) for w in weights])
    tiles, table, gain_1, gain_2 = prepared[:4]
    cot_pieces = prepared[4 : 4 + count]
    w_q, w_k, w_v = prepared[4 + count :]

    keys_all = 2 * half_len + BLK
    hidden_ff = w_inner.shape[1]
    partner = [swap_dp(piece_rows, 1) for piece_rows in own]
    normed = pl.pallas_call(
        functools.partial(first_kernel, count, piece),
        out_shape=held((half_len, width), bf16),
        in_specs=[vmem_spec()] * (count + 1),
        out_specs=vmem_spec(),
        compiler_params=params(A_MIB),
        cost_estimate=cost(1e10, 8e6),
    )(*own, gain_1)
    cots = [permute(cot_pieces[k], there(k)) for k in range(count)]

    made = pl.pallas_call(
        functools.partial(forward_kernel, count, piece, rows_own),
        out_shape=[
            pltpu.HBM((heads // 2, 2, keys_all, half_len), bf16),
            held((8, BLK), i32),
            held((BLK, width), bf16),
            held((half_len, width), bf16),
            held((keys_all, width), bf16),
            held((keys_all, width), bf16),
            held((width, half_len), bf16),
            held((heads, half_len), f32),
            held((half_len, width), f32),
            held((hidden_ff, half_len), bf16),
        ]
        + [held(w.shape, bf16) for w in (w_output, w_inner, w_outer)]
        + [piece_like] * count,
        in_specs=[vmem_spec()] * (2 * count + 10) + [any_spec()] * 3,
        out_specs=[any_spec()] + [vmem_spec()] * (12 + count),
        scratch_shapes=[
            pltpu.VMEM((2 * half_len + BLK, width), bf16),
            pltpu.VMEM((half_len, width), bf16),
            pltpu.VMEM((heads * BLK, half_len), f32),
            pltpu.VMEM((2, keys_all, QCOLS), f32),
            pltpu.VMEM((keys_all, PAIR), bf16),
            pltpu.VMEM((BLK, width), f32),
            pltpu.VMEM((2, 2, keys_all, half_len), bf16),
            pltpu.SemaphoreType.DMA((2,)),
            pltpu.SemaphoreType.DMA((3,)),
        ],
        compiler_params=params(F_MIB),
        cost_estimate=cost(3e10, 4e7, heads * half_len * keys_all),
    )(
        *own, *partner, normed, gain_1, gain_2, w_q, w_k, w_v, tiles, table, cols_mine, cols_other,
        *[in_hbm(w) for w in (w_output, w_inner, w_outer)],
    )
    got = [permute(made[13 + k], back_of(count, k)) for k in range(count)]
    w_o, w_i, w_out = made[10:13]
    e, marks, sent, q, kall, vall, mixed, inv, after, act = made[:10]

    half_rows = n_dp // 2 * rows_own
    kept, leaving = pl.pallas_call(
        functools.partial(backward_kernel, count, piece, rows_own),
        out_shape=[held((half_rows, width), f32), held((half_rows, width), bf16)],
        in_specs=[vmem_spec()] * (count + 17) + [any_spec()],
        out_specs=[vmem_spec()] * 2,
        scratch_shapes=[
            pltpu.VMEM((half_len, width), bf16),
            pltpu.VMEM((half_len, width), f32),
            pltpu.VMEM((half_len, width), bf16),
            pltpu.VMEM((width, half_len), f32),
            pltpu.VMEM((width, half_len), bf16),
            pltpu.VMEM((BLK, width), bf16),
            pltpu.VMEM((BLK, width), bf16),
            pltpu.VMEM((half_rows, width), f32),
            pltpu.VMEM((2, 2, keys_all, half_len), bf16),
            pltpu.SemaphoreType.DMA((2,)),
        ],
        compiler_params=params(B_MIB),
        cost_estimate=cost(3e10, 4e7),
    )(
        *cots, marks, act, after, mixed, inv, q, kall, vall, sent, gain_1, gain_2, w_out, w_i, w_o, w_q, w_k, w_v, in_hbm(e),
    )

    got, leaving = lax.optimization_barrier((got, leaving))
    order = [lax.rem(ctx + j + 1, count) for j in range(count)]
    output = jnp.stack(
        [functools.reduce(lambda a, k: jnp.where(order[k] == r, got[k], a), range(1, count), got[0]) for r in range(count)]
    )

    chips = n_dp // 2
    own_like = held((rows_own, width), f32)
    mine, *parts = pl.pallas_call(
        functools.partial(share_kernel, rows_own),
        out_shape=[own_like] + [held((rows_own, width), bf16)] * (chips - 1),
        in_specs=[vmem_spec()] * 2,
        out_specs=[vmem_spec()] * chips,
        scratch_shapes=[pltpu.VMEM((chips, rows_own, width), f32)],
        compiler_params=params(4),
        cost_estimate=cost(1e5, 1e5),
    )(kept, swap_dp(leaving, 1))
    for n in range(1, chips):
        mine = mine + swap_dp(parts[n - 1], 2 * n).astype(f32)
    line = mine.astype(bf16)
    line_parts = [swap_ctx(line, n) for n in range(1, n_ctx)]
    line_parts, output = lax.optimization_barrier((line_parts, output))
    grad_own, square = pl.pallas_call(
        square_kernel,
        out_shape=[held((rows_own, cols_own), f32), held((8, BLK), f32)],
        in_specs=[vmem_spec()] * n_ctx,
        out_specs=[vmem_spec()] * 2,
        compiler_params=params(4),
        cost_estimate=cost(1e5, 1e5),
    )(mine, *line_parts)
    square = square + swap_dp(square, 1)
    squares = [square] + [swap_dp(square, 2 * n) for n in range(1, chips)]
    own_out = out((rows_own, cols_own), f32)
    prompt_new, first_new, second_new = pl.pallas_call(
        functools.partial(update_kernel, float(0.5 * np.sqrt(np.float32(PROMPT * width)))),
        out_shape=[own_out] * 3,
        in_specs=[vmem_spec()] * (4 + chips),
        out_specs=[vmem_spec()] * 3,
        compiler_params=params(4),
        cost_estimate=cost(1e5, 1e5),
    )(grad_own, prompt, first_moment, second_moment, *squares)
    return (output, prompt_new, first_new, second_new)


def back_of(count, k):
    def target(d, z):
        half, c, r = d % 2, z // count, z % count
        return (2 * (d // 2) + c, half * count + (r - k - 1) % count)

    return target


def solution(mesh):
    rows, cols = P("dp", "ctx", None), P("dp", "ctx")
    placed = (rows, cols, cols, rows) + (P(),) * 9 + (cols,) * 3
    return jax.shard_map(
        functools.partial(on_device, (mesh.shape["dp"], mesh.shape["ctx"])),
        mesh=mesh,
        in_specs=placed,
        out_specs=(rows, cols, cols, cols),
        check_vma=False,
    )
```
